32 devices in a mesh: dom: 16 (over z, x, core), split: 2 (over y).
Axes of the slice: x: 2, y: 2, z: 4, core: 2. Of those that a mesh axis runs over, the one named last changes fastest.
Arguments:
- modes_now: float32 [64, 1024, 128], P('split', 'dom'), may hold values from -6 to 6
- modes_prev: float32 [64, 1024, 128], P('split', 'dom'), may hold values from -6 to 6
- z_extent: int32 [16], P('dom'), may hold values from 16 to 64, as said below
- lower_nbr: int32 [16], P('dom'), may hold values from -1 to 15, as said below
- upper_nbr: int32 [16], P('dom'), may hold values from -1 to 15
- x_shift: int32 [16, 2], P('dom'), may hold values from -32 to 32, as said below
- y_shift: int32 [16, 2], P('dom'), may hold values from -32 to 32, as said below
Outputs:
- modes_next: float32 [64, 1024, 128], P('split', 'dom')
- modes_cur: float32 [64, 1024, 128], P('split', 'dom')
- pressure: float32 [64, 1024, 128], P('split', 'dom')
The draws below stay inside these ranges and needn't reach their ends.
Inputs may be any that keep to these rules, and one draw needn't show every extreme that they name: `z_extent`: at least one cuboid reaches the full 64 slots. Cuboids form chains: if upper_nbr[a] = b then lower_nbr[b] = a, and no cuboid is its own neighbour. If upper_nbr[a] = b then x_shift[a, 1] = -x_shift[b, 0]; zero at walls. If upper_nbr[a] = b then y_shift[a, 1] = -y_shift[b, 0]; zero at walls.
All inputs are finite; a program needn't handle non-finite values.
Results may differ from the reference program's by a relative error of at most 0.0003.
Values sent between devices are 32-bit elements; how exact they have to be, the bound alone decides.
No kernel may reach another device: no remote copies, remote signals or barrier semaphores. Data moves between devices by JAX's collectives and lax.ppermute only.
A program may use at most 64 MiB of HBM per device.

```python
import jax
import jax.numpy as jnp
from jax import lax

NX = 64
NY = 128
ZC = 64
STEPS = 2
GROUPS = 16
TOTALZ = 1024


def chains(key):
    base = jax.random.fold_in(key, 7)
    order = jax.random.permutation(base, GROUPS).astype(jnp.int32)
    position = jnp.arange(GROUPS)
    cut = (jax.random.randint(jax.random.fold_in(base, 1), (GROUPS,), 0, 4) == 0) & (position > 0)
    link = jnp.logical_not(cut) & (position < GROUPS - 1)
    following = jnp.roll(order, -1)
    preceding = jnp.roll(order, 1)
    link_before = jnp.roll(link, 1) & (position > 0)
    upper = jnp.zeros((GROUPS,), jnp.int32).at[order].set(jnp.where(link, following, -1).astype(jnp.int32))
    lower = jnp.zeros((GROUPS,), jnp.int32).at[order].set(jnp.where(link_before, preceding, -1).astype(jnp.int32))
    move_x = jax.random.randint(jax.random.fold_in(base, 2), (GROUPS,), -(NX // 2), NX // 2 + 1)
    move_y = jax.random.randint(jax.random.fold_in(base, 3), (GROUPS,), -(NY // 4), NY // 4 + 1)
    move_x = jnp.where(position == 0, NX // 2, move_x).astype(jnp.int32)
    move_y = jnp.where(position == 0, NY // 4, move_y).astype(jnp.int32)
    up_x = jnp.where(link, move_x, 0).astype(jnp.int32)
    low_x = jnp.where(link_before, -jnp.roll(move_x, 1), 0).astype(jnp.int32)
    up_y = jnp.where(link, move_y, 0).astype(jnp.int32)
    low_y = jnp.where(link_before, -jnp.roll(move_y, 1), 0).astype(jnp.int32)
    shift_x = jnp.zeros((GROUPS, 2), jnp.int32).at[order].set(jnp.stack([low_x, up_x], axis=1))
    shift_y = jnp.zeros((GROUPS, 2), jnp.int32).at[order].set(jnp.stack([low_y, up_y], axis=1))
    return (lower, upper, shift_x, shift_y)


def draw_lower_nbr(key, part):
    return chains(key)[0]


def draw_upper_nbr(key, part):
    return chains(key)[1]


def draw_x_shift(key, part):
    return chains(key)[2]


def draw_y_shift(key, part):
    return chains(key)[3]


def draw_z_extent(key, part):
    base = jax.random.fold_in(key, 3)
    extent = jax.random.randint(base, (GROUPS,), ZC // 4, ZC + 1).astype(jnp.int32)
    spot = jax.random.randint(jax.random.fold_in(base, 1), (), 0, GROUPS)
    return extent.at[spot].set(ZC).astype(jnp.int32)


def shard_levels(own_key, shape, split, low, largest):
    def one(dim, parts):
        heights = jax.random.uniform(jax.random.fold_in(jax.random.fold_in(own_key, 6), dim), (parts,), jnp.float32, low / len(split), largest / len(split))
        return jnp.repeat(jnp.exp(heights), shape[dim] // parts).reshape((-1,) + (1,) * (len(shape) - dim - 1))

    level = one(*split[0])
    for cut in split[1:]:
        level = level * one(*cut)
    return level


def gaussian(own_key, shape, spread, most, split=(), kind=jnp.bfloat16):
    values = spread * jax.random.normal(own_key, shape, jnp.float32)
    if split:
        values = values * shard_levels(own_key, shape, split, -0.22, 0.18)
    return jnp.clip(values, -most, most).astype(kind)


def setup_inputs(seed: int = 0) -> dict:
    seeds = jax.random.split(jax.random.key(seed), 8)
    return {
        "modes_now": gaussian(seeds[0], (NX, TOTALZ, NY), 1.0, 6.0, ((0, 2), (1, 16)), jnp.float32),
        "modes_prev": gaussian(seeds[1], (NX, TOTALZ, NY), 1.0, 6.0, ((0, 2), (1, 16)), jnp.float32),
        "z_extent": draw_z_extent(jax.random.fold_in(seeds[7], 71), 0),
        "lower_nbr": draw_lower_nbr(jax.random.fold_in(seeds[7], 71), 0),
        "upper_nbr": draw_upper_nbr(jax.random.fold_in(seeds[7], 71), 0),
        "x_shift": draw_x_shift(jax.random.fold_in(seeds[7], 71), 0),
        "y_shift": draw_y_shift(jax.random.fold_in(seeds[7], 71), 0),
    }


HIGH = lax.Precision.HIGHEST
STENCIL = (-490.0 / 180.0, 270.0 / 180.0, -27.0 / 180.0, 2.0 / 180.0)
COURANT = 0.5

def cosine_table(kk, xx, length):
    scale = jnp.where(kk == 0, jnp.sqrt(1.0 / length), jnp.sqrt(2.0 / length))
    return scale * jnp.cos(jnp.pi * kk * (xx + 0.5) / length)

def square_table(count):
    index = jnp.arange(count).astype(jnp.float32)
    return cosine_table(index[:, None], index[None, :], jnp.float32(count))

def shifted(face, rows, move_y):
    count = face.shape[0]
    width = face.shape[2]
    cols = jnp.arange(width).astype(jnp.int32) + move_y
    rows_ok = (rows >= 0) & (rows < count)
    cols_ok = (cols >= 0) & (cols < width)
    picked = jnp.take(face, jnp.clip(rows, 0, count - 1).astype(jnp.int32), axis=0)
    picked = jnp.take(picked, jnp.clip(cols, 0, width - 1).astype(jnp.int32), axis=2)
    mask = (rows_ok[:, None, None] & cols_ok[None, None, :]).astype(jnp.float32)
    return (picked, mask)

def aligned(face, move_x, move_y):
    rows = jnp.arange(NX).astype(jnp.int32) + move_x
    return shifted(face, rows, move_y)

def z_tables(extent):
    zidx = jnp.arange(ZC).astype(jnp.int32)
    live = zidx < extent
    kz = zidx.astype(jnp.float32)
    lenf = extent.astype(jnp.float32)
    ztable = jnp.where(live[:, None] & live[None, :], cosine_table(kz[:, None], kz[None, :], lenf), 0.0)
    rows = jnp.array([0, 1, 2, -3, -2, -1], jnp.int32) + jnp.where(jnp.arange(6) >= 3, extent, 0).astype(jnp.int32)
    onerow = (zidx[None, :] == rows[:, None]).astype(jnp.float32)
    row_table = jnp.dot(ztable, onerow.T, precision=HIGH, preferred_element_type=jnp.float32)
    kx = jnp.arange(NX).astype(jnp.float32)
    ky = jnp.arange(NY).astype(jnp.float32)
    freq = COURANT * jnp.pi * jnp.sqrt((kx / NX)[:, None, None] ** 2 + (kz / lenf)[None, :, None] ** 2 + (ky / NY)[None, None, :] ** 2)
    twice_cos = 2.0 * jnp.cos(freq)
    gain = jnp.sinc(freq / (2.0 * jnp.pi)) ** 2
    return (ztable, row_table, twice_cos, gain)

def interface(lower_face, upper_face, from_lower, from_upper, has_lower, has_upper):
    low_rows = []
    for jj in range(3):
        total = jnp.zeros_like(lower_face[..., 0, :])
        for mm in range(-3, 0):
            if abs(jj - mm) <= 3:
                total = total + STENCIL[abs(jj - mm)] * (from_lower[..., mm + 3, :] - lower_face[..., -1 - mm, :])
        low_rows.append(total)
    up_rows = []
    for aa in range(3):
        tt = aa - 3
        total = jnp.zeros_like(upper_face[..., 0, :])
        for mm in range(3):
            if abs(tt - mm) <= 3:
                total = total + STENCIL[abs(tt - mm)] * (from_upper[..., mm, :] - upper_face[..., 2 - mm, :])
        up_rows.append(total)
    low = jnp.stack(low_rows, axis=-2) * has_lower
    upp = jnp.stack(up_rows, axis=-2) * has_upper
    return COURANT ** 2 * jnp.concatenate([low, upp], axis=-2)

def reference(modes_now, modes_prev, z_extent, lower_nbr, upper_nbr, x_shift, y_shift):
    xtable = square_table(NX)
    ytable = square_table(NY)
    zidx = jnp.arange(ZC).astype(jnp.int32)

    def to_groups(arr):
        return arr.reshape(NX, GROUPS, ZC, NY).transpose(1, 0, 2, 3)

    def masked(arr, extent):
        return arr * (zidx < extent).astype(jnp.float32)[None, :, None]
    now = lax.map(lambda a: masked(a[0], a[1]), (to_groups(modes_now), z_extent))
    prev = lax.map(lambda a: masked(a[0], a[1]), (to_groups(modes_prev), z_extent))

    def strip_of(args):
        mode, extent = args
        ztable, row_table, twice_cos, gain = z_tables(extent)
        part = jnp.einsum('kr,xky->xry', row_table, mode, precision=HIGH, preferred_element_type=jnp.float32)
        part = jnp.einsum('xrk,ky->xry', part, ytable, precision=HIGH, preferred_element_type=jnp.float32)
        return jnp.einsum('kx,kry->xry', xtable, part, precision=HIGH, preferred_element_type=jnp.float32)
    has_lower = (lower_nbr >= 0).astype(jnp.float32)[:, None, None, None]
    has_upper = (upper_nbr >= 0).astype(jnp.float32)[:, None, None, None]
    low_index = jnp.maximum(lower_nbr, 0).astype(jnp.int32)
    up_index = jnp.maximum(upper_nbr, 0).astype(jnp.int32)
    for step in range(STEPS):
        strips = lax.map(strip_of, (now, z_extent))
        lower_face = strips[:, :, 0:3]
        upper_face = strips[:, :, 3:6]
        from_lower, mask_low = jax.vmap(aligned)(upper_face[low_index], x_shift[:, 0], y_shift[:, 0])
        from_upper, mask_up = jax.vmap(aligned)(lower_face[up_index], x_shift[:, 1], y_shift[:, 1])
        forcing = interface(lower_face, upper_face, from_lower, from_upper, has_lower * mask_low, has_upper * mask_up)

        def update(args):
            mode, older, force, extent = args
            ztable, row_table, twice_cos, gain = z_tables(extent)
            part = jnp.einsum('xry,ky->xrk', force, ytable, precision=HIGH, preferred_element_type=jnp.float32)
            part = jnp.einsum('kx,xry->kry', xtable, part, precision=HIGH, preferred_element_type=jnp.float32)
            fmodes = jnp.einsum('kr,xry->xky', row_table, part, precision=HIGH, preferred_element_type=jnp.float32)
            return twice_cos * mode - older + gain * fmodes
        newer = lax.map(update, (now, prev, forcing, z_extent))
        prev, now = (now, newer)

    def field_of(args):
        mode, extent = args
        ztable, row_table, twice_cos, gain = z_tables(extent)
        part = jnp.einsum('kz,xky->xzy', ztable, mode, precision=HIGH, preferred_element_type=jnp.float32)
        part = jnp.einsum('xzk,ky->xzy', part, ytable, precision=HIGH, preferred_element_type=jnp.float32)
        return jnp.einsum('kx,kzy->xzy', xtable, part, precision=HIGH, preferred_element_type=jnp.float32)
    field = lax.map(field_of, (now, z_extent))

    def back(arr):
        return arr.transpose(1, 0, 2, 3).reshape(NX, GROUPS * ZC, NY)
    return (back(now), back(prev), back(field))
```

```python
import math

import jax
import jax.numpy as jnp
import numpy as np
from jax import lax
from jax.sharding import PartitionSpec as P

STEPS = 2
HIGH = lax.Precision.HIGHEST
STENCIL = (-490.0 / 180.0, 270.0 / 180.0, -27.0 / 180.0, 2.0 / 180.0)
COURANT = 0.5
FACE = 3
HEAD = 8
TERMS = 9


def static_table(count):
    kk = np.arange(count)[:, None]
    xx = np.arange(count)[None, :]
    scale = np.where(kk == 0, np.sqrt(1.0 / count), np.sqrt(2.0 / count))
    return scale * np.cos(np.pi * kk * (xx + 0.5) / count)


def cosine_table(kk, xx, length):
    scale = jnp.where(kk == 0, jnp.sqrt(1.0 / length), jnp.sqrt(2.0 / length))
    return scale * jnp.cos(jnp.pi * kk * (xx + 0.5) / length)


def mul(spec, left, right):
    return jnp.einsum(spec, left, right, precision=HIGH, preferred_element_type=jnp.float32)


def gain_of(square):
    total = jnp.full_like(square, 0.0)
    for n in reversed(range(TERMS)):
        total = total * square + (-1) ** n * 2.0 / math.factorial(2 * n + 2)
    return total


def inner_size(count):
    best = 1
    for n in range(1, count + 1):
        if count % n == 0 and n * n <= count:
            best = n
    return best


def relation(table, move):
    count = table.shape[0]
    wide = jnp.asarray(np.pad(table, ((0, 0), (count, count))).astype(np.float32))
    plain = jnp.asarray(table.astype(np.float32))
    slid = lax.dynamic_slice(wide, (0, count + move), (count, count))
    at = jnp.arange(count) + move
    valid = ((at >= 0) & (at < count)).astype(jnp.float32)
    return mul("ax,bx->ab", plain, slid), mul("ax,bx->ab", plain * valid[None, :], plain)


def stencil(face, order):
    rows = []
    for jj in range(FACE):
        total = 0.0
        for mm in range(FACE - jj):
            total = total + STENCIL[jj + mm + 1] * face[order[mm]]
        rows.append(total)
    return rows


def shifts(count, width, hi):
    def to(step):
        pairs = []
        for at in range(count):
            h, l = divmod(at, width)
            if hi:
                pairs.append((at, (h + step) % (count // width) * width + l))
            else:
                pairs.append((at, h * width + (l + step) % width))
        return pairs

    return to


def route(face, target, source, group, hi_first):
    count = lax.axis_size("dom")
    width = inner_size(count)
    tall = count // width
    first, second = (tall, width) if hi_first else (width, tall)
    to_first = shifts(count, width, hi_first)
    to_second = shifts(count, width, not hi_first)
    head = jnp.full((HEAD, face.shape[1]), target, jnp.float32)
    packet = jnp.concatenate([face, head], axis=0)
    held = [packet] + [lax.ppermute(packet, "dom", to_first(k)) for k in range(1, first)]
    h, l = group // width, group % width
    rows = face.shape[0]
    result = None
    for k in range(second):
        dest = h * width + (l + k) % width if hi_first else (h + k) % tall * width + l
        dest = dest.astype(jnp.float32)
        chosen = held[0][:rows]
        for other in held[1:]:
            chosen = jnp.where(other[rows : rows + 1] == dest, other[:rows], chosen)
        if k:
            chosen = lax.ppermute(chosen, "dom", to_second(k))
        if hi_first:
            here = source % width == (l - k) % width
        else:
            here = source // width == (h - k) % tall
        result = chosen if result is None else jnp.where(here, chosen, result)
    return result


def over_split(piece, own):
    count = lax.axis_size("split")
    parts = [piece]
    for k in range(1, count):
        parts.append(lax.ppermute(piece, "split", [(i, (i + k) % count) for i in range(count)]))
    stacked = jnp.stack(parts, axis=0)
    return jnp.take(stacked, (own - jnp.arange(count)) % count, axis=0)


def whole_x(piece, own):
    rows = piece.shape[0]
    got = over_split(piece, own)
    return got.transpose(1, 0, 2, 3).reshape(rows, -1, piece.shape[2])


def on_device(modes_now, modes_prev, z_extent, lower_nbr, upper_nbr, x_shift, y_shift):
    slab, zcap, width = modes_now.shape
    parts = lax.axis_size("split")
    full = slab * parts
    own = lax.axis_index("split")
    group = lax.axis_index("dom")
    below, above = lower_nbr[0], upper_nbr[0]
    extent = z_extent[0]
    lenf = extent.astype(jnp.float32)
    zidx = jnp.arange(zcap)
    live = zidx < extent
    kz = zidx.astype(jnp.float32)
    near = cosine_table(kz[:, None], jnp.arange(FACE).astype(jnp.float32)[None, :], lenf)
    near = jnp.where(live[:, None], near, 0.0)
    sign = (1 - 2 * (zidx % 2)).astype(jnp.float32)[:, None]
    row_table = jnp.concatenate([near, near[:, ::-1] * sign], axis=1)
    keep = live.astype(jnp.float32)[None, :, None]
    now = modes_now * keep
    prev = modes_prev * keep
    strip = mul("kr,xky->rxy", row_table, now)

    def exchange(strip):
        low = strip[:FACE].reshape(FACE * slab, width)
        upp = strip[FACE:].reshape(FACE * slab, width)
        got_low = route(upp, above, below, group, True)
        got_up = route(low, below, above, group, False)
        return jnp.concatenate([got_low, got_up], axis=0).reshape(2 * FACE, slab, width)

    xtable = static_table(full)
    ytable = static_table(width)
    base = (COURANT * np.pi) ** 2
    allx = jnp.asarray((base * (np.arange(full) / full) ** 2).astype(np.float32))
    ally = jnp.asarray((base * (np.arange(width) / width) ** 2).astype(np.float32))
    allz = (base * (kz / lenf) ** 2).astype(jnp.float32)
    square = allx[:, None, None] + allz[None, :, None] + ally[None, None, :]
    gain = gain_of(square)
    twice_cos = 2.0 - square * gain
    start = own * slab
    gain_own = lax.dynamic_slice_in_dim(gain, start, slab, 0)
    cos_own = lax.dynamic_slice_in_dim(twice_cos, start, slab, 0)
    ahead = cos_own * now - prev
    strip_ahead = mul("kr,xky->rxy", row_table, ahead)
    free = cos_own * ahead - now

    ztable = jnp.where(
        live[:, None] & live[None, :], cosine_table(kz[:, None], kz[None, :], lenf), 0.0
    )
    xmat = jnp.asarray(xtable.astype(np.float32))
    ymat = jnp.asarray(ytable.astype(np.float32))

    field = mul("kz,xky->xzy", ztable, free)
    field = mul("xzk,ky->xzy", field, ymat)
    rows_own = lax.dynamic_slice_in_dim(xmat, start, slab, 0)
    pressure = mul("kx,kzy->xzy", lax.dynamic_slice_in_dim(rows_own, start, slab, 1), field)
    for k in range(1, parts):
        cols = lax.dynamic_slice_in_dim(rows_own, (own + k) % parts * slab, slab, 1)
        part = mul("kx,kzy->xzy", cols, field)
        pressure = pressure + lax.ppermute(part, "split", [(i, (i + k) % parts) for i in range(parts)])

    low_x, keep_low_x = relation(xtable, x_shift[0, 0])
    low_y, keep_low_y = relation(ytable, y_shift[0, 0])
    up_x, keep_up_x = relation(xtable, x_shift[0, 1])
    up_y, keep_up_y = relation(ytable, y_shift[0, 1])
    has = COURANT**2 * jnp.stack([(below >= 0), (above >= 0)]).astype(jnp.float32)
    take_x = jnp.stack([low_x, up_x])
    take_y = jnp.stack([low_y, up_y])
    keep_x = jnp.stack([keep_low_x, keep_up_x])
    keep_y = jnp.stack([keep_low_y, keep_up_y])

    def forcing(got, mine):
        far = jnp.stack([jnp.stack(stencil(got[:FACE], (2, 1, 0))), jnp.stack(stencil(got[FACE:], (0, 1, 2)))])
        near = jnp.stack([jnp.stack(stencil(mine[:FACE], (0, 1, 2))), jnp.stack(stencil(mine[FACE:], (2, 1, 0)))])
        far = mul("fax,frxy->fray", take_x, far)
        far = mul("fray,fby->frab", far, take_y)
        near = mul("fax,frxy->fray", keep_x, near)
        near = mul("fray,fby->frab", near, keep_y)
        both = (far - near) * has[:, None, None, None]
        return jnp.concatenate([both[0], both[1][::-1]], axis=0)

    pairs = row_table[:, :, None] * row_table[:, None, :]
    mixing = mul("krs,xky->rsxy", pairs, gain)
    mine = whole_x(strip, own)
    ahead_all = whole_x(strip_ahead, own)
    force1 = forcing(whole_x(exchange(strip), own), mine)
    strip_all = ahead_all + jnp.sum(mixing * force1[None], axis=1)
    strip2 = lax.dynamic_slice_in_dim(strip_all, start, slab, 1)
    got2 = whole_x(exchange(strip2), own)

    part1 = gain * mul("kr,rxy->xky", row_table, force1)
    modes_cur = ahead + lax.dynamic_slice_in_dim(part1, start, slab, 0)

    def finish(modes):
        out = mul("kz,xky->xzy", ztable, modes)
        out = mul("kx,kzy->xzy", lax.dynamic_slice_in_dim(xmat, start, slab, 1), out)
        return mul("xzk,ky->xzy", out, ymat)

    pressure = pressure + finish(twice_cos * part1)
    force2 = forcing(got2, strip_all)
    part2 = gain * mul("kr,rxy->xky", row_table, force2)
    modes_next = cos_own * modes_cur - now + lax.dynamic_slice_in_dim(part2, start, slab, 0)
    pressure = pressure + finish(part2)
    return (modes_next, modes_cur, pressure)


def solution(mesh):
    placed = (
        P("split", "dom", None),
        P("split", "dom", None),
        P("dom"),
        P("dom"),
        P("dom"),
        P("dom", None),
        P("dom", None),
    )
    return jax.shard_map(
        on_device,
        mesh=mesh,
        in_specs=placed,
        out_specs=(P("split", "dom", None), P("split", "dom", None), P("split", "dom", None)),
        check_vma=False,
    )
```

```python
import functools
import math

import jax
import jax.numpy as jnp
import numpy as np
from jax import lax
from jax.experimental import pallas as pl
from jax.experimental.pallas import tpu as pltpu
from jax.sharding import PartitionSpec as P

HIGH = lax.Precision.HIGHEST
F32 = jnp.float32
BF16 = jnp.bfloat16
STENCIL = (-490.0 / 180.0, 270.0 / 180.0, -27.0 / 180.0, 2.0 / 180.0)
COURANT = 0.5
FACE = 3
ROWS = 2 * FACE
HEAD = 8
TERMS = 9
SERIES = [(-1) ** n * 2.0 / math.factorial(2 * n + 2) for n in range(TERMS)]
BASE = (COURANT * math.pi) ** 2
PAIRS = [(r, q) for r in range(ROWS) for q in range(r, ROWS)]
VMEM = pl.BlockSpec(memory_space=pltpu.VMEM)
SMEM = pl.BlockSpec(memory_space=pltpu.SMEM)
ANY = pl.BlockSpec(memory_space=pl.ANY)
LIMIT = 40 * 1024 * 1024


def static_table(count):
    kk = np.arange(count)[:, None]
    xx = np.arange(count)[None, :]
    scale = np.where(kk == 0, np.sqrt(1.0 / count), np.sqrt(2.0 / count))
    return scale * np.cos(np.pi * kk * (xx + 0.5) / count)


def halves(table):
    high = table.astype(np.float32).astype(BF16)
    low = (table.astype(np.float32) - high.astype(np.float32)).astype(BF16)
    return high, low


def inner_size(count):
    best = 1
    for n in range(1, count + 1):
        if count % n == 0 and n * n <= count:
            best = n
    return best


def tall_split(data):
    high = data.astype(BF16).astype(F32)
    return jnp.concatenate([high, high, data - high], axis=0).astype(BF16)


def wide_split(data):
    high = data.astype(BF16)
    return jnp.concatenate([high, (data - high.astype(F32)).astype(BF16)], axis=1)


def dot(left, right):
    return jnp.dot(left, right, preferred_element_type=F32)


def exact_dot(left, right):
    return jnp.dot(left, right, precision=HIGH, preferred_element_type=F32)


def exact_dot_t(left, right):
    return lax.dot_general(
        left, right, (((1,), (1,)), ((), ())), precision=HIGH, preferred_element_type=F32
    )


def along_y(data, ystack):
    width = data.shape[1]
    both = dot(wide_split(data), ystack)
    return both[:, :width] + both[:, width:]


def cosine_of(count, odd, lenf):
    prod = count * odd
    turn = 4.0 * lenf
    rest = prod - jnp.floor(prod / turn) * turn
    return jnp.cos(rest * (0.5 * jnp.pi / lenf))


def scale_of(kk, lenf):
    return jnp.where(kk == 0, jnp.sqrt(1.0 / lenf), jnp.sqrt(2.0 / lenf))


def face_rows(near, flip, shape, extent):
    kk = lax.broadcasted_iota(jnp.int32, shape, 0)
    kf = kk.astype(F32)
    lenf = jnp.full(shape, extent.astype(F32))
    table = scale_of(kk, lenf) * cosine_of(kf, 2.0 * near + 1.0, lenf)
    sign = jnp.where((flip > 0) & (kk % 2 == 1), -1.0, 1.0)
    return jnp.where(kk < extent, table * sign, 0.0)


def gain_of(square):
    total = jnp.full_like(square, SERIES[-1])
    for value in reversed(SERIES[:-1]):
        total = total * square + value
    return total


def plane_square(shape, extent):
    kk = lax.broadcasted_iota(jnp.int32, shape, 0)
    kf = kk.astype(F32) / jnp.full(shape, extent.astype(F32))
    kf = jnp.where(kk < extent, kf, 0.0)
    ky = lax.broadcasted_iota(jnp.int32, shape, 1).astype(F32) / shape[1]
    return BASE * (kf * kf + ky * ky)


def x_square(kx, full):
    frac = kx.astype(F32) / full
    return BASE * (frac * frac)


def stencil(face, order):
    rows = []
    for jj in range(FACE):
        total = None
        for mm in range(FACE - jj):
            term = STENCIL[jj + mm + 1] * face[order[mm]]
            total = term if total is None else total + term
        rows.append(total)
    return rows


def through(planes, across, along):
    full, width = planes[0].shape
    out = exact_dot(across, jnp.concatenate(planes, axis=1))
    out = jnp.concatenate([out[:, i * width : (i + 1) * width] for i in range(FACE)], axis=0)
    out = exact_dot_t(out, along)
    return [out[i * full : (i + 1) * full] for i in range(FACE)]


def gather_kx(out, pieces, own):
    count = len(pieces)
    slab = pieces[0].shape[0] // ROWS
    full = slab * count
    for k, piece in enumerate(pieces):
        at = pl.multiple_of(lax.rem(own + count - k, count) * slab, slab)
        for r in range(ROWS):
            out[pl.ds(r * full + at, slab), :] = piece[r * slab : (r + 1) * slab, :]


def plane(ref, r):
    full = ref.shape[0] // ROWS
    return ref[r * full : (r + 1) * full, :]


def call(kernel, out_shape, in_specs, scratch=(), flops=0, moved=0, name=None, out_specs=None):
    if out_specs is None:
        out_specs = [VMEM] * len(out_shape)
    return pl.pallas_call(
        kernel,
        out_shape=out_shape,
        in_specs=in_specs,
        out_specs=out_specs,
        scratch_shapes=list(scratch),
        compiler_params=pltpu.CompilerParams(vmem_limit_bytes=LIMIT),
        cost_estimate=pl.CostEstimate(flops=flops, bytes_accessed=moved, transcendentals=0),
        name=name,
    )


def shape_of(*dims, dtype=F32):
    return jax.ShapeDtypeStruct(dims, dtype)


def strip_kernel(extent, below, above, now, lanes, packet, rows):
    slab, zcap, width = now.shape
    table = face_rows(lanes[0:1, :], lanes[1:2, :], (zcap, width), extent[0])
    rows[...] = table
    for r in range(ROWS):
        weight = jnp.broadcast_to(table[:, r : r + 1], (zcap, width))
        packet[r * slab : (r + 1) * slab, :] = jnp.sum(now[...] * weight[None], axis=1)
    at = lax.broadcasted_iota(jnp.int32, (HEAD, width), 0)
    names = jnp.where(at < HEAD // 2, above[0], below[0])
    packet[ROWS * slab :, :] = names.astype(F32)


def ahead_kernel(
    extent, own, now, prev, rows, lanes, series, xparts, ystack,
    strip, free, zstack, coefs, field, *, full,
):
    slab, zcap, width = now.shape
    ext = extent[0]
    kk = lax.broadcasted_iota(jnp.int32, (zcap, zcap), 1)
    zz = lax.broadcasted_iota(jnp.int32, (zcap, zcap), 0)
    lenf = jnp.full((zcap, zcap), ext.astype(F32))
    ztable = scale_of(kk, lenf) * cosine_of(kk.astype(F32), 2.0 * zz.astype(F32) + 1.0, lenf)
    ztable = jnp.where((kk < ext) & (zz < ext), ztable, 0.0)
    high = ztable.astype(BF16).astype(F32)
    stacked = jnp.concatenate([high, ztable - high, high], axis=1).astype(BF16)
    zstack[...] = stacked

    kz = lax.broadcasted_iota(jnp.int32, (zcap, width), 0)
    bz = kz.astype(F32) / jnp.full((zcap, width), ext.astype(F32))
    bz = jnp.where(kz < ext, BASE * bz * bz, 0.0)
    total = jnp.zeros((zcap, width), F32)
    for j in reversed(range(TERMS)):
        total = total * bz + series[j : j + 1, :]
    pairs = face_rows(lanes[2:3, :], lanes[3:4, :], (zcap, width), ext)
    pairs = pairs * face_rows(lanes[4:5, :], lanes[5:6, :], (zcap, width), ext)
    coefs[...] = exact_dot(total.T[: coefs.shape[0]], pairs)

    keep = lax.broadcasted_iota(jnp.int32, (zcap, width), 0) < ext
    square = plane_square((zcap, width), ext)
    weights = [jnp.broadcast_to(rows[:, r : r + 1], (zcap, width)) for r in range(ROWS)]

    def body(i, _):
        frees = []
        for half in range(2):
            kx = 2 * i + half
            local = square + x_square(own[0] * slab + kx, full)
            twice = 2.0 - local * gain_of(local)
            first = jnp.where(keep, now[kx], 0.0)
            ahead = twice * first - jnp.where(keep, prev[kx], 0.0)
            for r in range(ROWS):
                strip[pl.ds(r * slab + kx, 1), :] = jnp.sum(
                    ahead * weights[r], axis=0, keepdims=True
                )
            frees.append(twice * ahead - first)
        wide = dot(stacked, tall_split(jnp.concatenate(frees, axis=1)))
        for half in range(2):
            at = pl.multiple_of((2 * i + half) * zcap, zcap)
            field[pl.ds(at, zcap), :] = wide[:, half * width : (half + 1) * width]
        return 0

    lax.fori_loop(0, slab // 2, body, 0)
    block = min(8, slab) * zcap

    def turn(i, _):
        at = pl.multiple_of(i * block, block)
        field[pl.ds(at, block), :] = along_y(field[pl.ds(at, block), :], ystack[...])
        return 0

    lax.fori_loop(0, slab * zcap // block, turn, 0)
    parts = full // slab
    across = xparts[own[0]]

    def spread(i, _):
        pair = [field[pl.ds(2 * i + half, slab, stride=zcap), :] for half in range(2)]
        wide = dot(across, tall_split(jnp.concatenate(pair, axis=1)))
        for k in range(parts):
            for half in range(2):
                free[k, pl.ds(2 * i + half, slab, stride=zcap), :] = wide[
                    k * slab : (k + 1) * slab, half * width : (half + 1) * width
                ]
        return 0

    lax.fori_loop(0, zcap // 2, spread, 0)


def relation_kernel(
    below, above, x_shift, y_shift, own, coefs, after, xplain, xtall, yplain, ytall, *rest, parts
):
    strips, (tx, uy, vx, wy, near, mixing, mine) = rest[:parts], rest[parts:]
    full, width = xplain.shape[0], yplain.shape[0]
    for f, (nbr, dx, dy) in enumerate(
        ((below, x_shift[0, 0], y_shift[0, 0]), (above, x_shift[0, 1], y_shift[0, 1]))
    ):
        has = jnp.where(nbr[0] >= 0, COURANT**2, 0.0).astype(F32)
        for count, move, plain, tall, take, keep, scale in (
            (full, dx, xplain, xtall, tx, vx, has),
            (width, dy, yplain, ytall, uy, wy, None),
        ):
            move = jnp.clip(move, -count, count)
            slid = tall[pl.ds(count + move, count), :]
            at = lax.broadcasted_iota(jnp.int32, (count, count), 0) + move
            kept = jnp.where((at >= 0) & (at < count), tall[count : 2 * count, :], 0.0)
            taken, stay = exact_dot(plain[...], slid), exact_dot(plain[...], kept)
            take[f] = taken if scale is None else taken * scale
            keep[f] = stay if scale is None else stay * scale
    gather_kx(mine, strips, own[0])
    near_planes(mine, vx, wy, near)
    shape = (full, width)
    ax = lax.broadcasted_iota(jnp.int32, shape, 0).astype(F32) / full
    ay = lax.broadcasted_iota(jnp.int32, shape, 1).astype(F32) / width
    square = BASE * (ax * ax + ay * ay)
    for p in range(len(PAIRS)):
        total = jnp.full(shape, coefs[TERMS - 1, p])
        for n in reversed(range(TERMS - 1)):
            total = total * square + coefs[n, p]
        mixing[p] = total


def near_planes(mine, vx, wy, near):
    full = vx.shape[1]
    low = through(stencil([plane(mine, r) for r in range(FACE)], (0, 1, 2)), vx[0], wy[0])
    upp = through(stencil([plane(mine, FACE + r) for r in range(FACE)], (2, 1, 0)), vx[1], wy[1])
    for r, value in enumerate(low + upp[::-1]):
        near[r * full : (r + 1) * full, :] = value


def force_planes(far, near, tx, uy, force):
    full = tx.shape[1]
    low = through(stencil([plane(far, r) for r in range(FACE)], (2, 1, 0)), tx[0], uy[0])
    upp = through(stencil([plane(far, FACE + r) for r in range(FACE)], (0, 1, 2)), tx[1], uy[1])
    for r, value in enumerate(low + upp[::-1]):
        force[r * full : (r + 1) * full, :] = value - plane(near, r)


def choose_kernel(group, *refs, width):
    held, out = refs[:width], refs[width:]
    rows = out[0].shape[0]
    half = rows // 2
    h, l = group[0] // width, lax.rem(group[0], width)
    for k in range(len(out)):
        dest = (lax.rem(h + k, len(out)) * width + l).astype(F32)
        for f in range(2):
            lo, hi = f * half, (f + 1) * half
            row = rows + (0 if f == 1 else HEAD // 2)
            chosen = held[0][lo:hi, :]
            for other in held[1:]:
                chosen = jnp.where(other[row : row + 1, :] == dest, other[lo:hi, :], chosen)
            out[k][lo:hi, :] = chosen


def pick_kernel(group, below, above, *refs, tall, width):
    got, out = refs[:-1], refs[-1]
    half = out.shape[0] // 2
    h = group[0] // width
    for f, nbr in enumerate((below, above)):
        lo = half if f == 0 else 0
        value = got[0][lo : lo + half, :]
        for k in range(1, tall):
            here = jnp.maximum(nbr[0], 0) // width == lax.rem(h + tall - k, tall)
            value = jnp.where(here, got[k][lo : lo + half, :], value)
        out[f * half : (f + 1) * half, :] = value


def middle_kernel(own, below, above, near, tx, uy, mixing, *rest, parts):
    far, ahead = rest[:parts], rest[parts : 2 * parts]
    packet, force, strip, spare = rest[2 * parts :]
    gather_kx(spare, far, own[0])
    force_planes(spare, near, tx, uy, force)
    gather_kx(strip, ahead, own[0])
    full = tx.shape[1]
    slab = full // parts
    for r in range(ROWS):
        total = plane(strip, r)
        for q in range(ROWS):
            total = total + mixing[PAIRS.index((min(r, q), max(r, q)))] * plane(force, q)
        strip[r * full : (r + 1) * full, :] = total
    at = pl.multiple_of(own[0] * slab, slab)
    for r in range(ROWS):
        packet[r * slab : (r + 1) * slab, :] = strip[pl.ds(r * full + at, slab), :]
    at = lax.broadcasted_iota(jnp.int32, (HEAD, packet.shape[1]), 0)
    names = jnp.where(at < HEAD // 2, above[0], below[0])
    packet[ROWS * slab :, :] = names.astype(F32)


def near_kernel(strip, vx, wy, near):
    near_planes(strip, vx, wy, near)


def lift(ext, own, force, rows, zstack, ystack, xown, store, field, turned, full, lead):
    zcap, width = rows.shape
    slab = turned.shape[0] // zcap
    square = plane_square((zcap, width), ext)
    weights = [jnp.broadcast_to(rows[:, r : r + 1], (zcap, width)) for r in range(ROWS)]

    def body(i, _):
        planes = []
        for half in range(2):
            kx = 2 * i + half
            local = square + x_square(kx, full)
            gain = gain_of(local)
            total = None
            for r in range(ROWS):
                term = weights[r] * force[pl.ds(r * full + kx, 1), :]
                total = term if total is None else total + term
            total = gain * total
            planes.append(lead(local, gain) * total if lead else total)
            store(kx, local, gain, total)
        wide = dot(zstack[...], tall_split(jnp.concatenate(planes, axis=1)))
        for half in range(2):
            at = pl.multiple_of((2 * i + half) * zcap, zcap)
            field[pl.ds(at, zcap), :] = wide[:, half * width : (half + 1) * width]
        return 0

    lax.fori_loop(0, full // 2, body, 0)
    across = xown[own]

    def spread(i, _):
        pair = [field[pl.ds(2 * i + half, full, stride=zcap), :] for half in range(2)]
        wide = dot(across, tall_split(jnp.concatenate(pair, axis=1)))
        for half in range(2):
            turned[pl.ds(2 * i + half, slab, stride=zcap), :] = wide[
                :, half * width : (half + 1) * width
            ]
        return 0

    lax.fori_loop(0, zcap // 2, spread, 0)


def between_kernel(
    extent, own, now, prev, force, rows, zstack, ystack, xown, free,
    current, onward, summed, field, turned, *, full,
):
    slab, zcap, width = now.shape
    keep = lax.broadcasted_iota(jnp.int32, (zcap, width), 0) < extent[0]

    def store(kx, local, gain, total):
        at = kx - own[0] * slab

        @pl.when((at >= 0) & (at < slab))
        def _():
            twice = 2.0 - local * gain
            first = jnp.where(keep, now[at], 0.0)
            value = twice * first - jnp.where(keep, prev[at], 0.0) + total
            current[at] = value
            onward[at] = twice * value - first

    lift(
        extent[0], own[0], force, rows, zstack, ystack, xown, store, field, turned, full,
        lambda local, gain: 2.0 - local * gain,
    )
    block = min(8, slab) * zcap

    def turn(i, _):
        at = pl.multiple_of(i * block, block)
        summed[pl.ds(at, block), :] = free[0, pl.ds(at, block), :] + along_y(
            turned[pl.ds(at, block), :], ystack[...]
        )
        return 0

    lax.fori_loop(0, slab * zcap // block, turn, 0)


def last_kernel(
    extent, own, near, tx, uy, onward, summed, rows, zstack, ystack, xown, *rest, full, parts
):
    far, given = rest[:parts], rest[parts : 2 * parts - 1]
    modes, pressure, spare, force, field, turned = rest[2 * parts - 1 :]
    slab, zcap, width = onward.shape
    gather_kx(spare, far, own[0])
    force_planes(spare, near, tx, uy, force)

    def store(kx, local, gain, total):
        at = kx - own[0] * slab

        @pl.when((at >= 0) & (at < slab))
        def _():
            modes[at] = onward[at] + total

    lift(
        extent[0], own[0], force, rows, zstack, ystack, xown, store, field, turned, full, None
    )
    block = min(8, slab) * zcap

    def turn(i, _):
        at = pl.multiple_of(i * block, block)
        value = summed[pl.ds(at, block), :]
        for piece in given:
            value = value + piece[pl.ds(at, block), :]
        pressure[pl.ds(at, block), :] = value + along_y(turned[pl.ds(at, block), :], ystack[...])
        return 0

    lax.fori_loop(0, slab * zcap // block, turn, 0)


def on_device(modes_now, modes_prev, z_extent, lower_nbr, upper_nbr, x_shift, y_shift):
    slab, zcap, width = modes_now.shape
    parts = lax.axis_size("split")
    count = lax.axis_size("dom")
    full = slab * parts
    own = lax.axis_index("split").astype(jnp.int32)[None]
    group = lax.axis_index("dom").astype(jnp.int32)[None]
    inner = inner_size(count)
    tall = count // inner
    size = ROWS * slab
    big = 4 * slab * zcap * width

    xtable, ytable = static_table(full), static_table(width)
    lanes = np.zeros((8, width), np.float32)
    for r in range(ROWS):
        lanes[0, r], lanes[1, r] = (r, 0) if r < FACE else (ROWS - 1 - r, 1)
    for p, (r, q) in enumerate(PAIRS):
        lanes[2, p], lanes[3, p] = lanes[0, r], lanes[1, r]
        lanes[4, p], lanes[5, p] = lanes[0, q], lanes[1, q]
    series = np.zeros((16, width), np.float32)
    for j in range(TERMS):
        for n in range(TERMS - j):
            series[j, n] = SERIES[n + j] * math.comb(n + j, n)
    yhigh, ylow = halves(ytable)
    ystack = np.block([[yhigh, ylow], [yhigh, np.zeros_like(yhigh)]])
    xhigh, xlow = halves(xtable.T)
    xown = np.stack(
        [
            np.concatenate([t[s * slab : (s + 1) * slab] for t in (xhigh, xlow, xhigh)], axis=1)
            for s in range(parts)
        ]
    )
    xparts = np.stack(
        [
            np.concatenate(
                [
                    np.concatenate(
                        [
                            t[(s + k) % parts * slab : ((s + k) % parts + 1) * slab,
                              s * slab : (s + 1) * slab]
                            for k in range(parts)
                        ],
                        axis=0,
                    )
                    for t in (xhigh, xlow, xhigh)
                ],
                axis=1,
            )
            for s in range(parts)
        ]
    )

    def tall_of(table):
        n = table.shape[0]
        return np.pad(table.T, ((n, n), (0, 0))).astype(np.float32)

    lanes, series, ystack, xown, xparts = map(jnp.asarray, (lanes, series, ystack, xown, xparts))
    xplain, xtall = jnp.asarray(xtable.astype(np.float32)), jnp.asarray(tall_of(xtable))
    yplain, ytall = jnp.asarray(ytable.astype(np.float32)), jnp.asarray(tall_of(ytable))

    def swap(piece):
        got = [piece]
        for k in range(1, parts):
            got.append(lax.ppermute(piece, "split", [(i, (i + k) % parts) for i in range(parts)]))
        return got

    def spread(packet):
        held = [packet]
        for k in range(1, inner):
            to = [(i, i // inner * inner + (i + k) % inner) for i in range(count)]
            held.append(lax.ppermute(packet, "dom", to))
        return call(
            functools.partial(choose_kernel, width=inner),
            [shape_of(size, width)] * tall,
            [SMEM] + [VMEM] * inner,
            moved=8 * size * width * 4,
            name="choose",
        )(group, *held)

    def deliver(chosen):
        got = [chosen[0]]
        for k in range(1, tall):
            to = [(i, (i + k * inner) % count) for i in range(count)]
            got.append(lax.ppermute(chosen[k], "dom", to))
        picked = call(
            functools.partial(pick_kernel, tall=tall, width=inner),
            [shape_of(size, width)],
            [SMEM] * 3 + [VMEM] * tall,
            moved=5 * size * width * 4,
            name="pick",
        )(group, lower_nbr, upper_nbr, *got)[0]
        return swap(picked)

    packet, rows = call(
        strip_kernel,
        [shape_of(size + HEAD, width), shape_of(zcap, width)],
        [SMEM] * 3 + [VMEM] * 2,
        moved=big,
        name="strip",
    )(z_extent, lower_nbr, upper_nbr, modes_now, lanes)
    chosen = spread(packet)
    mine = swap(packet[:size])

    ahead, free, zstack, coefs = call(
        functools.partial(ahead_kernel, full=full),
        [
            shape_of(size, width),
            shape_of(parts, slab * zcap, width),
            shape_of(zcap, 3 * zcap, dtype=BF16),
            shape_of(16, width),
        ],
        [SMEM] * 2 + [VMEM] * 7,
        scratch=[pltpu.VMEM((slab * zcap, width), F32)],
        flops=10**9,
        moved=4 * big,
        name="ahead",
    )(z_extent, own, modes_now, modes_prev, rows, lanes, series, xparts, ystack)
    aheads = swap(ahead)
    given = [
        lax.ppermute(free[k], "split", [(i, (i + k) % parts) for i in range(parts)])
        for k in range(1, parts)
    ]

    tx, uy, vx, wy, near1, mixing, _ = call(
        functools.partial(relation_kernel, parts=parts),
        [
            shape_of(2, full, full),
            shape_of(2, width, width),
            shape_of(2, full, full),
            shape_of(2, width, width),
            shape_of(ROWS * full, width),
            shape_of(len(PAIRS), full, width),
            shape_of(ROWS * full, width),
        ],
        [SMEM] * 6 + [ANY] + [VMEM] * (4 + parts),
        flops=10**8,
        moved=2 * big,
        name="relation",
    )(
        lower_nbr, upper_nbr, x_shift, y_shift, own, coefs, chosen[0],
        xplain, xtall, yplain, ytall, *mine,
    )

    packet2, force1, strip2 = call(
        functools.partial(middle_kernel, parts=parts),
        [
            shape_of(size + HEAD, width),
            shape_of(ROWS * full, width),
            shape_of(ROWS * full, width),
        ],
        [SMEM] * 3 + [VMEM] * (4 + 2 * parts),
        scratch=[pltpu.VMEM((ROWS * full, width), F32)],
        flops=10**8,
        moved=2 * big,
        name="middle",
    )(own, lower_nbr, upper_nbr, near1, tx, uy, mixing, *deliver(chosen), *aheads)

    chosen2 = spread(packet2)
    current, onward, summed = call(
        functools.partial(between_kernel, full=full),
        [
            shape_of(slab, zcap, width),
            shape_of(slab, zcap, width),
            shape_of(slab * zcap, width),
        ],
        [SMEM] * 2 + [VMEM] * 8,
        scratch=[
            pltpu.VMEM((full * zcap, width), F32),
            pltpu.VMEM((slab * zcap, width), F32),
        ],
        flops=10**9,
        moved=6 * big,
        name="between",
    )(z_extent, own, modes_now, modes_prev, force1, rows, zstack, ystack, xown, free)
    near2 = call(
        near_kernel,
        [shape_of(ROWS * full, width)],
        [VMEM] * 3,
        flops=10**7,
        moved=big,
        name="near",
    )(strip2, vx, wy)[0]

    modes, pressure = call(
        functools.partial(last_kernel, full=full, parts=parts),
        [shape_of(slab, zcap, width), shape_of(slab * zcap, width)],
        [SMEM] * 2 + [VMEM] * (9 + 2 * parts - 1),
        scratch=[
            pltpu.VMEM((ROWS * full, width), F32),
            pltpu.VMEM((ROWS * full, width), F32),
            pltpu.VMEM((full * zcap, width), F32),
            pltpu.VMEM((slab * zcap, width), F32),
        ],
        flops=10**9,
        moved=6 * big,
        name="last",
    )(
        z_extent, own, near2, tx, uy, onward, summed, rows, zstack, ystack, xown,
        *deliver(chosen2), *given,
    )
    return (modes, current, pressure.reshape(slab, zcap, width))


def solution(mesh):
    placed = (
        P("split", "dom", None),
        P("split", "dom", None),
        P("dom"),
        P("dom"),
        P("dom"),
        P("dom", None),
        P("dom", None),
    )
    return jax.shard_map(
        on_device,
        mesh=mesh,
        in_specs=placed,
        out_specs=(P("split", "dom", None), P("split", "dom", None), P("split", "dom", None)),
        check_vma=False,
    )
```

```python
import functools
import math

import jax
import jax.numpy as jnp
import numpy as np
from jax import lax
from jax.experimental import pallas as pl
from jax.experimental.pallas import tpu as pltpu
from jax.sharding import PartitionSpec as P

HIGH = lax.Precision.HIGHEST
F32 = jnp.float32
BF16 = jnp.bfloat16
STENCIL = (-490.0 / 180.0, 270.0 / 180.0, -27.0 / 180.0, 2.0 / 180.0)
COURANT = 0.5
FACE = 3
ROWS = 2 * FACE
HEAD = 8
SERIES = [(-1) ** n * 2.0 / math.factorial(2 * n + 2) for n in range(10)]
TERMS = 7
BASE = (COURANT * math.pi) ** 2
PAIRS = [(r, q) for r in range(ROWS) for q in range(r, ROWS)]
VMEM = pl.BlockSpec(memory_space=pltpu.VMEM)
SMEM = pl.BlockSpec(memory_space=pltpu.SMEM)
ANY = pl.BlockSpec(memory_space=pl.ANY)
LIMIT = 12 * 1024 * 1024


def static_table(count):
    kk = np.arange(count)[:, None]
    xx = np.arange(count)[None, :]
    scale = np.where(kk == 0, np.sqrt(1.0 / count), np.sqrt(2.0 / count))
    return scale * np.cos(np.pi * kk * (xx + 0.5) / count)


def halves(table):
    high = table.astype(np.float32).astype(BF16)
    low = (table.astype(np.float32) - high.astype(np.float32)).astype(BF16)
    return high, low


def inner_size(count):
    best = 1
    for n in range(1, count + 1):
        if count % n == 0 and n * n <= count:
            best = n
    return best


def tall_split(data):
    high = data.astype(BF16).astype(F32)
    return jnp.concatenate([high, high, data - high], axis=0).astype(BF16)


def wide_split(data):
    high = data.astype(BF16)
    return jnp.concatenate([high, (data - high.astype(F32)).astype(BF16)], axis=1)


def dot(left, right):
    return jnp.dot(left, right, preferred_element_type=F32)


def exact_dot(left, right):
    return jnp.dot(left, right, precision=HIGH, preferred_element_type=F32)


def exact_dot_t(left, right):
    return lax.dot_general(
        left, right, (((1,), (1,)), ((), ())), precision=HIGH, preferred_element_type=F32
    )


def along_y(data, ystack):
    width = data.shape[1]
    both = dot(wide_split(data), ystack)
    return both[:, :width] + both[:, width:]


def cosine_of(count, odd, lenf):
    prod = count * odd
    turn = 4.0 * lenf
    rest = prod - jnp.floor(prod / turn) * turn
    return jnp.cos(rest * (0.5 * jnp.pi / lenf))


def scale_of(kk, lenf):
    return jnp.where(kk == 0, jnp.sqrt(1.0 / lenf), jnp.sqrt(2.0 / lenf))


def face_rows(near, flip, shape, extent):
    kk = lax.broadcasted_iota(jnp.int32, shape, 0)
    kf = kk.astype(F32)
    lenf = jnp.full(shape, extent.astype(F32))
    table = scale_of(kk, lenf) * cosine_of(kf, 2.0 * near + 1.0, lenf)
    sign = jnp.where((flip > 0) & (kk % 2 == 1), -1.0, 1.0)
    return jnp.where(kk < extent, table * sign, 0.0)


def gain_of(square):
    total = jnp.full_like(square, SERIES[-1])
    for value in reversed(SERIES[:-1]):
        total = total * square + value
    return total


def plane_square(shape, extent):
    kk = lax.broadcasted_iota(jnp.int32, shape, 0)
    kf = kk.astype(F32) / jnp.full(shape, extent.astype(F32))
    kf = jnp.where(kk < extent, kf, 0.0)
    ky = lax.broadcasted_iota(jnp.int32, shape, 1).astype(F32) / shape[1]
    return BASE * (kf * kf + ky * ky)


def x_square(kx, full):
    frac = kx.astype(F32) / full
    return BASE * (frac * frac)


def stencil(face, order):
    rows = []
    for jj in range(FACE):
        total = None
        for mm in range(FACE - jj):
            term = STENCIL[jj + mm + 1] * face[order[mm]]
            total = term if total is None else total + term
        rows.append(total)
    return rows


def through(planes, across, along):
    full, width = planes[0].shape
    out = exact_dot(across, jnp.concatenate(planes, axis=1))
    out = jnp.concatenate([out[:, i * width : (i + 1) * width] for i in range(FACE)], axis=0)
    out = exact_dot_t(out, along)
    return [out[i * full : (i + 1) * full] for i in range(FACE)]


def gather_kx(out, pieces, own):
    count = len(pieces)
    slab = pieces[0].shape[0] // ROWS
    full = slab * count
    for k, piece in enumerate(pieces):
        at = pl.multiple_of(lax.rem(own + count - k, count) * slab, slab)
        for r in range(ROWS):
            out[pl.ds(r * full + at, slab), :] = piece[r * slab : (r + 1) * slab, :]


def plane(ref, r):
    full = ref.shape[0] // ROWS
    return ref[r * full : (r + 1) * full, :]


def call(kernel, out_shape, in_specs, scratch=(), flops=0, moved=0, name=None, out_specs=None):
    if out_specs is None:
        out_specs = [VMEM] * len(out_shape)
    return pl.pallas_call(
        kernel,
        out_shape=out_shape,
        in_specs=in_specs,
        out_specs=out_specs,
        scratch_shapes=list(scratch),
        compiler_params=pltpu.CompilerParams(vmem_limit_bytes=LIMIT),
        cost_estimate=pl.CostEstimate(flops=flops, bytes_accessed=moved, transcendentals=0),
        name=name,
    )


def shape_of(*dims, dtype=F32):
    return jax.ShapeDtypeStruct(dims, dtype)


def strip_kernel(extent, below, above, now, consts, packet, rows):
    slab, zcap, width = now.shape
    table = face_rows(consts[0:1, :], consts[1:2, :], (zcap, width), extent[0])
    rows[...] = table
    for r in range(ROWS):
        weight = jnp.broadcast_to(table[:, r : r + 1], (zcap, width))
        packet[r * slab : (r + 1) * slab, :] = jnp.sum(now[...] * weight[None], axis=1)
    at = lax.broadcasted_iota(jnp.int32, (HEAD, width), 0)
    names = jnp.where(at < HEAD // 2, above[0], below[0])
    packet[ROWS * slab :, :] = names.astype(F32)


def lane_series(consts, first, shape, extent):
    kz = lax.broadcasted_iota(jnp.int32, shape, 0)
    frac = kz.astype(F32) / jnp.full(shape, extent.astype(F32))
    middle = jnp.where(kz < extent, BASE * frac * frac, 0.0) + BASE
    total = jnp.zeros(shape, F32)
    for j in reversed(range(len(SERIES))):
        total = total * middle + consts[first + j : first + j + 1, :]
    return total


def stack_lanes(table, depth):
    table = table[:, :depth]
    high = table.astype(BF16).astype(F32)
    return jnp.concatenate([high, table - high, high], axis=1).astype(BF16)


def ahead_kernel(
    extent, own, now, prev, rows, consts, strip, zstack, estack, hstack, coefs, *, full
):
    slab, zcap, width = now.shape
    ext = extent[0]
    kk = lax.broadcasted_iota(jnp.int32, (zcap, zcap), 1)
    zz = lax.broadcasted_iota(jnp.int32, (zcap, zcap), 0)
    lenf = jnp.full((zcap, zcap), ext.astype(F32))
    ztable = scale_of(kk, lenf) * cosine_of(kk.astype(F32), 2.0 * zz.astype(F32) + 1.0, lenf)
    ztable = jnp.where((kk < ext) & (zz < ext), ztable, 0.0)
    zstack[...] = stack_lanes(ztable, zcap)

    shape = (zcap, width)
    pairs = face_rows(consts[2:3, :], consts[3:4, :], shape, ext)
    pairs = pairs * face_rows(consts[4:5, :], consts[5:6, :], shape, ext)
    coefs[...] = exact_dot(lane_series(consts, 8, shape, ext).T[: coefs.shape[0]], pairs)
    terms = face_rows(consts[6:7, :], consts[7:8, :], shape, ext)
    terms = terms * lane_series(consts, 24, shape, ext)
    depth = estack.shape[1] // 3
    estack[...] = stack_lanes(terms, depth)
    hstack[...] = stack_lanes(exact_dot(ztable, terms), depth)

    keep = lax.broadcasted_iota(jnp.int32, shape, 0) < ext
    square = plane_square(shape, ext)
    weights = [jnp.broadcast_to(rows[:, r : r + 1], shape) for r in range(ROWS)]
    group = min(4, slab)

    def body(i, _):
        for half in range(group):
            kx = group * i + half
            local = square + x_square(own[0] * slab + kx, full)
            twice = 2.0 - local * gain_of(local)
            ahead = twice * now[kx] - prev[kx]
            ahead = jnp.where(keep, ahead, 0.0)
            for r in range(ROWS):
                strip[pl.ds(r * slab + kx, 1), :] = jnp.sum(
                    ahead * weights[r], axis=0, keepdims=True
                )
        return 0

    lax.fori_loop(0, slab // group, body, 0)


def relation_kernel(
    below, above, x_shift, y_shift, own, coefs, after, xtall, ytall, *rest, parts
):
    strips, (tx, uy, vx, wy, near, mixing, mine) = rest[:parts], rest[parts:]
    full, width = xtall.shape[1], ytall.shape[1]
    for f, (nbr, dx, dy) in enumerate(
        ((below, x_shift[0, 0], y_shift[0, 0]), (above, x_shift[0, 1], y_shift[0, 1]))
    ):
        has = jnp.where(nbr[0] >= 0, COURANT**2, 0.0).astype(F32)
        for count, move, tall, take, keep, scale in (
            (full, dx, xtall, tx, vx, has),
            (width, dy, ytall, uy, wy, None),
        ):
            move = jnp.clip(move, -count, count)
            slid = tall[pl.ds(count + move, count), :]
            at = lax.broadcasted_iota(jnp.int32, (count, count), 0) + move
            kept = jnp.where((at >= 0) & (at < count), tall[count : 2 * count, :], 0.0)
            plain = tall[3 * count :, :]
            taken, stay = exact_dot(plain, slid), exact_dot(plain, kept)
            take[f] = taken if scale is None else taken * scale
            keep[f] = stay if scale is None else stay * scale
    gather_kx(mine, strips, own[0])
    near_planes(mine, vx, wy, near)
    shape = (full, width)
    ax = lax.broadcasted_iota(jnp.int32, shape, 0).astype(F32) / full
    ay = lax.broadcasted_iota(jnp.int32, shape, 1).astype(F32) / width
    square = BASE * (ax * ax + ay * ay) - BASE
    for p in range(len(PAIRS)):
        total = jnp.full(shape, coefs[TERMS - 1, p])
        for n in reversed(range(TERMS - 1)):
            total = total * square + coefs[n, p]
        mixing[p] = total


def near_planes(mine, vx, wy, near):
    full = vx.shape[1]
    low = through(stencil([plane(mine, r) for r in range(FACE)], (0, 1, 2)), vx[0], wy[0])
    upp = through(stencil([plane(mine, FACE + r) for r in range(FACE)], (2, 1, 0)), vx[1], wy[1])
    for r, value in enumerate(low + upp[::-1]):
        near[r * full : (r + 1) * full, :] = value


def force_planes(far, near, tx, uy, force):
    full = tx.shape[1]
    low = through(stencil([plane(far, r) for r in range(FACE)], (2, 1, 0)), tx[0], uy[0])
    upp = through(stencil([plane(far, FACE + r) for r in range(FACE)], (0, 1, 2)), tx[1], uy[1])
    for r, value in enumerate(low + upp[::-1]):
        force[r * full : (r + 1) * full, :] = value - plane(near, r)


def choose_kernel(group, *refs, width):
    held, out = refs[:width], refs[width:]
    rows = out[0].shape[0]
    half = rows // 2
    h, l = group[0] // width, lax.rem(group[0], width)
    for k in range(len(out)):
        dest = (lax.rem(h + k, len(out)) * width + l).astype(F32)
        for f in range(2):
            lo, hi = f * half, (f + 1) * half
            row = rows + (0 if f == 1 else HEAD // 2)
            chosen = held[0][lo:hi, :]
            for other in held[1:]:
                chosen = jnp.where(other[row : row + 1, :] == dest, other[lo:hi, :], chosen)
            out[k][lo:hi, :] = chosen


def pick_kernel(group, below, above, *refs, tall, width):
    got, out = refs[:-1], refs[-1]
    half = out.shape[0] // 2
    h = group[0] // width
    for f, nbr in enumerate((below, above)):
        lo = half if f == 0 else 0
        value = got[0][lo : lo + half, :]
        for k in range(1, tall):
            here = jnp.maximum(nbr[0], 0) // width == lax.rem(h + tall - k, tall)
            value = jnp.where(here, got[k][lo : lo + half, :], value)
        out[f * half : (f + 1) * half, :] = value


def middle_kernel(own, below, above, near, tx, uy, mixing, *rest, parts):
    far, ahead = rest[:parts], rest[parts : 2 * parts]
    packet, force, strip, spare = rest[2 * parts :]
    gather_kx(spare, far, own[0])
    force_planes(spare, near, tx, uy, force)
    gather_kx(strip, ahead, own[0])
    full = tx.shape[1]
    slab = full // parts
    for r in range(ROWS):
        total = plane(strip, r)
        for q in range(ROWS):
            total = total + mixing[PAIRS.index((min(r, q), max(r, q)))] * plane(force, q)
        strip[r * full : (r + 1) * full, :] = total
    at = pl.multiple_of(own[0] * slab, slab)
    for r in range(ROWS):
        packet[r * slab : (r + 1) * slab, :] = strip[pl.ds(r * full + at, slab), :]
    at = lax.broadcasted_iota(jnp.int32, (HEAD, packet.shape[1]), 0)
    names = jnp.where(at < HEAD // 2, above[0], below[0])
    packet[ROWS * slab :, :] = names.astype(F32)


def near_kernel(strip, vx, wy, near):
    near_planes(strip, vx, wy, near)


def between_kernel(
    extent, own, now, prev, force, rows, zstack, ystack, xparts, current, onward, *rest, full,
):
    free, field = rest[:-1], rest[-1]
    slab, zcap, width = now.shape
    shape = (zcap, width)
    keep = lax.broadcasted_iota(jnp.int32, shape, 0) < extent[0]
    square = plane_square(shape, extent[0])
    weights = [jnp.broadcast_to(rows[:, r : r + 1], shape) for r in range(ROWS)]
    group = min(4, slab)

    def body(i, _):
        planes = []
        for half in range(group):
            at = group * i + half
            kx = own[0] * slab + at
            local = square + x_square(kx, full)
            gain = gain_of(local)
            total = None
            for r in range(ROWS):
                term = weights[r] * force[pl.ds(r * full + kx, 1), :]
                total = term if total is None else total + term
            twice = 2.0 - local * gain
            first = jnp.where(keep, now[at], 0.0)
            value = twice * first - jnp.where(keep, prev[at], 0.0) + gain * total
            current[at] = value
            later = twice * value - first
            onward[at] = later
            planes.append(later)
        for j in range(0, group, 2):
            wide = dot(zstack[...], tall_split(jnp.concatenate(planes[j : j + 2], axis=1)))
            for half in range(2):
                at = pl.multiple_of((group * i + j + half) * zcap, zcap)
                field[pl.ds(at, zcap), :] = wide[:, half * width : (half + 1) * width]
        return 0

    lax.fori_loop(0, slab // group, body, 0)
    block = min(16, slab) * zcap
    for i in range(slab * zcap // block):
        span = slice(i * block, (i + 1) * block)
        field[span, :] = along_y(field[span, :], ystack[...])
    parts = full // slab
    across = xparts[own[0]]
    for i in range(0, zcap, 2):
        pair = [field[pl.ds(i + half, slab, stride=zcap), :] for half in range(2)]
        wide = dot(across, tall_split(jnp.concatenate(pair, axis=1)))
        for k in range(parts):
            for half in range(2):
                free[k][pl.ds(i + half, slab, stride=zcap), :] = wide[
                    k * slab : (k + 1) * slab, half * width : (half + 1) * width
                ]


def last_kernel(own, near, tx, uy, onward, estack, hstack, ystack, xown, *rest, full, parts):
    far, given = rest[:parts], rest[parts : 2 * parts]
    modes, pressure, spare, force, terms, turned = rest[2 * parts :]
    slab, zcap, width = onward.shape
    depth = estack.shape[1] // 3
    used = TERMS * ROWS
    gather_kx(spare, far, own[0])
    force_planes(spare, near, tx, uy, force)
    ax = lax.broadcasted_iota(jnp.int32, (full, width), 0).astype(F32) / full
    ay = lax.broadcasted_iota(jnp.int32, (full, width), 1).astype(F32) / width
    square = BASE * (ax * ax + ay * ay) - BASE
    terms[used * full :, :] = jnp.zeros(((depth - used) * full, width), F32)
    turned[used * slab :, :] = jnp.zeros(((depth - used) * slab, width), F32)
    across = xown[own[0]]
    planes = [plane(force, r) for r in range(ROWS)]
    for n in range(TERMS):
        if n:
            planes = [value * square for value in planes]
        for r in range(0, ROWS, 2):
            at = n * ROWS + r
            for half in range(2):
                terms[(at + half) * full : (at + half + 1) * full, :] = planes[r + half]
            wide = dot(across, tall_split(jnp.concatenate(planes[r : r + 2], axis=1)))
            for half in range(2):
                turned[(at + half) * slab : (at + half + 1) * slab, :] = wide[
                    :, half * width : (half + 1) * width
                ]
    block = ROWS * slab
    for n in range(TERMS):
        span = slice(n * block, (n + 1) * block)
        turned[span, :] = along_y(turned[span, :], ystack[...])
    own_at = own[0] * slab
    for i in range(0, slab, 2):
        pair = [terms[pl.ds(own_at + i + half, depth, stride=full), :] for half in range(2)]
        wide = dot(estack[...], tall_split(jnp.concatenate(pair, axis=1)))
        for half in range(2):
            modes[i + half] = onward[i + half] + wide[:, half * width : (half + 1) * width]
    for i in range(0, slab, 2):
        pair = [turned[pl.ds(i + half, depth, stride=slab), :] for half in range(2)]
        wide = dot(hstack[...], tall_split(jnp.concatenate(pair, axis=1)))
        for half in range(2):
            span = slice((i + half) * zcap, (i + half + 1) * zcap)
            value = wide[:, half * width : (half + 1) * width]
            for piece in given:
                value = value + piece[span, :]
            pressure[span, :] = value


def on_device(modes_now, modes_prev, z_extent, lower_nbr, upper_nbr, x_shift, y_shift):
    slab, zcap, width = modes_now.shape
    parts = lax.axis_size("split")
    count = lax.axis_size("dom")
    full = slab * parts
    own = lax.axis_index("split").astype(jnp.int32)[None]
    group = lax.axis_index("dom").astype(jnp.int32)[None]
    inner = inner_size(count)
    tall = count // inner
    size = ROWS * slab
    big = 4 * slab * zcap * width

    xtable, ytable = static_table(full), static_table(width)
    consts = np.zeros((40, width), np.float32)
    for r in range(ROWS):
        consts[0, r], consts[1, r] = (r, 0) if r < FACE else (ROWS - 1 - r, 1)
    for p, (r, q) in enumerate(PAIRS):
        consts[2:4, p], consts[4:6, p] = consts[0:2, r], consts[0:2, q]
    for n in range(TERMS):
        for j in range(len(SERIES) - n):
            value = SERIES[n + j] * math.comb(n + j, n)
            consts[8 + j, n] = value
            consts[24 + j, n * ROWS : (n + 1) * ROWS] = value
        consts[6:8, n * ROWS : (n + 1) * ROWS] = consts[0:2, :ROWS]
    depth = -(-TERMS * ROWS // 16) * 16
    yhigh, ylow = halves(ytable)
    ystack = np.block([[yhigh, ylow], [yhigh, np.zeros_like(yhigh)]])
    xhigh, xlow = halves(xtable.T)
    xown = np.stack(
        [
            np.concatenate([t[s * slab : (s + 1) * slab] for t in (xhigh, xlow, xhigh)], axis=1)
            for s in range(parts)
        ]
    )
    xparts = np.stack(
        [
            np.concatenate(
                [
                    np.concatenate(
                        [
                            t[(s + k) % parts * slab : ((s + k) % parts + 1) * slab,
                              s * slab : (s + 1) * slab]
                            for k in range(parts)
                        ],
                        axis=0,
                    )
                    for t in (xhigh, xlow, xhigh)
                ],
                axis=1,
            )
            for s in range(parts)
        ]
    )

    def tall_of(table):
        n = table.shape[0]
        tall = np.pad(table.T, ((n, n), (0, 0)))
        return jnp.asarray(np.concatenate([tall, table], axis=0).astype(np.float32))

    consts, ystack, xown, xparts = map(jnp.asarray, (consts, ystack, xown, xparts))
    xtall, ytall = tall_of(xtable), tall_of(ytable)

    def swap(piece):
        got = [piece]
        for k in range(1, parts):
            got.append(lax.ppermute(piece, "split", [(i, (i + k) % parts) for i in range(parts)]))
        return got

    def spread(packet):
        held = [packet]
        for k in range(1, inner):
            to = [(i, i // inner * inner + (i + k) % inner) for i in range(count)]
            held.append(lax.ppermute(packet, "dom", to))
        return call(
            functools.partial(choose_kernel, width=inner),
            [shape_of(size, width)] * tall,
            [SMEM] + [VMEM] * inner,
            moved=8 * size * width * 4,
            name="choose",
        )(group, *held)

    def deliver(chosen):
        got = [chosen[0]]
        for k in range(1, tall):
            to = [(i, (i + k * inner) % count) for i in range(count)]
            got.append(lax.ppermute(chosen[k], "dom", to))
        picked = call(
            functools.partial(pick_kernel, tall=tall, width=inner),
            [shape_of(size, width)],
            [SMEM] * 3 + [VMEM] * tall,
            moved=5 * size * width * 4,
            name="pick",
        )(group, lower_nbr, upper_nbr, *got)[0]
        return swap(picked)

    packet, rows = call(
        strip_kernel,
        [shape_of(size + HEAD, width), shape_of(zcap, width)],
        [SMEM] * 3 + [VMEM] * 2,
        moved=big,
        name="strip",
    )(z_extent, lower_nbr, upper_nbr, modes_now, consts)
    chosen = spread(packet)
    mine = swap(packet[:size])

    ahead, zstack, estack, hstack, coefs = call(
        functools.partial(ahead_kernel, full=full),
        [
            shape_of(size, width),
            shape_of(zcap, 3 * zcap, dtype=BF16),
            shape_of(zcap, 3 * depth, dtype=BF16),
            shape_of(zcap, 3 * depth, dtype=BF16),
            shape_of(16, width),
        ],
        [SMEM] * 2 + [VMEM] * 4,
        flops=10**8,
        moved=2 * big,
        name="ahead",
    )(z_extent, own, modes_now, modes_prev, rows, consts)
    aheads = swap(ahead)

    tx, uy, vx, wy, near1, mixing, _ = call(
        functools.partial(relation_kernel, parts=parts),
        [
            shape_of(2, full, full),
            shape_of(2, width, width),
            shape_of(2, full, full),
            shape_of(2, width, width),
            shape_of(ROWS * full, width),
            shape_of(len(PAIRS), full, width),
            shape_of(ROWS * full, width),
        ],
        [SMEM] * 6 + [ANY] + [VMEM] * (2 + parts),
        flops=10**8,
        moved=2 * big,
        name="relation",
    )(lower_nbr, upper_nbr, x_shift, y_shift, own, coefs, chosen[0], xtall, ytall, *mine)

    packet2, force1, strip2 = call(
        functools.partial(middle_kernel, parts=parts),
        [
            shape_of(size + HEAD, width),
            shape_of(ROWS * full, width),
            shape_of(ROWS * full, width),
        ],
        [SMEM] * 3 + [VMEM] * (4 + 2 * parts),
        scratch=[pltpu.VMEM((ROWS * full, width), F32)],
        flops=10**8,
        moved=2 * big,
        name="middle",
    )(own, lower_nbr, upper_nbr, near1, tx, uy, mixing, *deliver(chosen), *aheads)

    chosen2 = spread(packet2)
    current, onward, *free = call(
        functools.partial(between_kernel, full=full),
        [shape_of(slab, zcap, width)] * 2 + [shape_of(slab * zcap, width)] * parts,
        [SMEM] * 2 + [VMEM] * 7,
        scratch=[pltpu.VMEM((slab * zcap, width), F32)],
        flops=10**9,
        moved=6 * big,
        name="between",
    )(z_extent, own, modes_now, modes_prev, force1, rows, zstack, ystack, xparts)
    given = [free[0]] + [
        lax.ppermute(free[k], "split", [(i, (i + k) % parts) for i in range(parts)])
        for k in range(1, parts)
    ]
    near2 = call(
        near_kernel,
        [shape_of(ROWS * full, width)],
        [VMEM] * 3,
        flops=10**7,
        moved=big,
        name="near",
    )(strip2, vx, wy)[0]

    modes, pressure = call(
        functools.partial(last_kernel, full=full, parts=parts),
        [shape_of(slab, zcap, width), shape_of(slab * zcap, width)],
        [SMEM] + [VMEM] * (8 + 2 * parts),
        scratch=[
            pltpu.VMEM((ROWS * full, width), F32),
            pltpu.VMEM((ROWS * full, width), F32),
            pltpu.VMEM((depth * full, width), F32),
            pltpu.VMEM((depth * slab, width), F32),
        ],
        flops=10**9,
        moved=6 * big,
        name="last",
    )(own, near2, tx, uy, onward, estack, hstack, ystack, xown, *deliver(chosen2), *given)
    return (modes, current, pressure.reshape(slab, zcap, width))


def solution(mesh):
    placed = (
        P("split", "dom", None),
        P("split", "dom", None),
        P("dom"),
        P("dom"),
        P("dom"),
        P("dom", None),
        P("dom", None),
    )
    return jax.shard_map(
        on_device,
        mesh=mesh,
        in_specs=placed,
        out_specs=(P("split", "dom", None), P("split", "dom", None), P("split", "dom", None)),
        check_vma=False,
    )
```

```python
import functools
import math

import jax
import jax.numpy as jnp
import numpy as np
from jax import lax
from jax.experimental import pallas as pl
from jax.experimental.pallas import tpu as pltpu
from jax.sharding import PartitionSpec as P

HIGH = lax.Precision.HIGHEST
F32 = jnp.float32
BF16 = jnp.bfloat16
STENCIL = (-490.0 / 180.0, 270.0 / 180.0, -27.0 / 180.0, 2.0 / 180.0)
COURANT = 0.5
FACE = 3
ROWS = 2 * FACE
HEAD = 8
SERIES = [(-1) ** n * 2.0 / math.factorial(2 * n + 2) for n in range(10)]
TERMS = 7
BASE = (COURANT * math.pi) ** 2
PAIRS = [(r, q) for r in range(ROWS) for q in range(r, ROWS)]
VMEM = pl.BlockSpec(memory_space=pltpu.VMEM)
SMEM = pl.BlockSpec(memory_space=pltpu.SMEM)
ANY = pl.BlockSpec(memory_space=pl.ANY)
HBM = pl.BlockSpec(memory_space=pltpu.HBM)
CHUNK = 8
COVER = 10**10
LIMIT = 12 * 1024 * 1024


def static_table(count):
    kk = np.arange(count)[:, None]
    xx = np.arange(count)[None, :]
    scale = np.where(kk == 0, np.sqrt(1.0 / count), np.sqrt(2.0 / count))
    return scale * np.cos(np.pi * kk * (xx + 0.5) / count)


def halves(table):
    high = table.astype(np.float32).astype(BF16)
    low = (table.astype(np.float32) - high.astype(np.float32)).astype(BF16)
    return high, low


def inner_size(count):
    best = 1
    for n in range(1, count + 1):
        if count % n == 0 and n * n <= count:
            best = n
    return best


def partner(place, step, count):
    if count & (count - 1) == 0:
        return place ^ step
    return (place + step) % count


def giver(place, step, count):
    return partner(place, step if count & (count - 1) == 0 else count - step, count)


def tall_split(data):
    high = data.astype(BF16).astype(F32)
    return jnp.concatenate([high, high, data - high], axis=0).astype(BF16)


def wide_split(data):
    high = data.astype(BF16)
    return jnp.concatenate([high, (data - high.astype(F32)).astype(BF16)], axis=1)


def dot(left, right):
    return jnp.dot(left, right, preferred_element_type=F32)


def exact_dot(left, right):
    return jnp.dot(left, right, precision=HIGH, preferred_element_type=F32)


def exact_dot_t(left, right):
    return lax.dot_general(
        left, right, (((1,), (1,)), ((), ())), precision=HIGH, preferred_element_type=F32
    )


def along_y(data, ystack):
    width = data.shape[1]
    both = dot(wide_split(data), ystack)
    return both[:, :width] + both[:, width:]


def cosine_of(count, odd, lenf):
    prod = count * odd
    turn = 4.0 * lenf
    rest = prod - jnp.floor(prod / turn) * turn
    return jnp.cos(rest * (0.5 * jnp.pi / lenf))


def scale_of(kk, lenf):
    return jnp.where(kk == 0, jnp.sqrt(1.0 / lenf), jnp.sqrt(2.0 / lenf))


def face_rows(near, flip, shape, extent):
    kk = lax.broadcasted_iota(jnp.int32, shape, 0)
    kf = kk.astype(F32)
    lenf = jnp.full(shape, extent.astype(F32))
    table = scale_of(kk, lenf) * cosine_of(kf, 2.0 * near + 1.0, lenf)
    sign = jnp.where((flip > 0) & (kk % 2 == 1), -1.0, 1.0)
    return jnp.where(kk < extent, table * sign, 0.0)


def gain_of(square):
    total = jnp.full_like(square, SERIES[-1])
    for value in reversed(SERIES[:-1]):
        total = total * square + value
    return total


def plane_square(shape, extent):
    kk = lax.broadcasted_iota(jnp.int32, shape, 0)
    kf = kk.astype(F32) / jnp.full(shape, extent.astype(F32))
    kf = jnp.where(kk < extent, kf, 0.0)
    ky = lax.broadcasted_iota(jnp.int32, shape, 1).astype(F32) / shape[1]
    return BASE * (kf * kf + ky * ky)


def x_square(kx, full):
    frac = kx.astype(F32) / full
    return BASE * (frac * frac)


def stencil(face, order):
    rows = []
    for jj in range(FACE):
        total = None
        for mm in range(FACE - jj):
            term = STENCIL[jj + mm + 1] * face[order[mm]]
            total = term if total is None else total + term
        rows.append(total)
    return rows


def through(planes, across, along):
    full, width = planes[0].shape
    out = exact_dot(across, jnp.concatenate(planes, axis=1))
    out = jnp.concatenate([out[:, i * width : (i + 1) * width] for i in range(FACE)], axis=0)
    out = exact_dot_t(out, along)
    return [out[i * full : (i + 1) * full] for i in range(FACE)]


def gather_kx(out, pieces, own):
    count = len(pieces)
    slab = pieces[0].shape[0] // ROWS
    full = slab * count
    for k, piece in enumerate(pieces):
        at = pl.multiple_of(lax.rem(own + count - k, count) * slab, slab)
        for r in range(ROWS):
            out[pl.ds(r * full + at, slab), :] = piece[r * slab : (r + 1) * slab, :]


def plane(ref, r):
    full = ref.shape[0] // ROWS
    return ref[r * full : (r + 1) * full, :]


def call(kernel, out_shape, in_specs, scratch=(), flops=0, moved=0, name=None, limit=LIMIT):
    return pl.pallas_call(
        kernel,
        out_shape=out_shape,
        in_specs=in_specs,
        out_specs=[VMEM] * len(out_shape),
        scratch_shapes=list(scratch),
        compiler_params=pltpu.CompilerParams(vmem_limit_bytes=limit),
        cost_estimate=pl.CostEstimate(flops=flops, bytes_accessed=moved, transcendentals=0),
        name=name,
    )


def shape_of(*dims, dtype=F32):
    return jax.ShapeDtypeStruct(dims, dtype)


def load_chunks(source, held, sems):
    copies = []
    for i in range(held.shape[0] // CHUNK):
        span = pl.ds(i * CHUNK, CHUNK)
        copies.append(pltpu.make_async_copy(source.at[span], held.at[span], sems.at[i]))
        copies[-1].start()
    return copies


def strip_kernel(extent, below, above, now, packet, rows, held, sems):
    slab, zcap, width = now.shape
    copies = load_chunks(now, held, sems)
    at = lax.broadcasted_iota(jnp.int32, (1, width), 1)
    far_face = at >= FACE
    near = jnp.where(far_face, ROWS - 1 - at, at)
    near = jnp.where(at < ROWS, near, 0).astype(F32)
    table = face_rows(near, far_face.astype(F32), (zcap, width), extent[0])
    rows[...] = table
    at = lax.broadcasted_iota(jnp.int32, (HEAD, width), 0)
    names = jnp.where(at < HEAD // 2, above[0], below[0])
    packet[ROWS * slab :, :] = names.astype(F32)
    weights = [jnp.broadcast_to(table[:, r : r + 1], (zcap, width)) for r in range(ROWS)]
    for i, copy in enumerate(copies):
        copy.wait()
        part = held[i * CHUNK : (i + 1) * CHUNK]
        for r in range(ROWS):
            span = slice(r * slab + i * CHUNK, r * slab + (i + 1) * CHUNK)
            packet[span, :] = jnp.sum(part * weights[r][None], axis=1)


def lane_series(consts, first, shape, extent):
    kz = lax.broadcasted_iota(jnp.int32, shape, 0)
    frac = kz.astype(F32) / jnp.full(shape, extent.astype(F32))
    middle = jnp.where(kz < extent, BASE * frac * frac, 0.0) + BASE
    total = jnp.zeros(shape, F32)
    for j in reversed(range(len(SERIES))):
        total = total * middle + consts[first + j : first + j + 1, :]
    return total


def stack_lanes(table, depth):
    table = table[:, :depth]
    high = table.astype(BF16).astype(F32)
    return jnp.concatenate([high, table - high, high], axis=1).astype(BF16)


def ahead_kernel(
    extent, own, now_far, prev_far, rows, consts, strip, zstack, estack, hstack, coefs,
    now, prev, sems, *, full,
):
    slab, zcap, width = now.shape
    ext = extent[0]
    copies = zip(load_chunks(now_far, now, sems.at[0]), load_chunks(prev_far, prev, sems.at[1]))
    kk = lax.broadcasted_iota(jnp.int32, (zcap, zcap), 1)
    zz = lax.broadcasted_iota(jnp.int32, (zcap, zcap), 0)
    lenf = jnp.full((zcap, zcap), ext.astype(F32))
    ztable = scale_of(kk, lenf) * cosine_of(kk.astype(F32), 2.0 * zz.astype(F32) + 1.0, lenf)
    ztable = jnp.where((kk < ext) & (zz < ext), ztable, 0.0)
    zstack[...] = stack_lanes(ztable, zcap)

    shape = (zcap, width)
    pairs = face_rows(consts[2:3, :], consts[3:4, :], shape, ext)
    pairs = pairs * face_rows(consts[4:5, :], consts[5:6, :], shape, ext)
    coefs[...] = exact_dot(lane_series(consts, 8, shape, ext).T[: coefs.shape[0]], pairs)
    terms = face_rows(consts[6:7, :], consts[7:8, :], shape, ext)
    terms = terms * lane_series(consts, 24, shape, ext)
    depth = estack.shape[1] // 3
    estack[...] = stack_lanes(terms, depth)
    hstack[...] = stack_lanes(exact_dot(ztable, terms), depth)

    keep = lax.broadcasted_iota(jnp.int32, shape, 0) < ext
    square = plane_square(shape, ext)
    weights = [jnp.broadcast_to(rows[:, r : r + 1], shape) for r in range(ROWS)]
    for i, pair in enumerate(copies):
        for copy in pair:
            copy.wait()
        for kx in range(i * CHUNK, (i + 1) * CHUNK):
            local = square + x_square(own[0] * slab + kx, full)
            twice = 2.0 - local * gain_of(local)
            ahead = jnp.where(keep, twice * now[kx] - prev[kx], 0.0)
            for r in range(ROWS):
                strip[r * slab + kx : r * slab + kx + 1, :] = jnp.sum(
                    ahead * weights[r], axis=0, keepdims=True
                )


def relation_kernel(
    below, above, x_shift, y_shift, own, coefs, after, xtall, ytall, *rest, parts
):
    strips, (tx, uy, vx, wy, near, mixing, mine) = rest[:parts], rest[parts:]
    full, width = xtall.shape[1], ytall.shape[1]
    for f, (nbr, dx, dy) in enumerate(
        ((below, x_shift[0, 0], y_shift[0, 0]), (above, x_shift[0, 1], y_shift[0, 1]))
    ):
        has = jnp.where(nbr[0] >= 0, COURANT**2, 0.0).astype(F32)
        for count, move, tall, take, keep, scale in (
            (full, dx, xtall, tx, vx, has),
            (width, dy, ytall, uy, wy, None),
        ):
            move = jnp.clip(move, -count, count)
            slid = tall[pl.ds(count + move, count), :]
            at = lax.broadcasted_iota(jnp.int32, (count, count), 0) + move
            kept = jnp.where((at >= 0) & (at < count), tall[count : 2 * count, :], 0.0)
            plain = tall[3 * count :, :]
            taken, stay = exact_dot(plain, slid), exact_dot(plain, kept)
            take[f] = taken if scale is None else taken * scale
            keep[f] = stay if scale is None else stay * scale
    gather_kx(mine, strips, own[0])
    near_planes(mine, vx, wy, near)
    shape = (full, width)
    ax = lax.broadcasted_iota(jnp.int32, shape, 0).astype(F32) / full
    ay = lax.broadcasted_iota(jnp.int32, shape, 1).astype(F32) / width
    square = BASE * (ax * ax + ay * ay) - BASE
    for p in range(len(PAIRS)):
        total = jnp.full(shape, coefs[TERMS - 1, p])
        for n in reversed(range(TERMS - 1)):
            total = total * square + coefs[n, p]
        mixing[p] = total


def near_planes(mine, vx, wy, near):
    full = vx.shape[1]
    low = through(stencil([plane(mine, r) for r in range(FACE)], (0, 1, 2)), vx[0], wy[0])
    upp = through(stencil([plane(mine, FACE + r) for r in range(FACE)], (2, 1, 0)), vx[1], wy[1])
    for r, value in enumerate(low + upp[::-1]):
        near[r * full : (r + 1) * full, :] = value


def force_planes(far, near, tx, uy, force):
    full = tx.shape[1]
    low = through(stencil([plane(far, r) for r in range(FACE)], (2, 1, 0)), tx[0], uy[0])
    upp = through(stencil([plane(far, FACE + r) for r in range(FACE)], (0, 1, 2)), tx[1], uy[1])
    for r, value in enumerate(low + upp[::-1]):
        force[r * full : (r + 1) * full, :] = value - plane(near, r)


def choose_kernel(group, after, *refs, width):
    held, out = refs[:width], refs[width:]
    rows = out[0].shape[0]
    half = rows // 2
    h, l = group[0] // width, lax.rem(group[0], width)
    for k in range(len(out)):
        dest = (partner(h, k, len(out)) * width + l).astype(F32)
        for f in range(2):
            lo, hi = f * half, (f + 1) * half
            row = rows + (0 if f == 1 else HEAD // 2)
            chosen = held[0][lo:hi, :]
            for other in held[1:]:
                chosen = jnp.where(other[row : row + 1, :] == dest, other[lo:hi, :], chosen)
            out[k][lo:hi, :] = chosen


def pick_kernel(group, below, above, *refs, tall, width):
    got, out = refs[:-1], refs[-1]
    half = out.shape[0] // 2
    h = group[0] // width
    for f, nbr in enumerate((below, above)):
        lo = half if f == 0 else 0
        value = got[0][lo : lo + half, :]
        for k in range(1, tall):
            here = jnp.maximum(nbr[0], 0) // width == giver(h, k, tall)
            value = jnp.where(here, got[k][lo : lo + half, :], value)
        out[f * half : (f + 1) * half, :] = value


def middle_kernel(own, below, above, near, tx, uy, mixing, *rest, parts):
    far, ahead = rest[:parts], rest[parts : 2 * parts]
    packet, force, strip, spare = rest[2 * parts :]
    gather_kx(spare, far, own[0])
    force_planes(spare, near, tx, uy, force)
    gather_kx(strip, ahead, own[0])
    full = tx.shape[1]
    slab = full // parts
    for r in range(ROWS):
        total = plane(strip, r)
        for q in range(ROWS):
            total = total + mixing[PAIRS.index((min(r, q), max(r, q)))] * plane(force, q)
        strip[r * full : (r + 1) * full, :] = total
    at = pl.multiple_of(own[0] * slab, slab)
    for r in range(ROWS):
        packet[r * slab : (r + 1) * slab, :] = strip[pl.ds(r * full + at, slab), :]
    at = lax.broadcasted_iota(jnp.int32, (HEAD, packet.shape[1]), 0)
    names = jnp.where(at < HEAD // 2, above[0], below[0])
    packet[ROWS * slab :, :] = names.astype(F32)


def near_kernel(strip, vx, wy, near):
    near_planes(strip, vx, wy, near)


def between_kernel(
    extent, own, now, prev, force, rows, zstack, ystack, xparts, current, onward, *rest, full,
):
    free, field = rest[:-1], rest[-1]
    slab, zcap, width = now.shape
    shape = (zcap, width)
    keep = lax.broadcasted_iota(jnp.int32, shape, 0) < extent[0]
    square = plane_square(shape, extent[0])
    weights = [jnp.broadcast_to(rows[:, r : r + 1], shape) for r in range(ROWS)]
    group = min(4, slab)

    def body(i, _):
        planes = []
        for half in range(group):
            at = group * i + half
            kx = own[0] * slab + at
            local = square + x_square(kx, full)
            gain = gain_of(local)
            total = None
            for r in range(ROWS):
                term = weights[r] * force[pl.ds(r * full + kx, 1), :]
                total = term if total is None else total + term
            twice = 2.0 - local * gain
            first = jnp.where(keep, now[at], 0.0)
            value = twice * first - jnp.where(keep, prev[at], 0.0) + gain * total
            current[at] = value
            later = twice * value - first
            onward[at] = later
            planes.append(later)
        for j in range(0, group, 2):
            wide = dot(zstack[...], tall_split(jnp.concatenate(planes[j : j + 2], axis=1)))
            for half in range(2):
                at = pl.multiple_of((group * i + j + half) * zcap, zcap)
                field[pl.ds(at, zcap), :] = wide[:, half * width : (half + 1) * width]
        return 0

    lax.fori_loop(0, slab // group, body, 0)
    block = min(16, slab) * zcap
    for i in range(slab * zcap // block):
        span = slice(i * block, (i + 1) * block)
        field[span, :] = along_y(field[span, :], ystack[...])
    parts = full // slab
    across = xparts[own[0]]
    for i in range(0, zcap, 2):
        pair = [field[pl.ds(i + half, slab, stride=zcap), :] for half in range(2)]
        wide = dot(across, tall_split(jnp.concatenate(pair, axis=1)))
        for k in range(parts):
            for half in range(2):
                free[k][pl.ds(i + half, slab, stride=zcap), :] = wide[
                    k * slab : (k + 1) * slab, half * width : (half + 1) * width
                ]


def last_kernel(own, near, tx, uy, onward, estack, hstack, ystack, xown, *rest, full, parts):
    far, given = rest[:parts], rest[parts : 2 * parts]
    modes, pressure, spare, force, terms, turned = rest[2 * parts :]
    slab, zcap, width = onward.shape
    depth = estack.shape[1] // 3
    used = TERMS * ROWS
    gather_kx(spare, far, own[0])
    force_planes(spare, near, tx, uy, force)
    ax = lax.broadcasted_iota(jnp.int32, (full, width), 0).astype(F32) / full
    ay = lax.broadcasted_iota(jnp.int32, (full, width), 1).astype(F32) / width
    square = BASE * (ax * ax + ay * ay) - BASE
    terms[used * full :, :] = jnp.zeros(((depth - used) * full, width), F32)
    turned[used * slab :, :] = jnp.zeros(((depth - used) * slab, width), F32)
    across = xown[own[0]]
    planes = [plane(force, r) for r in range(ROWS)]
    for n in range(TERMS):
        if n:
            planes = [value * square for value in planes]
        for r in range(0, ROWS, 2):
            at = n * ROWS + r
            for half in range(2):
                terms[(at + half) * full : (at + half + 1) * full, :] = planes[r + half]
            wide = dot(across, tall_split(jnp.concatenate(planes[r : r + 2], axis=1)))
            for half in range(2):
                turned[(at + half) * slab : (at + half + 1) * slab, :] = wide[
                    :, half * width : (half + 1) * width
                ]
    block = ROWS * slab
    for n in range(TERMS):
        span = slice(n * block, (n + 1) * block)
        turned[span, :] = along_y(turned[span, :], ystack[...])
    own_at = own[0] * slab
    for i in range(0, slab, 2):
        pair = [terms[pl.ds(own_at + i + half, depth, stride=full), :] for half in range(2)]
        wide = dot(estack[...], tall_split(jnp.concatenate(pair, axis=1)))
        for half in range(2):
            modes[i + half] = onward[i + half] + wide[:, half * width : (half + 1) * width]
    for i in range(0, slab, 2):
        pair = [turned[pl.ds(i + half, depth, stride=slab), :] for half in range(2)]
        wide = dot(hstack[...], tall_split(jnp.concatenate(pair, axis=1)))
        for half in range(2):
            span = slice((i + half) * zcap, (i + half + 1) * zcap)
            value = wide[:, half * width : (half + 1) * width]
            for piece in given:
                value = value + piece[span, :]
            pressure[span, :] = value


def on_device(modes_now, modes_prev, z_extent, lower_nbr, upper_nbr, x_shift, y_shift):
    slab, zcap, width = modes_now.shape
    parts = lax.axis_size("split")
    count = lax.axis_size("dom")
    full = slab * parts
    own = lax.axis_index("split").astype(jnp.int32)[None]
    group = lax.axis_index("dom").astype(jnp.int32)[None]
    inner = inner_size(count)
    tall = count // inner
    size = ROWS * slab
    big = 4 * slab * zcap * width

    xtable, ytable = static_table(full), static_table(width)
    consts = np.zeros((40, width), np.float32)
    for r in range(ROWS):
        consts[0, r], consts[1, r] = (r, 0) if r < FACE else (ROWS - 1 - r, 1)
    for p, (r, q) in enumerate(PAIRS):
        consts[2:4, p], consts[4:6, p] = consts[0:2, r], consts[0:2, q]
    for n in range(TERMS):
        for j in range(len(SERIES) - n):
            value = SERIES[n + j] * math.comb(n + j, n)
            consts[8 + j, n] = value
            consts[24 + j, n * ROWS : (n + 1) * ROWS] = value
        consts[6:8, n * ROWS : (n + 1) * ROWS] = consts[0:2, :ROWS]
    depth = -(-TERMS * ROWS // 16) * 16
    yhigh, ylow = halves(ytable)
    ystack = np.block([[yhigh, ylow], [yhigh, np.zeros_like(yhigh)]])
    xhigh, xlow = halves(xtable.T)
    xown = np.stack(
        [
            np.concatenate([t[s * slab : (s + 1) * slab] for t in (xhigh, xlow, xhigh)], axis=1)
            for s in range(parts)
        ]
    )
    xparts = np.stack(
        [
            np.concatenate(
                [
                    np.concatenate(
                        [
                            t[(s + k) % parts * slab : ((s + k) % parts + 1) * slab,
                              s * slab : (s + 1) * slab]
                            for k in range(parts)
                        ],
                        axis=0,
                    )
                    for t in (xhigh, xlow, xhigh)
                ],
                axis=1,
            )
            for s in range(parts)
        ]
    )

    def tall_of(table):
        n = table.shape[0]
        tall = np.pad(table.T, ((n, n), (0, 0)))
        return jnp.asarray(np.concatenate([tall, table], axis=0).astype(np.float32))

    consts, ystack, xown, xparts = map(jnp.asarray, (consts, ystack, xown, xparts))
    xtall, ytall = tall_of(xtable), tall_of(ytable)

    def swap(piece):
        got = [piece]
        for k in range(1, parts):
            got.append(lax.ppermute(piece, "split", [(i, (i + k) % parts) for i in range(parts)]))
        return got

    def spread(packet):
        held = [packet]
        for k in range(1, inner):
            to = [(i, i // inner * inner + partner(i % inner, k, inner)) for i in range(count)]
            held.append(lax.ppermute(packet, "dom", to))
        return held

    def choose(held, after):
        return call(
            functools.partial(choose_kernel, width=inner),
            [shape_of(size, width)] * tall,
            [SMEM, ANY] + [VMEM] * inner,
            flops=COVER,
            moved=8 * size * width * 4,
            name="choose",
        )(group, after, *held)

    def deliver(chosen):
        got = [chosen[0]]
        for k in range(1, tall):
            to = [(i, partner(i // inner, k, tall) * inner + i % inner) for i in range(count)]
            got.append(lax.ppermute(chosen[k], "dom", to))
        picked = call(
            functools.partial(pick_kernel, tall=tall, width=inner),
            [shape_of(size, width)],
            [SMEM] * 3 + [VMEM] * tall,
            moved=5 * size * width * 4,
            name="pick",
        )(group, lower_nbr, upper_nbr, *got)[0]
        return swap(picked)

    packet, rows = call(
        strip_kernel,
        [shape_of(size + HEAD, width), shape_of(zcap, width)],
        [SMEM] * 3 + [HBM],
        scratch=[
            pltpu.VMEM((slab, zcap, width), F32),
            pltpu.SemaphoreType.DMA((slab // CHUNK,)),
        ],
        moved=big,
        name="strip",
        limit=63 * 1024 * 1024,
    )(z_extent, lower_nbr, upper_nbr, modes_now)
    held = spread(packet)

    ahead, zstack, estack, hstack, coefs = call(
        functools.partial(ahead_kernel, full=full),
        [
            shape_of(size, width),
            shape_of(zcap, 3 * zcap, dtype=BF16),
            shape_of(zcap, 3 * depth, dtype=BF16),
            shape_of(zcap, 3 * depth, dtype=BF16),
            shape_of(16, width),
        ],
        [SMEM] * 2 + [HBM] * 2 + [VMEM] * 2,
        scratch=[
            pltpu.VMEM((slab, zcap, width), F32),
            pltpu.VMEM((slab, zcap, width), F32),
            pltpu.SemaphoreType.DMA((2, slab // CHUNK)),
        ],
        flops=10**8,
        moved=2 * big,
        name="ahead",
    )(z_extent, own, modes_now, modes_prev, rows, consts)
    chosen = choose(held, ahead)
    mine = swap(packet[:size])
    aheads = swap(ahead)

    tx, uy, vx, wy, near1, mixing, _ = call(
        functools.partial(relation_kernel, parts=parts),
        [
            shape_of(2, full, full),
            shape_of(2, width, width),
            shape_of(2, full, full),
            shape_of(2, width, width),
            shape_of(ROWS * full, width),
            shape_of(len(PAIRS), full, width),
            shape_of(ROWS * full, width),
        ],
        [SMEM] * 6 + [ANY] + [VMEM] * (2 + parts),
        flops=10**8,
        moved=2 * big,
        name="relation",
    )(lower_nbr, upper_nbr, x_shift, y_shift, own, coefs, chosen[0], xtall, ytall, *mine)

    packet2, force1, strip2 = call(
        functools.partial(middle_kernel, parts=parts),
        [
            shape_of(size + HEAD, width),
            shape_of(ROWS * full, width),
            shape_of(ROWS * full, width),
        ],
        [SMEM] * 3 + [VMEM] * (4 + 2 * parts),
        scratch=[pltpu.VMEM((ROWS * full, width), F32)],
        flops=10**8,
        moved=2 * big,
        name="middle",
    )(own, lower_nbr, upper_nbr, near1, tx, uy, mixing, *deliver(chosen), *aheads)

    chosen2 = choose(spread(packet2), packet2)
    current, onward, *free = call(
        functools.partial(between_kernel, full=full),
        [shape_of(slab, zcap, width)] * 2 + [shape_of(slab * zcap, width)] * parts,
        [SMEM] * 2 + [VMEM] * 7,
        scratch=[pltpu.VMEM((slab * zcap, width), F32)],
        flops=10**9,
        moved=6 * big,
        name="between",
    )(z_extent, own, modes_now, modes_prev, force1, rows, zstack, ystack, xparts)
    given = [free[0]] + [
        lax.ppermute(free[k], "split", [(i, (i + k) % parts) for i in range(parts)])
        for k in range(1, parts)
    ]
    near2 = call(
        near_kernel,
        [shape_of(ROWS * full, width)],
        [VMEM] * 3,
        flops=10**7,
        moved=big,
        name="near",
    )(strip2, vx, wy)[0]

    modes, pressure = call(
        functools.partial(last_kernel, full=full, parts=parts),
        [shape_of(slab, zcap, width), shape_of(slab * zcap, width)],
        [SMEM] + [VMEM] * (8 + 2 * parts),
        scratch=[
            pltpu.VMEM((ROWS * full, width), F32),
            pltpu.VMEM((ROWS * full, width), F32),
            pltpu.VMEM((depth * full, width), F32),
            pltpu.VMEM((depth * slab, width), F32),
        ],
        flops=10**9,
        moved=6 * big,
        name="last",
    )(own, near2, tx, uy, onward, estack, hstack, ystack, xown, *deliver(chosen2), *given)
    return (modes, current, pressure.reshape(slab, zcap, width))


def solution(mesh):
    placed = (
        P("split", "dom", None),
        P("split", "dom", None),
        P("dom"),
        P("dom"),
        P("dom"),
        P("dom", None),
        P("dom", None),
    )
    return jax.shard_map(
        on_device,
        mesh=mesh,
        in_specs=placed,
        out_specs=(P("split", "dom", None), P("split", "dom", None), P("split", "dom", None)),
        check_vma=False,
    )
```

```python
import functools
import math

import jax
import jax.numpy as jnp
import numpy as np
from jax import lax
from jax.experimental import pallas as pl
from jax.experimental.pallas import tpu as pltpu
from jax.sharding import PartitionSpec as P

HIGH = lax.Precision.HIGHEST
F32 = jnp.float32
BF16 = jnp.bfloat16
STENCIL = (-490.0 / 180.0, 270.0 / 180.0, -27.0 / 180.0, 2.0 / 180.0)
COURANT = 0.5
FACE = 3
ROWS = 2 * FACE
HEAD = 8
SERIES = [(-1) ** n * 2.0 / math.factorial(2 * n + 2) for n in range(10)]
TERMS = 6
DOUBLE = [(-1) ** (n + 1) * (4 - 2.0 * 4.0 ** (n + 1)) / math.factorial(2 * n + 2) for n in range(14)]
DOUBLE_TERMS = 9
WIDE = 63 * 1024 * 1024
BASE = (COURANT * math.pi) ** 2
PAIRS = [(r, q) for r in range(ROWS) for q in range(r, ROWS)]
VMEM = pl.BlockSpec(memory_space=pltpu.VMEM)
SMEM = pl.BlockSpec(memory_space=pltpu.SMEM)
ANY = pl.BlockSpec(memory_space=pl.ANY)
HBM = pl.BlockSpec(memory_space=pltpu.HBM)
CHUNK = 8
COVER = 10**10
LIMIT = 12 * 1024 * 1024


def static_table(count):
    kk = np.arange(count)[:, None]
    xx = np.arange(count)[None, :]
    scale = np.where(kk == 0, np.sqrt(1.0 / count), np.sqrt(2.0 / count))
    return scale * np.cos(np.pi * kk * (xx + 0.5) / count)


def halves(table):
    high = table.astype(np.float32).astype(BF16)
    low = (table.astype(np.float32) - high.astype(np.float32)).astype(BF16)
    return high, low


def inner_size(count):
    best = 1
    for n in range(1, count + 1):
        if count % n == 0 and n * n <= count:
            best = n
    return best


def partner(place, step, count):
    if count & (count - 1) == 0:
        return place ^ step
    return (place + step) % count


def giver(place, step, count):
    return partner(place, step if count & (count - 1) == 0 else count - step, count)


def tall_split(data):
    high = data.astype(BF16).astype(F32)
    return jnp.concatenate([high, high, data - high], axis=0).astype(BF16)


def wide_split(data):
    high = data.astype(BF16)
    return jnp.concatenate([high, (data - high.astype(F32)).astype(BF16)], axis=1)


def dot(left, right):
    return jnp.dot(left, right, preferred_element_type=F32)


def exact_dot(left, right):
    return jnp.dot(left, right, precision=HIGH, preferred_element_type=F32)


def exact_dot_t(left, right):
    return lax.dot_general(
        left, right, (((1,), (1,)), ((), ())), precision=HIGH, preferred_element_type=F32
    )


def along_y(data, ystack):
    width = data.shape[1]
    both = dot(wide_split(data), ystack)
    return both[:, :width] + both[:, width:]


def cosine_of(count, odd, lenf):
    prod = count * odd
    turn = 4.0 * lenf
    rest = prod - jnp.floor(prod / turn) * turn
    return jnp.cos(rest * (0.5 * jnp.pi / lenf))


def scale_of(kk, lenf):
    return jnp.where(kk == 0, jnp.sqrt(1.0 / lenf), jnp.sqrt(2.0 / lenf))


def face_rows(near, flip, shape, extent):
    kk = lax.broadcasted_iota(jnp.int32, shape, 0)
    kf = kk.astype(F32)
    lenf = jnp.full(shape, extent.astype(F32))
    table = scale_of(kk, lenf) * cosine_of(kf, 2.0 * near + 1.0, lenf)
    sign = jnp.where((flip > 0) & (kk % 2 == 1), -1.0, 1.0)
    return jnp.where(kk < extent, table * sign, 0.0)


def gain_of(square):
    total = jnp.full_like(square, SERIES[-1])
    for value in reversed(SERIES[:-1]):
        total = total * square + value
    return total


def plane_square(shape, extent):
    kk = lax.broadcasted_iota(jnp.int32, shape, 0)
    kf = kk.astype(F32) / jnp.full(shape, extent.astype(F32))
    kf = jnp.where(kk < extent, kf, 0.0)
    ky = lax.broadcasted_iota(jnp.int32, shape, 1).astype(F32) / shape[1]
    return BASE * (kf * kf + ky * ky)


def x_square(kx, full):
    frac = kx.astype(F32) / full
    return BASE * (frac * frac)


def stencil(face, order):
    rows = []
    for jj in range(FACE):
        total = None
        for mm in range(FACE - jj):
            term = STENCIL[jj + mm + 1] * face[order[mm]]
            total = term if total is None else total + term
        rows.append(total)
    return rows


def through(planes, across, along):
    full, width = planes[0].shape
    out = exact_dot(across, jnp.concatenate(planes, axis=1))
    out = jnp.concatenate([out[:, i * width : (i + 1) * width] for i in range(FACE)], axis=0)
    out = exact_dot_t(out, along)
    return [out[i * full : (i + 1) * full] for i in range(FACE)]


def gather_kx(out, pieces, own):
    count = len(pieces)
    slab = pieces[0].shape[0] // ROWS
    full = slab * count
    for k, piece in enumerate(pieces):
        at = pl.multiple_of(lax.rem(own + count - k, count) * slab, slab)
        for r in range(ROWS):
            out[pl.ds(r * full + at, slab), :] = piece[r * slab : (r + 1) * slab, :]


def plane(ref, r):
    full = ref.shape[0] // ROWS
    return ref[r * full : (r + 1) * full, :]


def call(kernel, out_shape, in_specs, scratch=(), flops=0, moved=0, name=None, limit=LIMIT):
    return pl.pallas_call(
        kernel,
        out_shape=out_shape,
        in_specs=in_specs,
        out_specs=[VMEM] * len(out_shape),
        scratch_shapes=list(scratch),
        compiler_params=pltpu.CompilerParams(vmem_limit_bytes=limit),
        cost_estimate=pl.CostEstimate(flops=flops, bytes_accessed=moved, transcendentals=0),
        name=name,
    )


def shape_of(*dims, dtype=F32):
    return jax.ShapeDtypeStruct(dims, dtype)


def load_chunks(source, held, sems):
    copies = []
    for i in range(held.shape[0] // CHUNK):
        span = pl.ds(i * CHUNK, CHUNK)
        copies.append(pltpu.make_async_copy(source.at[span], held.at[span], sems.at[i]))
        copies[-1].start()
    return copies


def strip_kernel(extent, below, above, now, packet, rows, held, sems):
    slab, zcap, width = now.shape
    copies = load_chunks(now, held, sems)
    at = lax.broadcasted_iota(jnp.int32, (1, width), 1)
    far_face = at >= FACE
    near = jnp.where(far_face, ROWS - 1 - at, at)
    near = jnp.where(at < ROWS, near, 0).astype(F32)
    table = face_rows(near, far_face.astype(F32), (zcap, width), extent[0])
    rows[...] = table
    at = lax.broadcasted_iota(jnp.int32, (HEAD, width), 0)
    names = jnp.where(at < HEAD // 2, above[0], below[0])
    packet[ROWS * slab :, :] = names.astype(F32)
    weights = [jnp.broadcast_to(table[:, r : r + 1], (zcap, width)) for r in range(ROWS)]
    for i, copy in enumerate(copies):
        copy.wait()
        part = held[i * CHUNK : (i + 1) * CHUNK]
        for r in range(ROWS):
            span = slice(r * slab + i * CHUNK, r * slab + (i + 1) * CHUNK)
            packet[span, :] = jnp.sum(part * weights[r][None], axis=1)


def lane_series(consts, first, count, shape, extent):
    kz = lax.broadcasted_iota(jnp.int32, shape, 0)
    frac = kz.astype(F32) / jnp.full(shape, extent.astype(F32))
    middle = jnp.where(kz < extent, BASE * frac * frac, 0.0) + BASE
    total = jnp.zeros(shape, F32)
    for j in reversed(range(count)):
        total = total * middle + consts[first + j : first + j + 1, :]
    return total


def stack_lanes(table, depth):
    table = table[:, :depth]
    high = table.astype(BF16).astype(F32)
    return jnp.concatenate([high, table - high, high], axis=1).astype(BF16)


def ahead_kernel(
    extent, own, now_far, prev_far, rows, consts, strip, coefs, now, prev, sems, *, full
):
    slab, zcap, width = now.shape
    ext = extent[0]
    copies = zip(load_chunks(now_far, now, sems.at[0]), load_chunks(prev_far, prev, sems.at[1]))

    shape = (zcap, width)
    pairs = face_rows(consts[2:3, :], consts[3:4, :], shape, ext)
    pairs = pairs * face_rows(consts[4:5, :], consts[5:6, :], shape, ext)
    series = lane_series(consts, 8, len(SERIES), shape, ext)
    coefs[...] = exact_dot(series.T[: coefs.shape[0]], pairs)

    keep = lax.broadcasted_iota(jnp.int32, shape, 0) < ext
    square = plane_square(shape, ext)
    weights = [jnp.broadcast_to(rows[:, r : r + 1], shape) for r in range(ROWS)]
    for i, pair in enumerate(copies):
        for copy in pair:
            copy.wait()
        for kx in range(i * CHUNK, (i + 1) * CHUNK):
            local = square + x_square(own[0] * slab + kx, full)
            twice = 2.0 - local * gain_of(local)
            ahead = jnp.where(keep, twice * now[kx] - prev[kx], 0.0)
            for r in range(ROWS):
                strip[r * slab + kx : r * slab + kx + 1, :] = jnp.sum(
                    ahead * weights[r], axis=0, keepdims=True
                )


def relation_kernel(
    below, above, x_shift, y_shift, own, coefs, after, xtall, ytall, *rest, parts
):
    strips, (tx, uy, vx, wy, near, mixing, mine) = rest[:parts], rest[parts:]
    full, width = xtall.shape[1], ytall.shape[1]
    for f, (nbr, dx, dy) in enumerate(
        ((below, x_shift[0, 0], y_shift[0, 0]), (above, x_shift[0, 1], y_shift[0, 1]))
    ):
        has = jnp.where(nbr[0] >= 0, COURANT**2, 0.0).astype(F32)
        for count, move, tall, take, keep, scale in (
            (full, dx, xtall, tx, vx, has),
            (width, dy, ytall, uy, wy, None),
        ):
            move = jnp.clip(move, -count, count)
            slid = tall[pl.ds(count + move, count), :]
            at = lax.broadcasted_iota(jnp.int32, (count, count), 0) + move
            kept = jnp.where((at >= 0) & (at < count), tall[count : 2 * count, :], 0.0)
            plain = tall[3 * count :, :]
            taken, stay = exact_dot(plain, slid), exact_dot(plain, kept)
            take[f] = taken if scale is None else taken * scale
            keep[f] = stay if scale is None else stay * scale
    gather_kx(mine, strips, own[0])
    near_planes(mine, vx, wy, near)
    shape = (full, width)
    ax = lax.broadcasted_iota(jnp.int32, shape, 0).astype(F32) / full
    ay = lax.broadcasted_iota(jnp.int32, shape, 1).astype(F32) / width
    square = BASE * (ax * ax + ay * ay) - BASE
    for p in range(len(PAIRS)):
        total = jnp.full(shape, coefs[TERMS - 1, p])
        for n in reversed(range(TERMS - 1)):
            total = total * square + coefs[n, p]
        mixing[p] = total


def near_planes(mine, vx, wy, near):
    full = vx.shape[1]
    low = through(stencil([plane(mine, r) for r in range(FACE)], (0, 1, 2)), vx[0], wy[0])
    upp = through(stencil([plane(mine, FACE + r) for r in range(FACE)], (2, 1, 0)), vx[1], wy[1])
    for r, value in enumerate(low + upp[::-1]):
        near[r * full : (r + 1) * full, :] = value


def force_planes(far, near, tx, uy, force):
    full = tx.shape[1]
    low = through(stencil([plane(far, r) for r in range(FACE)], (2, 1, 0)), tx[0], uy[0])
    upp = through(stencil([plane(far, FACE + r) for r in range(FACE)], (0, 1, 2)), tx[1], uy[1])
    for r, value in enumerate(low + upp[::-1]):
        force[r * full : (r + 1) * full, :] = value - plane(near, r)


def choose_kernel(group, after, *refs, width):
    held, out = refs[:width], refs[width:]
    rows = out[0].shape[0]
    half = rows // 2
    h, l = group[0] // width, lax.rem(group[0], width)
    for k in range(len(out)):
        dest = (partner(h, k, len(out)) * width + l).astype(F32)
        for f in range(2):
            lo, hi = f * half, (f + 1) * half
            row = rows + (0 if f == 1 else HEAD // 2)
            chosen = held[0][lo:hi, :]
            for other in held[1:]:
                chosen = jnp.where(other[row : row + 1, :] == dest, other[lo:hi, :], chosen)
            out[k][lo:hi, :] = chosen


def pick_kernel(group, below, above, after, *refs, tall, width):
    got, out = refs[:-1], refs[-1]
    half = out.shape[0] // 2
    h = group[0] // width
    for f, nbr in enumerate((below, above)):
        lo = half if f == 0 else 0
        value = got[0][lo : lo + half, :]
        for k in range(1, tall):
            here = jnp.maximum(nbr[0], 0) // width == giver(h, k, tall)
            value = jnp.where(here, got[k][lo : lo + half, :], value)
        out[f * half : (f + 1) * half, :] = value


def middle_kernel(own, below, above, after, near, tx, uy, mixing, *rest, parts):
    far, ahead = rest[:parts], rest[parts : 2 * parts]
    packet, force, strip, spare = rest[2 * parts :]
    gather_kx(spare, far, own[0])
    force_planes(spare, near, tx, uy, force)
    gather_kx(strip, ahead, own[0])
    full = tx.shape[1]
    slab = full // parts
    for r in range(ROWS):
        total = plane(strip, r)
        for q in range(ROWS):
            total = total + mixing[PAIRS.index((min(r, q), max(r, q)))] * plane(force, q)
        strip[r * full : (r + 1) * full, :] = total
    at = pl.multiple_of(own[0] * slab, slab)
    for r in range(ROWS):
        packet[r * slab : (r + 1) * slab, :] = strip[pl.ds(r * full + at, slab), :]
    at = lax.broadcasted_iota(jnp.int32, (HEAD, packet.shape[1]), 0)
    names = jnp.where(at < HEAD // 2, above[0], below[0])
    packet[ROWS * slab :, :] = names.astype(F32)


def near_kernel(strip, vx, wy, near):
    near_planes(strip, vx, wy, near)


def unforced_kernel(
    extent, own, after, now, prev, consts, ystack, xparts, estack, hstack, gstack, *rest, full
):
    free, field = rest[:-1], rest[-1]
    slab, zcap, width = now.shape
    shape = (zcap, width)
    ext = extent[0]
    kk = lax.broadcasted_iota(jnp.int32, (zcap, zcap), 1)
    zz = lax.broadcasted_iota(jnp.int32, (zcap, zcap), 0)
    lenf = jnp.full((zcap, zcap), ext.astype(F32))
    ztable = scale_of(kk, lenf) * cosine_of(kk.astype(F32), 2.0 * zz.astype(F32) + 1.0, lenf)
    ztable = jnp.where((kk < ext) & (zz < ext), ztable, 0.0)
    zstack = stack_lanes(ztable, zcap)
    face = face_rows(consts[6:7, :], consts[7:8, :], shape, ext)
    terms = face * lane_series(consts, 24, len(SERIES), shape, ext)
    depth = estack.shape[1] // 3
    estack[...] = stack_lanes(terms, depth)
    hstack[...] = stack_lanes(exact_dot(ztable, terms), depth)
    terms = face * lane_series(consts, 40, len(DOUBLE), shape, ext)
    gstack[...] = stack_lanes(exact_dot(ztable, terms), gstack.shape[1] // 3)

    keep = lax.broadcasted_iota(jnp.int32, shape, 0) < ext
    square = plane_square(shape, ext)
    group = min(4, slab)

    def body(i, _):
        planes = []
        for half in range(group):
            at = group * i + half
            local = square + x_square(own[0] * slab + at, full)
            twice = 2.0 - local * gain_of(local)
            first = now[at]
            later = twice * (twice * first - prev[at]) - first
            planes.append(jnp.where(keep, later, 0.0))
        for j in range(0, group, 2):
            wide = dot(zstack, tall_split(jnp.concatenate(planes[j : j + 2], axis=1)))
            for half in range(2):
                at = pl.multiple_of((group * i + j + half) * zcap, zcap)
                field[pl.ds(at, zcap), :] = wide[:, half * width : (half + 1) * width]
        return 0

    lax.fori_loop(0, slab // group, body, 0)
    block = min(16, slab) * zcap
    for i in range(slab * zcap // block):
        span = slice(i * block, (i + 1) * block)
        field[span, :] = along_y(field[span, :], ystack[...])
    parts = full // slab
    across = xparts[own[0]]
    for i in range(0, zcap, 2):
        pair = [field[pl.ds(i + half, slab, stride=zcap), :] for half in range(2)]
        wide = dot(across, tall_split(jnp.concatenate(pair, axis=1)))
        for k in range(parts):
            for half in range(2):
                free[k][pl.ds(i + half, slab, stride=zcap), :] = wide[
                    k * slab : (k + 1) * slab, half * width : (half + 1) * width
                ]


def between_kernel(extent, own, now, prev, force, rows, current, onward, *, full):
    slab, zcap, width = now.shape
    shape = (zcap, width)
    keep = lax.broadcasted_iota(jnp.int32, shape, 0) < extent[0]
    square = plane_square(shape, extent[0])
    weights = [jnp.broadcast_to(rows[:, r : r + 1], shape) for r in range(ROWS)]
    group = min(4, slab)

    def body(i, _):
        for half in range(group):
            at = group * i + half
            kx = own[0] * slab + at
            local = square + x_square(kx, full)
            gain = gain_of(local)
            total = None
            for r in range(ROWS):
                term = weights[r] * force[pl.ds(r * full + kx, 1), :]
                total = term if total is None else total + term
            twice = 2.0 - local * gain
            first = jnp.where(keep, now[at], 0.0)
            value = twice * first - jnp.where(keep, prev[at], 0.0) + gain * total
            current[at] = value
            onward[at] = twice * value - first
        return 0

    lax.fori_loop(0, slab // group, body, 0)


def lift(force, across, table, ystack, given, terms, turned, pressure, count):
    zcap = table.shape[0]
    depth = table.shape[1] // 3
    used = count * ROWS
    full, width = force.shape[0] // ROWS, force.shape[1]
    slab = across.shape[0]
    ax = lax.broadcasted_iota(jnp.int32, (full, width), 0).astype(F32) / full
    ay = lax.broadcasted_iota(jnp.int32, (full, width), 1).astype(F32) / width
    square = BASE * (ax * ax + ay * ay) - BASE
    if terms is not None:
        terms[used * full :, :] = jnp.zeros(((depth - used) * full, width), F32)
    turned[used * slab :, :] = jnp.zeros(((depth - used) * slab, width), F32)
    planes = [plane(force, r) for r in range(ROWS)]
    for n in range(count):
        if n:
            planes = [value * square for value in planes]
        for r in range(0, ROWS, 2):
            at = n * ROWS + r
            if terms is not None:
                for half in range(2):
                    terms[(at + half) * full : (at + half + 1) * full, :] = planes[r + half]
            wide = dot(across, tall_split(jnp.concatenate(planes[r : r + 2], axis=1)))
            for half in range(2):
                turned[(at + half) * slab : (at + half + 1) * slab, :] = wide[
                    :, half * width : (half + 1) * width
                ]
    block = ROWS * slab
    for n in range(count):
        span = slice(n * block, (n + 1) * block)
        turned[span, :] = along_y(turned[span, :], ystack[...])
    for i in range(0, slab, 2):
        pair = [turned[pl.ds(i + half, depth, stride=slab), :] for half in range(2)]
        wide = dot(table[...], tall_split(jnp.concatenate(pair, axis=1)))
        for half in range(2):
            span = slice((i + half) * zcap, (i + half + 1) * zcap)
            value = wide[:, half * width : (half + 1) * width]
            for piece in given:
                value = value + piece[span, :]
            pressure[span, :] = value


def first_kernel(own, force, gstack, ystack, xown, free, summed, turned):
    lift(force, xown[own[0]], gstack, ystack, [free], None, turned, summed, DOUBLE_TERMS)


def last_kernel(own, near, tx, uy, onward, estack, hstack, ystack, xown, *rest, full, parts):
    far, given = rest[:parts], rest[parts : 2 * parts]
    modes, pressure, spare, force, terms, turned = rest[2 * parts :]
    slab, zcap, width = onward.shape
    depth = estack.shape[1] // 3
    gather_kx(spare, far, own[0])
    force_planes(spare, near, tx, uy, force)
    lift(force, xown[own[0]], hstack, ystack, given, terms, turned, pressure, TERMS)
    own_at = own[0] * slab
    for i in range(0, slab, 2):
        pair = [terms[pl.ds(own_at + i + half, depth, stride=full), :] for half in range(2)]
        wide = dot(estack[...], tall_split(jnp.concatenate(pair, axis=1)))
        for half in range(2):
            modes[i + half] = onward[i + half] + wide[:, half * width : (half + 1) * width]


def on_device(modes_now, modes_prev, z_extent, lower_nbr, upper_nbr, x_shift, y_shift):
    slab, zcap, width = modes_now.shape
    parts = lax.axis_size("split")
    count = lax.axis_size("dom")
    full = slab * parts
    own = lax.axis_index("split").astype(jnp.int32)[None]
    group = lax.axis_index("dom").astype(jnp.int32)[None]
    inner = inner_size(count)
    tall = count // inner
    size = ROWS * slab
    big = 4 * slab * zcap * width

    xtable, ytable = static_table(full), static_table(width)
    consts = np.zeros((56, width), np.float32)
    for r in range(ROWS):
        consts[0, r], consts[1, r] = (r, 0) if r < FACE else (ROWS - 1 - r, 1)
    for p, (r, q) in enumerate(PAIRS):
        consts[2:4, p], consts[4:6, p] = consts[0:2, r], consts[0:2, q]
    for n in range(DOUBLE_TERMS):
        lanes = slice(n * ROWS, (n + 1) * ROWS)
        consts[6:8, lanes] = consts[0:2, :ROWS]
        for j in range(len(SERIES) - n if n < TERMS else 0):
            consts[8 + j, n] = consts[24 + j, lanes] = SERIES[n + j] * math.comb(n + j, n)
        for j in range(len(DOUBLE) - n):
            consts[40 + j, lanes] = DOUBLE[n + j] * math.comb(n + j, n)
    depth = -(-TERMS * ROWS // 16) * 16
    double_depth = -(-DOUBLE_TERMS * ROWS // 16) * 16
    yhigh, ylow = halves(ytable)
    ystack = np.block([[yhigh, ylow], [yhigh, np.zeros_like(yhigh)]])
    xhigh, xlow = halves(xtable.T)
    xown = np.stack(
        [
            np.concatenate([t[s * slab : (s + 1) * slab] for t in (xhigh, xlow, xhigh)], axis=1)
            for s in range(parts)
        ]
    )
    xparts = np.stack(
        [
            np.concatenate(
                [
                    np.concatenate(
                        [
                            t[(s + k) % parts * slab : ((s + k) % parts + 1) * slab,
                              s * slab : (s + 1) * slab]
                            for k in range(parts)
                        ],
                        axis=0,
                    )
                    for t in (xhigh, xlow, xhigh)
                ],
                axis=1,
            )
            for s in range(parts)
        ]
    )

    def tall_of(table):
        n = table.shape[0]
        tall = np.pad(table.T, ((n, n), (0, 0)))
        return jnp.asarray(np.concatenate([tall, table], axis=0).astype(np.float32))

    consts, ystack, xown, xparts = map(jnp.asarray, (consts, ystack, xown, xparts))
    xtall, ytall = tall_of(xtable), tall_of(ytable)

    def swap(piece):
        got = [piece]
        for k in range(1, parts):
            got.append(lax.ppermute(piece, "split", [(i, (i + k) % parts) for i in range(parts)]))
        return got

    def spread(packet):
        held = [packet]
        for k in range(1, inner):
            to = [(i, i // inner * inner + partner(i % inner, k, inner)) for i in range(count)]
            held.append(lax.ppermute(packet, "dom", to))
        return held

    def choose(held, after):
        return call(
            functools.partial(choose_kernel, width=inner),
            [shape_of(size, width)] * tall,
            [SMEM, ANY] + [VMEM] * inner,
            flops=COVER,
            moved=8 * size * width * 4,
            name="choose",
        )(group, after, *held)

    def deliver(chosen, after):
        got = [chosen[0]]
        for k in range(1, tall):
            to = [(i, partner(i // inner, k, tall) * inner + i % inner) for i in range(count)]
            got.append(lax.ppermute(chosen[k], "dom", to))
        picked = call(
            functools.partial(pick_kernel, tall=tall, width=inner),
            [shape_of(size, width)],
            [SMEM] * 3 + [ANY] + [VMEM] * tall,
            moved=5 * size * width * 4,
            name="pick",
        )(group, lower_nbr, upper_nbr, after, *got)[0]
        return swap(picked)

    packet, rows = call(
        strip_kernel,
        [shape_of(size + HEAD, width), shape_of(zcap, width)],
        [SMEM] * 3 + [HBM],
        scratch=[
            pltpu.VMEM((slab, zcap, width), F32),
            pltpu.SemaphoreType.DMA((slab // CHUNK,)),
        ],
        moved=big,
        name="strip",
        limit=WIDE,
    )(z_extent, lower_nbr, upper_nbr, modes_now)
    held = spread(packet)

    ahead, coefs = call(
        functools.partial(ahead_kernel, full=full),
        [shape_of(size, width), shape_of(16, width)],
        [SMEM] * 2 + [HBM] * 2 + [VMEM] * 2,
        scratch=[
            pltpu.VMEM((slab, zcap, width), F32),
            pltpu.VMEM((slab, zcap, width), F32),
            pltpu.SemaphoreType.DMA((2, slab // CHUNK)),
        ],
        flops=10**8,
        moved=2 * big,
        name="ahead",
        limit=WIDE,
    )(z_extent, own, modes_now, modes_prev, rows, consts)
    chosen = choose(held, ahead)
    mine = swap(packet[:size])
    aheads = swap(ahead)

    tx, uy, vx, wy, near1, mixing, _ = call(
        functools.partial(relation_kernel, parts=parts),
        [
            shape_of(2, full, full),
            shape_of(2, width, width),
            shape_of(2, full, full),
            shape_of(2, width, width),
            shape_of(ROWS * full, width),
            shape_of(len(PAIRS), full, width),
            shape_of(ROWS * full, width),
        ],
        [SMEM] * 6 + [ANY] + [VMEM] * (2 + parts),
        flops=10**8,
        moved=2 * big,
        name="relation",
    )(lower_nbr, upper_nbr, x_shift, y_shift, own, coefs, chosen[0], xtall, ytall, *mine)
    far1 = deliver(chosen, near1)

    estack, hstack, gstack, *free = call(
        functools.partial(unforced_kernel, full=full),
        [
            shape_of(zcap, 3 * depth, dtype=BF16),
            shape_of(zcap, 3 * depth, dtype=BF16),
            shape_of(zcap, 3 * double_depth, dtype=BF16),
        ]
        + [shape_of(slab * zcap, width)] * parts,
        [SMEM] * 2 + [ANY] + [VMEM] * 5,
        scratch=[pltpu.VMEM((slab * zcap, width), F32)],
        flops=10**9,
        moved=4 * big,
        name="unforced",
    )(z_extent, own, far1[0], modes_now, modes_prev, consts, ystack, xparts)
    given = [
        lax.ppermute(free[k], "split", [(i, (i + k) % parts) for i in range(parts)])
        for k in range(1, parts)
    ]

    packet2, force1, strip2 = call(
        functools.partial(middle_kernel, parts=parts),
        [
            shape_of(size + HEAD, width),
            shape_of(ROWS * full, width),
            shape_of(ROWS * full, width),
        ],
        [SMEM] * 3 + [ANY] + [VMEM] * (4 + 2 * parts),
        scratch=[pltpu.VMEM((ROWS * full, width), F32)],
        flops=10**8,
        moved=2 * big,
        name="middle",
    )(own, lower_nbr, upper_nbr, estack, near1, tx, uy, mixing, *far1, *aheads)

    current, onward = call(
        functools.partial(between_kernel, full=full),
        [shape_of(slab, zcap, width)] * 2,
        [SMEM] * 2 + [VMEM] * 4,
        flops=10**9,
        moved=4 * big,
        name="between",
    )(z_extent, own, modes_now, modes_prev, force1, rows)
    chosen2 = choose(spread(packet2), onward)
    summed = call(
        first_kernel,
        [shape_of(slab * zcap, width)],
        [SMEM] + [VMEM] * 5,
        scratch=[pltpu.VMEM((double_depth * slab, width), F32)],
        flops=10**9,
        moved=2 * big,
        name="first",
    )(own, force1, gstack, ystack, xown, free[0])[0]
    near2 = call(
        near_kernel,
        [shape_of(ROWS * full, width)],
        [VMEM] * 3,
        flops=10**7,
        moved=big,
        name="near",
    )(strip2, vx, wy)[0]

    modes, pressure = call(
        functools.partial(last_kernel, full=full, parts=parts),
        [shape_of(slab, zcap, width), shape_of(slab * zcap, width)],
        [SMEM] + [VMEM] * (8 + 2 * parts),
        scratch=[
            pltpu.VMEM((ROWS * full, width), F32),
            pltpu.VMEM((ROWS * full, width), F32),
            pltpu.VMEM((depth * full, width), F32),
            pltpu.VMEM((depth * slab, width), F32),
        ],
        flops=10**9,
        moved=6 * big,
        name="last",
    )(
        own, near2, tx, uy, onward, estack, hstack, ystack, xown,
        *deliver(chosen2, summed), summed, *given,
    )
    return (modes, current, pressure.reshape(slab, zcap, width))


def solution(mesh):
    placed = (
        P("split", "dom", None),
        P("split", "dom", None),
        P("dom"),
        P("dom"),
        P("dom"),
        P("dom", None),
        P("dom", None),
    )
    return jax.shard_map(
        on_device,
        mesh=mesh,
        in_specs=placed,
        out_specs=(P("split", "dom", None), P("split", "dom", None), P("split", "dom", None)),
        check_vma=False,
    )
```

```python
import functools
import math

import jax
import jax.numpy as jnp
import numpy as np
from jax import lax
from jax.experimental import pallas as pl
from jax.experimental.pallas import tpu as pltpu
from jax.sharding import PartitionSpec as P

HIGH = lax.Precision.HIGHEST
F32 = jnp.float32
BF16 = jnp.bfloat16
STENCIL = (-490.0 / 180.0, 270.0 / 180.0, -27.0 / 180.0, 2.0 / 180.0)
COURANT = 0.5
FACE = 3
ROWS = 2 * FACE
HEAD = 8
SERIES = [(-1) ** n * 2.0 / math.factorial(2 * n + 2) for n in range(10)]
TERMS = 6
DOUBLE = [(-1) ** (n + 1) * (4 - 2.0 * 4.0 ** (n + 1)) / math.factorial(2 * n + 2) for n in range(14)]
DOUBLE_TERMS = 9
BASE = (COURANT * math.pi) ** 2
PAIRS = [(r, q) for r in range(ROWS) for q in range(r, ROWS)]
VMEM = pl.BlockSpec(memory_space=pltpu.VMEM)
SMEM = pl.BlockSpec(memory_space=pltpu.SMEM)
ANY = pl.BlockSpec(memory_space=pl.ANY)
HBM = pl.BlockSpec(memory_space=pltpu.HBM)
CHUNK = 8
COVER = 10**10
LIMIT = 12 * 1024 * 1024


def static_table(count):
    kk = np.arange(count)[:, None]
    xx = np.arange(count)[None, :]
    scale = np.where(kk == 0, np.sqrt(1.0 / count), np.sqrt(2.0 / count))
    return scale * np.cos(np.pi * kk * (xx + 0.5) / count)


def halves(table):
    high = table.astype(np.float32).astype(BF16)
    low = (table.astype(np.float32) - high.astype(np.float32)).astype(BF16)
    return high, low


def inner_size(count):
    best = 1
    for n in range(1, count + 1):
        if count % n == 0 and n * n <= count:
            best = n
    return best


def partner(place, step, count):
    if count & (count - 1) == 0:
        return place ^ step
    return (place + step) % count


def giver(place, step, count):
    return partner(place, step if count & (count - 1) == 0 else count - step, count)


def tall_split(data):
    high = data.astype(BF16).astype(F32)
    return jnp.concatenate([high, high, data - high], axis=0).astype(BF16)


def wide_split(data):
    high = data.astype(BF16)
    return jnp.concatenate([high, (data - high.astype(F32)).astype(BF16)], axis=1)


def dot(left, right):
    return jnp.dot(left, right, preferred_element_type=F32)


def exact_dot(left, right):
    return jnp.dot(left, right, precision=HIGH, preferred_element_type=F32)


def exact_dot_t(left, right):
    return lax.dot_general(
        left, right, (((1,), (1,)), ((), ())), precision=HIGH, preferred_element_type=F32
    )


def along_y(data, ystack):
    width = data.shape[1]
    both = dot(wide_split(data), ystack)
    return both[:, :width] + both[:, width:]


def cosine_of(count, odd, lenf):
    prod = count * odd
    turn = 4.0 * lenf
    rest = prod - jnp.floor(prod / turn) * turn
    return jnp.cos(rest * (0.5 * jnp.pi / lenf))


def scale_of(kk, lenf):
    return jnp.where(kk == 0, jnp.sqrt(1.0 / lenf), jnp.sqrt(2.0 / lenf))


def face_rows(near, flip, shape, extent):
    kk = lax.broadcasted_iota(jnp.int32, shape, 0)
    kf = kk.astype(F32)
    lenf = jnp.full(shape, extent.astype(F32))
    table = scale_of(kk, lenf) * cosine_of(kf, 2.0 * near + 1.0, lenf)
    sign = jnp.where((flip > 0) & (kk % 2 == 1), -1.0, 1.0)
    return jnp.where(kk < extent, table * sign, 0.0)


def gain_of(square):
    total = jnp.full_like(square, SERIES[-1])
    for value in reversed(SERIES[:-1]):
        total = total * square + value
    return total


def plane_square(shape, extent):
    kk = lax.broadcasted_iota(jnp.int32, shape, 0)
    kf = kk.astype(F32) / jnp.full(shape, extent.astype(F32))
    kf = jnp.where(kk < extent, kf, 0.0)
    ky = lax.broadcasted_iota(jnp.int32, shape, 1).astype(F32) / shape[1]
    return BASE * (kf * kf + ky * ky)


def x_square(kx, full):
    frac = kx.astype(F32) / full
    return BASE * (frac * frac)


def stencil(face, order):
    rows = []
    for jj in range(FACE):
        total = None
        for mm in range(FACE - jj):
            term = STENCIL[jj + mm + 1] * face[order[mm]]
            total = term if total is None else total + term
        rows.append(total)
    return rows


def through(planes, across, along):
    full, width = planes[0].shape
    out = exact_dot(across, jnp.concatenate(planes, axis=1))
    out = jnp.concatenate([out[:, i * width : (i + 1) * width] for i in range(FACE)], axis=0)
    out = exact_dot_t(out, along)
    return [out[i * full : (i + 1) * full] for i in range(FACE)]


def gather_kx(out, pieces, own):
    count = len(pieces)
    slab = pieces[0].shape[0] // ROWS
    full = slab * count
    for k, piece in enumerate(pieces):
        at = pl.multiple_of(lax.rem(own + count - k, count) * slab, slab)
        for r in range(ROWS):
            out[pl.ds(r * full + at, slab), :] = piece[r * slab : (r + 1) * slab, :]


def plane(ref, r):
    full = ref.shape[0] // ROWS
    return ref[r * full : (r + 1) * full, :]


def call(
    kernel, out_shape, in_specs, scratch=(), flops=0, moved=0, name=None, out=VMEM
):
    return pl.pallas_call(
        kernel,
        out_shape=out_shape,
        in_specs=in_specs,
        out_specs=[out] * len(out_shape),
        scratch_shapes=list(scratch),
        compiler_params=pltpu.CompilerParams(vmem_limit_bytes=LIMIT),
        cost_estimate=pl.CostEstimate(flops=flops, bytes_accessed=moved, transcendentals=0),
        name=name,
    )


def shape_of(*dims, dtype=F32):
    return jax.ShapeDtypeStruct(dims, dtype)


def label(packet, nbr):
    packet[packet.shape[0] - HEAD :, :] = jnp.full((HEAD, packet.shape[1]), nbr.astype(F32))


def strip_kernel(extent, below, above, now, strip, upper, lower, rows):
    slab, zcap, width = now.shape
    at = lax.broadcasted_iota(jnp.int32, (1, width), 1)
    far_face = at >= FACE
    near = jnp.where(far_face, ROWS - 1 - at, at)
    near = jnp.where(at < ROWS, near, 0).astype(F32)
    table = face_rows(near, far_face.astype(F32), (zcap, width), extent[0])
    rows[...] = table
    label(upper, above[0])
    label(lower, below[0])
    weights = [jnp.broadcast_to(table[:, r : r + 1], (zcap, width)) for r in range(ROWS)]
    for i in range(slab // CHUNK):
        part = now[i * CHUNK : (i + 1) * CHUNK]
        for r in range(ROWS):
            value = jnp.sum(part * weights[r][None], axis=1)
            strip[r * slab + i * CHUNK : r * slab + (i + 1) * CHUNK, :] = value
            at = r % FACE * slab + i * CHUNK
            (lower if r < FACE else upper)[at : at + CHUNK, :] = value


def lane_series(consts, first, count, shape, extent):
    kz = lax.broadcasted_iota(jnp.int32, shape, 0)
    frac = kz.astype(F32) / jnp.full(shape, extent.astype(F32))
    middle = jnp.where(kz < extent, BASE * frac * frac, 0.0) + BASE
    total = jnp.zeros(shape, F32)
    for j in reversed(range(count)):
        total = total * middle + consts[first + j : first + j + 1, :]
    return total


def z_table(ext, zcap):
    kk = lax.broadcasted_iota(jnp.int32, (zcap, zcap), 1)
    zz = lax.broadcasted_iota(jnp.int32, (zcap, zcap), 0)
    lenf = jnp.full((zcap, zcap), ext.astype(F32))
    table = scale_of(kk, lenf) * cosine_of(kk.astype(F32), 2.0 * zz.astype(F32) + 1.0, lenf)
    return jnp.where((kk < ext) & (zz < ext), table, 0.0)


def stack_lanes(table, depth):
    table = table[:, :depth]
    high = table.astype(BF16).astype(F32)
    return jnp.concatenate([high, table - high, high], axis=1).astype(BF16)


def ahead_kernel(
    extent, own, now, prev, rows, consts, strip, coefs, *, full
):
    slab, zcap, width = now.shape
    ext = extent[0]

    shape = (zcap, width)
    pairs = face_rows(consts[2:3, :], consts[3:4, :], shape, ext)
    pairs = pairs * face_rows(consts[4:5, :], consts[5:6, :], shape, ext)
    series = lane_series(consts, 8, len(SERIES), shape, ext)
    coefs[...] = exact_dot(series.T[: coefs.shape[0]], pairs)

    keep = lax.broadcasted_iota(jnp.int32, shape, 0) < ext
    square = plane_square(shape, ext)
    weights = [jnp.broadcast_to(rows[:, r : r + 1], shape) for r in range(ROWS)]
    for kx in range(slab):
        local = square + x_square(own[0] * slab + kx, full)
        twice = 2.0 - local * gain_of(local)
        ahead = jnp.where(keep, twice * now[kx] - prev[kx], 0.0)
        for r in range(ROWS):
            strip[r * slab + kx : r * slab + kx + 1, :] = jnp.sum(
                ahead * weights[r], axis=0, keepdims=True
            )


def relation_kernel(
    below, above, x_shift, y_shift, own, coefs, after, xtall, ytall, *rest, parts
):
    strips, (tx, uy, vx, wy, near, mixing, mine) = rest[:parts], rest[parts:]
    full, width = xtall.shape[1], ytall.shape[1]
    for f, (nbr, dx, dy) in enumerate(
        ((below, x_shift[0, 0], y_shift[0, 0]), (above, x_shift[0, 1], y_shift[0, 1]))
    ):
        has = jnp.where(nbr[0] >= 0, COURANT**2, 0.0).astype(F32)
        for count, move, tall, take, keep, scale in (
            (full, dx, xtall, tx, vx, has),
            (width, dy, ytall, uy, wy, None),
        ):
            move = jnp.clip(move, -count, count)
            slid = tall[pl.ds(count + move, count), :]
            at = lax.broadcasted_iota(jnp.int32, (count, count), 0) + move
            kept = jnp.where((at >= 0) & (at < count), tall[count : 2 * count, :], 0.0)
            plain = tall[3 * count :, :]
            taken, stay = exact_dot(plain, slid), exact_dot(plain, kept)
            take[f] = taken if scale is None else taken * scale
            keep[f] = stay if scale is None else stay * scale
    gather_kx(mine, strips, own[0])
    near_planes(mine, vx, wy, near)
    shape = (full, width)
    ax = lax.broadcasted_iota(jnp.int32, shape, 0).astype(F32) / full
    ay = lax.broadcasted_iota(jnp.int32, shape, 1).astype(F32) / width
    square = BASE * (ax * ax + ay * ay) - BASE
    for p in range(len(PAIRS)):
        total = jnp.full(shape, coefs[TERMS - 1, p])
        for n in reversed(range(TERMS - 1)):
            total = total * square + coefs[n, p]
        mixing[p] = total


def near_planes(mine, vx, wy, near):
    full = vx.shape[1]
    low = through(stencil([plane(mine, r) for r in range(FACE)], (0, 1, 2)), vx[0], wy[0])
    upp = through(stencil([plane(mine, FACE + r) for r in range(FACE)], (2, 1, 0)), vx[1], wy[1])
    for r, value in enumerate(low + upp[::-1]):
        near[r * full : (r + 1) * full, :] = value


def force_planes(far, near, tx, uy, force):
    full = tx.shape[1]
    low = through(stencil([plane(far, r) for r in range(FACE)], (2, 1, 0)), tx[0], uy[0])
    upp = through(stencil([plane(far, FACE + r) for r in range(FACE)], (0, 1, 2)), tx[1], uy[1])
    for r, value in enumerate(low + upp[::-1]):
        force[r * full : (r + 1) * full, :] = value - plane(near, r)


def choose_kernel(group, after, *refs, tall, width):
    uppers, lowers = refs[:tall], refs[tall : tall + width]
    out = refs[tall + width :]
    h, l = group[0] // width, lax.rem(group[0], width)
    for held, packets, places in (
        (uppers, out[:width], [h * width + partner(l, k, width) for k in range(width)]),
        (lowers, out[width:], [partner(h, k, tall) * width + l for k in range(tall)]),
    ):
        rows = packets[0].shape[0]
        for packet, place in zip(packets, places):
            dest = place.astype(F32)
            chosen = held[0][:rows, :]
            for other in held[1:]:
                chosen = jnp.where(other[rows : rows + 1, :] == dest, other[:rows, :], chosen)
            packet[...] = chosen


def pick_kernel(group, below, above, after, *refs, tall, width):
    uppers, lowers, out = refs[:width], refs[width:-1], refs[-1]
    half = out.shape[0] // 2
    h, l = group[0] // width, lax.rem(group[0], width)
    value = uppers[0][...]
    for k in range(1, width):
        here = lax.rem(jnp.maximum(below[0], 0), width) == giver(l, k, width)
        value = jnp.where(here, uppers[k][...], value)
    out[:half, :] = value
    value = lowers[0][...]
    for k in range(1, tall):
        here = jnp.maximum(above[0], 0) // width == giver(h, k, tall)
        value = jnp.where(here, lowers[k][...], value)
    out[half:, :] = value


def middle_kernel(own, below, above, after, near, tx, uy, mixing, *rest, parts):
    far, ahead = rest[:parts], rest[parts : 2 * parts]
    upper, lower, force, strip, spare = rest[2 * parts :]
    gather_kx(spare, far, own[0])
    force_planes(spare, near, tx, uy, force)
    gather_kx(strip, ahead, own[0])
    full = tx.shape[1]
    slab = full // parts
    for r in range(ROWS):
        total = plane(strip, r)
        for q in range(ROWS):
            total = total + mixing[PAIRS.index((min(r, q), max(r, q)))] * plane(force, q)
        strip[r * full : (r + 1) * full, :] = total
    at = pl.multiple_of(own[0] * slab, slab)
    for r in range(ROWS):
        packet = lower if r < FACE else upper
        packet[r % FACE * slab : (r % FACE + 1) * slab, :] = strip[pl.ds(r * full + at, slab), :]
    label(upper, above[0])
    label(lower, below[0])


def near_kernel(strip, vx, wy, near):
    near_planes(strip, vx, wy, near)


def unforced_kernel(
    extent, own, after, now, prev, ystack, xparts, *rest, full
):
    free, field = rest[:-1], rest[-1]
    slab, zcap, width = now.shape
    shape = (zcap, width)
    ext = extent[0]
    zstack = stack_lanes(z_table(ext, zcap), zcap)
    keep = lax.broadcasted_iota(jnp.int32, shape, 0) < ext
    square = plane_square(shape, ext)
    group = min(4, slab)

    def body(i, _):
        planes = []
        for half in range(group):
            at = group * i + half
            local = square + x_square(own[0] * slab + at, full)
            twice = 2.0 - local * gain_of(local)
            first = now[at]
            later = twice * (twice * first - prev[at]) - first
            planes.append(jnp.where(keep, later, 0.0))
        for j in range(0, group, 2):
            wide = dot(zstack, tall_split(jnp.concatenate(planes[j : j + 2], axis=1)))
            for half in range(2):
                at = pl.multiple_of((group * i + j + half) * zcap, zcap)
                field[pl.ds(at, zcap), :] = wide[:, half * width : (half + 1) * width]
        return 0

    lax.fori_loop(0, slab // group, body, 0)
    block = min(16, slab) * zcap
    for i in range(slab * zcap // block):
        span = slice(i * block, (i + 1) * block)
        field[span, :] = along_y(field[span, :], ystack[...])
    parts = full // slab
    across = xparts[own[0]]
    for i in range(0, zcap, 2):
        pair = [field[pl.ds(i + half, slab, stride=zcap), :] for half in range(2)]
        wide = dot(across, tall_split(jnp.concatenate(pair, axis=1)))
        for k in range(parts):
            for half in range(2):
                free[k][pl.ds(i + half, slab, stride=zcap), :] = wide[
                    k * slab : (k + 1) * slab, half * width : (half + 1) * width
                ]


def between_kernel(
    extent, own, now, prev, force, rows, consts, current, onward, estack, hstack, gstack, *, full
):
    slab, zcap, width = now.shape
    shape = (zcap, width)
    ext = extent[0]
    ztable = z_table(ext, zcap)
    face = face_rows(consts[6:7, :], consts[7:8, :], shape, ext)
    terms = face * lane_series(consts, 24, len(SERIES), shape, ext)
    depth = estack.shape[1] // 3
    estack[...] = stack_lanes(terms, depth)
    hstack[...] = stack_lanes(exact_dot(ztable, terms), depth)
    terms = face * lane_series(consts, 40, len(DOUBLE), shape, ext)
    gstack[...] = stack_lanes(exact_dot(ztable, terms), gstack.shape[1] // 3)
    keep = lax.broadcasted_iota(jnp.int32, shape, 0) < extent[0]
    square = plane_square(shape, extent[0])
    weights = [jnp.broadcast_to(rows[:, r : r + 1], shape) for r in range(ROWS)]
    group = min(4, slab)

    def body(i, _):
        for half in range(group):
            at = group * i + half
            kx = own[0] * slab + at
            local = square + x_square(kx, full)
            gain = gain_of(local)
            total = None
            for r in range(ROWS):
                term = weights[r] * force[pl.ds(r * full + kx, 1), :]
                total = term if total is None else total + term
            twice = 2.0 - local * gain
            first = jnp.where(keep, now[at], 0.0)
            value = twice * first - jnp.where(keep, prev[at], 0.0) + gain * total
            current[at] = value
            onward[at] = twice * value - first
        return 0

    lax.fori_loop(0, slab // group, body, 0)


def series_planes(force, terms, count):
    full, width = force.shape[0] // ROWS, force.shape[1]
    ax = lax.broadcasted_iota(jnp.int32, (full, width), 0).astype(F32) / full
    ay = lax.broadcasted_iota(jnp.int32, (full, width), 1).astype(F32) / width
    square = BASE * (ax * ax + ay * ay) - BASE
    planes = [plane(force, r) for r in range(ROWS)]
    for n in range(count):
        if n:
            planes = [value * square for value in planes]
        for r in range(ROWS):
            at = (n * ROWS + r) * full
            terms[at : at + full, :] = planes[r]
    used = count * ROWS * full
    if used < terms.shape[0]:
        terms[used:, :] = jnp.zeros((terms.shape[0] - used, width), F32)


def lift(terms, across, table, ystack, given, turned, pressure, count, done):
    zcap = table.shape[0]
    depth = table.shape[1] // 3
    used = count * ROWS
    full, width = across.shape[1] // 3, terms.shape[1]
    slab = across.shape[0]
    turned[used * slab :, :] = jnp.zeros(((depth - used) * slab, width), F32)
    for at in range(0, used, 2):
        pair = [terms[(at + half) * full : (at + half + 1) * full, :] for half in range(2)]
        wide = dot(across, tall_split(jnp.concatenate(pair, axis=1)))
        for half in range(2):
            turned[(at + half) * slab : (at + half + 1) * slab, :] = wide[
                :, half * width : (half + 1) * width
            ]
    block = ROWS * slab
    for n in range(count):
        span = slice(n * block, (n + 1) * block)
        turned[span, :] = along_y(turned[span, :], ystack[...])
    for i in range(0, slab, 2):
        pair = [turned[pl.ds(i + half, depth, stride=slab), :] for half in range(2)]
        wide = dot(table[...], tall_split(jnp.concatenate(pair, axis=1)))
        for half in range(2):
            span = slice((i + half) * zcap, (i + half + 1) * zcap)
            value = wide[:, half * width : (half + 1) * width]
            for piece in given:
                value = value + piece[span, :]
            pressure[span, :] = value
        done(i + 2)


def first_kernel(own, force, gstack, ystack, xown, free, summed, terms, turned):
    series_planes(force, terms, DOUBLE_TERMS)
    lift(
        terms, xown[own[0]], gstack, ystack, [free], turned, summed, DOUBLE_TERMS, lambda i: None
    )


def last_kernel(own, near, tx, uy, onward, estack, hstack, ystack, xown, *rest, full, parts):
    far, given = rest[:parts], rest[parts : 2 * parts]
    modes_out, pressure_out, modes, pressure, spare, force, terms, turned, sems = rest[2 * parts :]
    slab, zcap, width = onward.shape
    depth = estack.shape[1] // 3
    gather_kx(spare, far, own[0])
    force_planes(spare, near, tx, uy, force)
    sends = []

    def send(source, target, at, size):
        span = pl.ds(at, size)
        sends.append(
            pltpu.make_async_copy(source.at[span], target.at[span], sems.at[len(sends)])
        )
        sends[-1].start()

    series_planes(force, terms, TERMS)
    own_at = own[0] * slab
    for i in range(0, slab, 2):
        pair = [terms[pl.ds(own_at + i + half, depth, stride=full), :] for half in range(2)]
        wide = dot(estack[...], tall_split(jnp.concatenate(pair, axis=1)))
        for half in range(2):
            modes[i + half] = onward[i + half] + wide[:, half * width : (half + 1) * width]
        if (i + 2) % CHUNK == 0:
            send(modes, modes_out, i + 2 - CHUNK, CHUNK)

    def done(i):
        if i % CHUNK == 0:
            send(pressure, pressure_out, (i - CHUNK) * zcap, CHUNK * zcap)

    lift(terms, xown[own[0]], hstack, ystack, given, turned, pressure, TERMS, done)
    for copy in sends:
        copy.wait()


def on_device(modes_now, modes_prev, z_extent, lower_nbr, upper_nbr, x_shift, y_shift):
    slab, zcap, width = modes_now.shape
    parts = lax.axis_size("split")
    count = lax.axis_size("dom")
    full = slab * parts
    own = lax.axis_index("split").astype(jnp.int32)[None]
    group = lax.axis_index("dom").astype(jnp.int32)[None]
    inner = inner_size(count)
    tall = count // inner
    size = ROWS * slab
    big = 4 * slab * zcap * width

    xtable, ytable = static_table(full), static_table(width)
    consts = np.zeros((56, width), np.float32)
    for r in range(ROWS):
        consts[0, r], consts[1, r] = (r, 0) if r < FACE else (ROWS - 1 - r, 1)
    for p, (r, q) in enumerate(PAIRS):
        consts[2:4, p], consts[4:6, p] = consts[0:2, r], consts[0:2, q]
    for n in range(DOUBLE_TERMS):
        lanes = slice(n * ROWS, (n + 1) * ROWS)
        consts[6:8, lanes] = consts[0:2, :ROWS]
        for j in range(len(SERIES) - n if n < TERMS else 0):
            consts[8 + j, n] = consts[24 + j, lanes] = SERIES[n + j] * math.comb(n + j, n)
        for j in range(len(DOUBLE) - n):
            consts[40 + j, lanes] = DOUBLE[n + j] * math.comb(n + j, n)
    depth = -(-TERMS * ROWS // 16) * 16
    double_depth = -(-DOUBLE_TERMS * ROWS // 16) * 16
    yhigh, ylow = halves(ytable)
    ystack = np.block([[yhigh, ylow], [yhigh, np.zeros_like(yhigh)]])
    xhigh, xlow = halves(xtable.T)
    xown = np.stack(
        [
            np.concatenate([t[s * slab : (s + 1) * slab] for t in (xhigh, xlow, xhigh)], axis=1)
            for s in range(parts)
        ]
    )
    xparts = np.stack(
        [
            np.concatenate(
                [
                    np.concatenate(
                        [
                            t[(s + k) % parts * slab : ((s + k) % parts + 1) * slab,
                              s * slab : (s + 1) * slab]
                            for k in range(parts)
                        ],
                        axis=0,
                    )
                    for t in (xhigh, xlow, xhigh)
                ],
                axis=1,
            )
            for s in range(parts)
        ]
    )

    def tall_of(table):
        n = table.shape[0]
        tall = np.pad(table.T, ((n, n), (0, 0)))
        return jnp.asarray(np.concatenate([tall, table], axis=0).astype(np.float32))

    consts, ystack, xown, xparts = map(jnp.asarray, (consts, ystack, xown, xparts))
    xtall, ytall = tall_of(xtable), tall_of(ytable)

    def swap(piece):
        got = [piece]
        for k in range(1, parts):
            got.append(lax.ppermute(piece, "split", [(i, (i + k) % parts) for i in range(parts)]))
        return got

    face = FACE * slab
    fast = lambda k: [(i, i // inner * inner + partner(i % inner, k, inner)) for i in range(count)]
    slow = lambda k: [(i, partner(i // inner, k, tall) * inner + i % inner) for i in range(count)]

    def spread(upper, lower):
        uppers = [upper] + [lax.ppermute(upper, "dom", slow(k)) for k in range(1, tall)]
        lowers = [lower] + [lax.ppermute(lower, "dom", fast(k)) for k in range(1, inner)]
        return uppers + lowers

    def choose(held, after):
        return call(
            functools.partial(choose_kernel, tall=tall, width=inner),
            [shape_of(face, width)] * (inner + tall),
            [SMEM, ANY] + [VMEM] * (inner + tall),
            flops=COVER,
            moved=8 * size * width * 4,
            name="choose",
        )(group, after, *held)

    def deliver(chosen, after):
        uppers, lowers = chosen[:inner], chosen[inner:]
        got = [uppers[0]] + [lax.ppermute(uppers[k], "dom", fast(k)) for k in range(1, inner)]
        got += [lowers[0]] + [lax.ppermute(lowers[k], "dom", slow(k)) for k in range(1, tall)]
        picked = call(
            functools.partial(pick_kernel, tall=tall, width=inner),
            [shape_of(size, width)],
            [SMEM] * 3 + [ANY] + [VMEM] * (inner + tall),
            moved=5 * size * width * 4,
            name="pick",
        )(group, lower_nbr, upper_nbr, after, *got)[0]
        return swap(picked)

    strip, upper, lower, rows = call(
        strip_kernel,
        [
            shape_of(size, width),
            shape_of(face + HEAD, width),
            shape_of(face + HEAD, width),
            shape_of(zcap, width),
        ],
        [SMEM] * 3 + [VMEM],
        moved=big,
        name="strip",
    )(z_extent, lower_nbr, upper_nbr, modes_now)
    held = spread(upper, lower)
    ahead, coefs = call(
        functools.partial(ahead_kernel, full=full),
        [shape_of(size, width), shape_of(16, width)],
        [SMEM] * 2 + [VMEM] * 4,
        flops=10**8,
        moved=2 * big,
        name="ahead",
    )(z_extent, own, modes_now, modes_prev, rows, consts)
    chosen = choose(held, ahead)
    mine = swap(strip)
    aheads = swap(ahead)

    tx, uy, vx, wy, near1, mixing, _ = call(
        functools.partial(relation_kernel, parts=parts),
        [
            shape_of(2, full, full),
            shape_of(2, width, width),
            shape_of(2, full, full),
            shape_of(2, width, width),
            shape_of(ROWS * full, width),
            shape_of(len(PAIRS), full, width),
            shape_of(ROWS * full, width),
        ],
        [SMEM] * 6 + [ANY] + [VMEM] * (2 + parts),
        flops=10**8,
        moved=2 * big,
        name="relation",
    )(lower_nbr, upper_nbr, x_shift, y_shift, own, coefs, chosen[0], xtall, ytall, *mine)
    far1 = deliver(chosen, near1)

    free = call(
        functools.partial(unforced_kernel, full=full),
        [shape_of(slab * zcap, width)] * parts,
        [SMEM] * 2 + [ANY] + [VMEM] * 4,
        scratch=[pltpu.VMEM((slab * zcap, width), F32)],
        flops=10**9,
        moved=4 * big,
        name="unforced",
    )(z_extent, own, far1[0], modes_now, modes_prev, ystack, xparts)
    given = [
        lax.ppermute(free[k], "split", [(i, (i + k) % parts) for i in range(parts)])
        for k in range(1, parts)
    ]

    upper2, lower2, force1, strip2 = call(
        functools.partial(middle_kernel, parts=parts),
        [
            shape_of(face + HEAD, width),
            shape_of(face + HEAD, width),
            shape_of(ROWS * full, width),
            shape_of(ROWS * full, width),
        ],
        [SMEM] * 3 + [ANY] + [VMEM] * (4 + 2 * parts),
        scratch=[pltpu.VMEM((ROWS * full, width), F32)],
        flops=10**8,
        moved=2 * big,
        name="middle",
    )(own, lower_nbr, upper_nbr, free[0], near1, tx, uy, mixing, *far1, *aheads)

    current, onward, estack, hstack, gstack = call(
        functools.partial(between_kernel, full=full),
        [
            shape_of(slab, zcap, width),
            shape_of(slab, zcap, width),
            shape_of(zcap, 3 * depth, dtype=BF16),
            shape_of(zcap, 3 * depth, dtype=BF16),
            shape_of(zcap, 3 * double_depth, dtype=BF16),
        ],
        [SMEM] * 2 + [VMEM] * 5,
        flops=10**9,
        moved=4 * big,
        name="between",
    )(z_extent, own, modes_now, modes_prev, force1, rows, consts)
    chosen2 = choose(spread(upper2, lower2), onward)
    summed = call(
        first_kernel,
        [shape_of(slab * zcap, width)],
        [SMEM] + [VMEM] * 5,
        scratch=[
            pltpu.VMEM((DOUBLE_TERMS * ROWS * full, width), F32),
            pltpu.VMEM((double_depth * slab, width), F32),
        ],
        flops=10**9,
        moved=2 * big,
        name="first",
    )(own, force1, gstack, ystack, xown, free[0])[0]
    near2 = call(
        near_kernel,
        [shape_of(ROWS * full, width)],
        [VMEM] * 3,
        flops=10**7,
        moved=big,
        name="near",
    )(strip2, vx, wy)[0]

    modes, pressure = call(
        functools.partial(last_kernel, full=full, parts=parts),
        [shape_of(slab, zcap, width), shape_of(slab * zcap, width)],
        [SMEM] + [VMEM] * (8 + 2 * parts),
        scratch=[
            pltpu.VMEM((slab, zcap, width), F32),
            pltpu.VMEM((slab * zcap, width), F32),
            pltpu.VMEM((ROWS * full, width), F32),
            pltpu.VMEM((ROWS * full, width), F32),
            pltpu.VMEM((depth * full, width), F32),
            pltpu.VMEM((depth * slab, width), F32),
            pltpu.SemaphoreType.DMA((2 * (slab // CHUNK),)),
        ],
        flops=10**9,
        moved=6 * big,
        name="last",
        out=HBM,
    )(
        own, near2, tx, uy, onward, estack, hstack, ystack, xown,
        *deliver(chosen2, summed), summed, *given,
    )
    return (modes, current, pressure.reshape(slab, zcap, width))


def solution(mesh):
    placed = (
        P("split", "dom", None),
        P("split", "dom", None),
        P("dom"),
        P("dom"),
        P("dom"),
        P("dom", None),
        P("dom", None),
    )
    return jax.shard_map(
        on_device,
        mesh=mesh,
        in_specs=placed,
        out_specs=(P("split", "dom", None), P("split", "dom", None), P("split", "dom", None)),
        check_vma=False,
    )
```

```python
import functools
import math

import jax
import jax.numpy as jnp
import numpy as np
from jax import lax
from jax.experimental import pallas as pl
from jax.experimental.pallas import tpu as pltpu
from jax.sharding import PartitionSpec as P

HIGH = lax.Precision.HIGHEST
F32 = jnp.float32
BF16 = jnp.bfloat16
STENCIL = (-490.0 / 180.0, 270.0 / 180.0, -27.0 / 180.0, 2.0 / 180.0)
COURANT = 0.5
FACE = 3
ROWS = 2 * FACE
HEAD = 8
SERIES = [(-1) ** n * 2.0 / math.factorial(2 * n + 2) for n in range(10)]
TERMS = 6
DOUBLE = [(-1) ** (n + 1) * (4 - 2.0 * 4.0 ** (n + 1)) / math.factorial(2 * n + 2) for n in range(14)]
DOUBLE_TERMS = 9
BASE = (COURANT * math.pi) ** 2
PAIRS = [(r, q) for r in range(ROWS) for q in range(r, ROWS)]
VMEM = pl.BlockSpec(memory_space=pltpu.VMEM)
SMEM = pl.BlockSpec(memory_space=pltpu.SMEM)
ANY = pl.BlockSpec(memory_space=pl.ANY)
HBM = pl.BlockSpec(memory_space=pltpu.HBM)
CHUNK = 8
COVER = 10**10
LIMIT = 12 * 1024 * 1024


def static_table(count):
    kk = np.arange(count)[:, None]
    xx = np.arange(count)[None, :]
    scale = np.where(kk == 0, np.sqrt(1.0 / count), np.sqrt(2.0 / count))
    return scale * np.cos(np.pi * kk * (xx + 0.5) / count)


def halves(table):
    high = table.astype(np.float32).astype(BF16)
    low = (table.astype(np.float32) - high.astype(np.float32)).astype(BF16)
    return high, low


def inner_size(count):
    best = 1
    for n in range(1, count + 1):
        if count % n == 0 and n * n <= count:
            best = n
    return best


def partner(place, step, count):
    if count & (count - 1) == 0:
        return place ^ step
    return (place + step) % count


def tall_split(data):
    high = data.astype(BF16).astype(F32)
    return jnp.concatenate([high, high, data - high], axis=0).astype(BF16)


def wide_split(data):
    high = data.astype(BF16)
    return jnp.concatenate([high, (data - high.astype(F32)).astype(BF16)], axis=1)


def dot(left, right):
    return jnp.dot(left, right, preferred_element_type=F32)


def exact_dot(left, right):
    return jnp.dot(left, right, precision=HIGH, preferred_element_type=F32)


def exact_dot_t(left, right):
    return lax.dot_general(
        left, right, (((1,), (1,)), ((), ())), precision=HIGH, preferred_element_type=F32
    )


def along_y(data, ystack):
    width = data.shape[1]
    both = dot(wide_split(data), ystack)
    return both[:, :width] + both[:, width:]


def cosine_of(count, odd, lenf):
    prod = count * odd
    turn = 4.0 * lenf
    rest = prod - jnp.floor(prod / turn) * turn
    return jnp.cos(rest * (0.5 * jnp.pi / lenf))


def scale_of(kk, lenf):
    return jnp.where(kk == 0, jnp.sqrt(1.0 / lenf), jnp.sqrt(2.0 / lenf))


def face_rows(near, flip, shape, extent):
    kk = lax.broadcasted_iota(jnp.int32, shape, 0)
    kf = kk.astype(F32)
    lenf = jnp.full(shape, extent.astype(F32))
    table = scale_of(kk, lenf) * cosine_of(kf, 2.0 * near + 1.0, lenf)
    sign = jnp.where((flip > 0) & (kk % 2 == 1), -1.0, 1.0)
    return jnp.where(kk < extent, table * sign, 0.0)


def gain_of(square):
    total = jnp.full_like(square, SERIES[-1])
    for value in reversed(SERIES[:-1]):
        total = total * square + value
    return total


def plane_square(shape, extent):
    kk = lax.broadcasted_iota(jnp.int32, shape, 0)
    kf = kk.astype(F32) / jnp.full(shape, extent.astype(F32))
    kf = jnp.where(kk < extent, kf, 0.0)
    ky = lax.broadcasted_iota(jnp.int32, shape, 1).astype(F32) / shape[1]
    return BASE * (kf * kf + ky * ky)


def x_square(kx, full):
    frac = kx.astype(F32) / full
    return BASE * (frac * frac)


def stencil(face, order):
    rows = []
    for jj in range(FACE):
        total = None
        for mm in range(FACE - jj):
            term = STENCIL[jj + mm + 1] * face[order[mm]]
            total = term if total is None else total + term
        rows.append(total)
    return rows


def through(planes, across, along):
    full, width = planes[0].shape
    out = exact_dot(across, jnp.concatenate(planes, axis=1))
    out = jnp.concatenate([out[:, i * width : (i + 1) * width] for i in range(FACE)], axis=0)
    out = exact_dot_t(out, along)
    return [out[i * full : (i + 1) * full] for i in range(FACE)]


def gather_kx(out, pieces, own):
    count = len(pieces)
    full = out.shape[0] // ROWS
    slab = full // count
    for k, piece in enumerate(pieces):
        at = pl.multiple_of(lax.rem(own + count - k, count) * slab, slab)
        for r in range(ROWS):
            out[pl.ds(r * full + at, slab), :] = piece[r * slab : (r + 1) * slab, :]


def plane(ref, r):
    full = ref.shape[0] // ROWS
    return ref[r * full : (r + 1) * full, :]


def call(
    kernel, out_shape, in_specs, scratch=(), flops=0, moved=0, name=None, out=VMEM
):
    return pl.pallas_call(
        kernel,
        out_shape=out_shape,
        in_specs=in_specs,
        out_specs=[out] * len(out_shape),
        scratch_shapes=list(scratch),
        compiler_params=pltpu.CompilerParams(vmem_limit_bytes=LIMIT),
        cost_estimate=pl.CostEstimate(flops=flops, bytes_accessed=moved, transcendentals=0),
        name=name,
    )


def shape_of(*dims, dtype=F32):
    return jax.ShapeDtypeStruct(dims, dtype)


def label(packet, below, above):
    at = lax.broadcasted_iota(jnp.int32, (HEAD, packet.shape[1]), 0)
    names = jnp.where(at < HEAD // 2, above, below)
    packet[packet.shape[0] - HEAD :, :] = names.astype(F32)


def strip_kernel(extent, below, above, now, packet, rows):
    slab, zcap, width = now.shape
    at = lax.broadcasted_iota(jnp.int32, (1, width), 1)
    far_face = at >= FACE
    near = jnp.where(far_face, ROWS - 1 - at, at)
    near = jnp.where(at < ROWS, near, 0).astype(F32)
    table = face_rows(near, far_face.astype(F32), (zcap, width), extent[0])
    rows[...] = table
    label(packet, below[0], above[0])
    weights = [jnp.broadcast_to(table[:, r : r + 1], (zcap, width)) for r in range(ROWS)]
    for i in range(slab // CHUNK):
        part = now[i * CHUNK : (i + 1) * CHUNK]
        for r in range(ROWS):
            span = slice(r * slab + i * CHUNK, r * slab + (i + 1) * CHUNK)
            packet[span, :] = jnp.sum(part * weights[r][None], axis=1)


def lane_series(consts, first, count, shape, extent):
    kz = lax.broadcasted_iota(jnp.int32, shape, 0)
    frac = kz.astype(F32) / jnp.full(shape, extent.astype(F32))
    middle = jnp.where(kz < extent, BASE * frac * frac, 0.0) + BASE
    total = jnp.zeros(shape, F32)
    for j in reversed(range(count)):
        total = total * middle + consts[first + j : first + j + 1, :]
    return total


def z_table(ext, zcap):
    kk = lax.broadcasted_iota(jnp.int32, (zcap, zcap), 1)
    zz = lax.broadcasted_iota(jnp.int32, (zcap, zcap), 0)
    lenf = jnp.full((zcap, zcap), ext.astype(F32))
    table = scale_of(kk, lenf) * cosine_of(kk.astype(F32), 2.0 * zz.astype(F32) + 1.0, lenf)
    return jnp.where((kk < ext) & (zz < ext), table, 0.0)


def stack_lanes(table, depth):
    table = table[:, :depth]
    high = table.astype(BF16).astype(F32)
    return jnp.concatenate([high, table - high, high], axis=1).astype(BF16)


def ahead_kernel(
    extent, own, now, prev, rows, consts, strip, coefs, *, full
):
    slab, zcap, width = now.shape
    ext = extent[0]

    shape = (zcap, width)
    pairs = face_rows(consts[2:3, :], consts[3:4, :], shape, ext)
    pairs = pairs * face_rows(consts[4:5, :], consts[5:6, :], shape, ext)
    series = lane_series(consts, 8, len(SERIES), shape, ext)
    coefs[...] = exact_dot(series.T[: coefs.shape[0]], pairs)

    keep = lax.broadcasted_iota(jnp.int32, shape, 0) < ext
    square = plane_square(shape, ext)
    weights = [jnp.broadcast_to(rows[:, r : r + 1], shape) for r in range(ROWS)]
    for kx in range(slab):
        local = square + x_square(own[0] * slab + kx, full)
        twice = 2.0 - local * gain_of(local)
        ahead = jnp.where(keep, twice * now[kx] - prev[kx], 0.0)
        for r in range(ROWS):
            strip[r * slab + kx : r * slab + kx + 1, :] = jnp.sum(
                ahead * weights[r], axis=0, keepdims=True
            )


def relation_kernel(
    below, above, x_shift, y_shift, own, coefs, after, xtall, ytall, *rest, parts
):
    strips, (tx, uy, vx, wy, near, mixing, mine) = rest[:parts], rest[parts:]
    full, width = xtall.shape[1], ytall.shape[1]
    for f, (nbr, dx, dy) in enumerate(
        ((below, x_shift[0, 0], y_shift[0, 0]), (above, x_shift[0, 1], y_shift[0, 1]))
    ):
        has = jnp.where(nbr[0] >= 0, COURANT**2, 0.0).astype(F32)
        for count, move, tall, take, keep, scale in (
            (full, dx, xtall, tx, vx, has),
            (width, dy, ytall, uy, wy, None),
        ):
            move = jnp.clip(move, -count, count)
            slid = tall[pl.ds(count + move, count), :]
            at = lax.broadcasted_iota(jnp.int32, (count, count), 0) + move
            kept = jnp.where((at >= 0) & (at < count), tall[count : 2 * count, :], 0.0)
            plain = tall[3 * count :, :]
            taken, stay = exact_dot(plain, slid), exact_dot(plain, kept)
            take[f] = taken if scale is None else taken * scale
            keep[f] = stay if scale is None else stay * scale
    gather_kx(mine, strips, own[0])
    near_planes(mine, vx, wy, near)
    shape = (full, width)
    ax = lax.broadcasted_iota(jnp.int32, shape, 0).astype(F32) / full
    ay = lax.broadcasted_iota(jnp.int32, shape, 1).astype(F32) / width
    square = BASE * (ax * ax + ay * ay) - BASE
    for p in range(len(PAIRS)):
        total = jnp.full(shape, coefs[TERMS - 1, p])
        for n in reversed(range(TERMS - 1)):
            total = total * square + coefs[n, p]
        mixing[p] = total


def near_planes(mine, vx, wy, near):
    full = vx.shape[1]
    low = through(stencil([plane(mine, r) for r in range(FACE)], (0, 1, 2)), vx[0], wy[0])
    upp = through(stencil([plane(mine, FACE + r) for r in range(FACE)], (2, 1, 0)), vx[1], wy[1])
    for r, value in enumerate(low + upp[::-1]):
        near[r * full : (r + 1) * full, :] = value


def force_planes(far, near, tx, uy, force):
    full = tx.shape[1]
    low = through(stencil([plane(far, r) for r in range(FACE)], (2, 1, 0)), tx[0], uy[0])
    upp = through(stencil([plane(far, FACE + r) for r in range(FACE)], (0, 1, 2)), tx[1], uy[1])
    for r, value in enumerate(low + upp[::-1]):
        force[r * full : (r + 1) * full, :] = value - plane(near, r)


def choose_kernel(group, after, *refs, width):
    held, out = refs[:width], refs[width:]
    rows = out[0].shape[0]
    half = rows // 2
    h, l = group[0] // width, lax.rem(group[0], width)
    for k in range(len(out)):
        dest = (lax.rem(h + k, len(out)) * width + l).astype(F32)
        for f in range(2):
            lo, hi = f * half, (f + 1) * half
            row = rows + (0 if f == 1 else HEAD // 2)
            chosen = held[0][lo:hi, :]
            for other in held[1:]:
                chosen = jnp.where(other[row : row + 1, :] == dest, other[lo:hi, :], chosen)
            out[k][lo:hi, :] = chosen


def pick_kernel(group, below, above, after, *refs, tall, width):
    got, out = refs[:-1], refs[-1]
    half = out.shape[0] // 2
    h = group[0] // width
    for f, nbr in enumerate((below, above)):
        lo = half if f == 0 else 0
        value = got[0][lo : lo + half, :]
        for k in range(1, tall):
            here = jnp.maximum(nbr[0], 0) // width == lax.rem(h + tall - k, tall)
            value = jnp.where(here, got[k][lo : lo + half, :], value)
        out[f * half : (f + 1) * half, :] = value


def middle_kernel(own, below, above, after, near, tx, uy, mixing, *rest, parts):
    far, ahead = rest[:parts], rest[parts : 2 * parts]
    packet, force, strip, spare = rest[2 * parts :]
    gather_kx(spare, far, own[0])
    force_planes(spare, near, tx, uy, force)
    gather_kx(strip, ahead, own[0])
    full = tx.shape[1]
    slab = full // parts
    for r in range(ROWS):
        total = plane(strip, r)
        for q in range(ROWS):
            total = total + mixing[PAIRS.index((min(r, q), max(r, q)))] * plane(force, q)
        strip[r * full : (r + 1) * full, :] = total
    at = pl.multiple_of(own[0] * slab, slab)
    for r in range(ROWS):
        packet[r * slab : (r + 1) * slab, :] = strip[pl.ds(r * full + at, slab), :]
    label(packet, below[0], above[0])


def near_kernel(strip, vx, wy, near):
    near_planes(strip, vx, wy, near)


def unforced_kernel(
    extent, own, after, now, prev, ystack, xparts, *rest, full
):
    free, field = rest[:-1], rest[-1]
    slab, zcap, width = now.shape
    shape = (zcap, width)
    ext = extent[0]
    zstack = stack_lanes(z_table(ext, zcap), zcap)
    keep = lax.broadcasted_iota(jnp.int32, shape, 0) < ext
    square = plane_square(shape, ext)
    group = min(4, slab)

    def body(i, _):
        planes = []
        for half in range(group):
            at = group * i + half
            local = square + x_square(own[0] * slab + at, full)
            twice = 2.0 - local * gain_of(local)
            first = now[at]
            later = twice * (twice * first - prev[at]) - first
            planes.append(jnp.where(keep, later, 0.0))
        for j in range(0, group, 2):
            wide = dot(zstack, tall_split(jnp.concatenate(planes[j : j + 2], axis=1)))
            for half in range(2):
                at = pl.multiple_of((group * i + j + half) * zcap, zcap)
                field[pl.ds(at, zcap), :] = wide[:, half * width : (half + 1) * width]
        return 0

    lax.fori_loop(0, slab // group, body, 0)
    block = min(16, slab) * zcap
    for i in range(slab * zcap // block):
        span = slice(i * block, (i + 1) * block)
        field[span, :] = along_y(field[span, :], ystack[...])
    parts = full // slab
    across = xparts[own[0]]
    for i in range(0, zcap, 2):
        pair = [field[pl.ds(i + half, slab, stride=zcap), :] for half in range(2)]
        wide = dot(across, tall_split(jnp.concatenate(pair, axis=1)))
        for k in range(parts):
            for half in range(2):
                free[k][pl.ds(i + half, slab, stride=zcap), :] = wide[
                    k * slab : (k + 1) * slab, half * width : (half + 1) * width
                ]


def between_kernel(
    extent, own, now, prev, force, rows, consts, current, onward, estack, hstack, gstack, *, full
):
    slab, zcap, width = now.shape
    shape = (zcap, width)
    ext = extent[0]
    ztable = z_table(ext, zcap)
    face = face_rows(consts[6:7, :], consts[7:8, :], shape, ext)
    terms = face * lane_series(consts, 24, len(SERIES), shape, ext)
    depth = estack.shape[1] // 3
    estack[...] = stack_lanes(terms, depth)
    hstack[...] = stack_lanes(exact_dot(ztable, terms), depth)
    terms = face * lane_series(consts, 40, len(DOUBLE), shape, ext)
    gstack[...] = stack_lanes(exact_dot(ztable, terms), gstack.shape[1] // 3)
    keep = lax.broadcasted_iota(jnp.int32, shape, 0) < extent[0]
    square = plane_square(shape, extent[0])
    weights = [jnp.broadcast_to(rows[:, r : r + 1], shape) for r in range(ROWS)]
    group = min(4, slab)

    def body(i, _):
        for half in range(group):
            at = group * i + half
            kx = own[0] * slab + at
            local = square + x_square(kx, full)
            gain = gain_of(local)
            total = None
            for r in range(ROWS):
                term = weights[r] * force[pl.ds(r * full + kx, 1), :]
                total = term if total is None else total + term
            twice = 2.0 - local * gain
            first = jnp.where(keep, now[at], 0.0)
            value = twice * first - jnp.where(keep, prev[at], 0.0) + gain * total
            current[at] = value
            onward[at] = twice * value - first
        return 0

    lax.fori_loop(0, slab // group, body, 0)


def series_planes(force, terms, count):
    full, width = force.shape[0] // ROWS, force.shape[1]
    ax = lax.broadcasted_iota(jnp.int32, (full, width), 0).astype(F32) / full
    ay = lax.broadcasted_iota(jnp.int32, (full, width), 1).astype(F32) / width
    square = BASE * (ax * ax + ay * ay) - BASE
    planes = [plane(force, r) for r in range(ROWS)]
    for n in range(count):
        if n:
            planes = [value * square for value in planes]
        for r in range(ROWS):
            at = (n * ROWS + r) * full
            terms[at : at + full, :] = planes[r]
    used = count * ROWS * full
    if used < terms.shape[0]:
        terms[used:, :] = jnp.zeros((terms.shape[0] - used, width), F32)


def lift(terms, across, table, ystack, given, turned, pressure, count, done):
    zcap = table.shape[0]
    depth = table.shape[1] // 3
    used = count * ROWS
    full, width = across.shape[1] // 3, terms.shape[1]
    slab = across.shape[0]
    turned[used * slab :, :] = jnp.zeros(((depth - used) * slab, width), F32)
    for at in range(0, used, 2):
        pair = [terms[(at + half) * full : (at + half + 1) * full, :] for half in range(2)]
        wide = dot(across, tall_split(jnp.concatenate(pair, axis=1)))
        for half in range(2):
            turned[(at + half) * slab : (at + half + 1) * slab, :] = wide[
                :, half * width : (half + 1) * width
            ]
    block = ROWS * slab
    for n in range(count):
        span = slice(n * block, (n + 1) * block)
        turned[span, :] = along_y(turned[span, :], ystack[...])
    for i in range(0, slab, 2):
        pair = [turned[pl.ds(i + half, depth, stride=slab), :] for half in range(2)]
        wide = dot(table[...], tall_split(jnp.concatenate(pair, axis=1)))
        for half in range(2):
            span = slice((i + half) * zcap, (i + half + 1) * zcap)
            value = wide[:, half * width : (half + 1) * width]
            for piece in given:
                value = value + piece[span, :]
            pressure[span, :] = value
        done(i + 2)


def first_kernel(own, force, gstack, ystack, xown, free, summed, terms, turned):
    series_planes(force, terms, DOUBLE_TERMS)
    lift(
        terms, xown[own[0]], gstack, ystack, [free], turned, summed, DOUBLE_TERMS, lambda i: None
    )


def last_kernel(own, near, tx, uy, onward, estack, hstack, ystack, xown, *rest, full, parts):
    far, given = rest[:parts], rest[parts : 2 * parts]
    modes_out, pressure_out, modes, pressure, spare, force, terms, turned, sems = rest[2 * parts :]
    slab, zcap, width = onward.shape
    depth = estack.shape[1] // 3
    gather_kx(spare, far, own[0])
    force_planes(spare, near, tx, uy, force)
    sends = []

    def send(source, target, at, size):
        span = pl.ds(at, size)
        sends.append(
            pltpu.make_async_copy(source.at[span], target.at[span], sems.at[len(sends)])
        )
        sends[-1].start()

    series_planes(force, terms, TERMS)
    own_at = own[0] * slab
    for i in range(0, slab, 2):
        pair = [terms[pl.ds(own_at + i + half, depth, stride=full), :] for half in range(2)]
        wide = dot(estack[...], tall_split(jnp.concatenate(pair, axis=1)))
        for half in range(2):
            modes[i + half] = onward[i + half] + wide[:, half * width : (half + 1) * width]
        if (i + 2) % CHUNK == 0:
            send(modes, modes_out, i + 2 - CHUNK, CHUNK)

    def done(i):
        if i % CHUNK == 0:
            send(pressure, pressure_out, (i - CHUNK) * zcap, CHUNK * zcap)

    lift(terms, xown[own[0]], hstack, ystack, given, turned, pressure, TERMS, done)
    for copy in sends:
        copy.wait()


def on_device(modes_now, modes_prev, z_extent, lower_nbr, upper_nbr, x_shift, y_shift):
    slab, zcap, width = modes_now.shape
    parts = lax.axis_size("split")
    count = lax.axis_size("dom")
    full = slab * parts
    own = lax.axis_index("split").astype(jnp.int32)[None]
    group = lax.axis_index("dom").astype(jnp.int32)[None]
    inner = inner_size(count)
    tall = count // inner
    size = ROWS * slab
    big = 4 * slab * zcap * width

    xtable, ytable = static_table(full), static_table(width)
    consts = np.zeros((56, width), np.float32)
    for r in range(ROWS):
        consts[0, r], consts[1, r] = (r, 0) if r < FACE else (ROWS - 1 - r, 1)
    for p, (r, q) in enumerate(PAIRS):
        consts[2:4, p], consts[4:6, p] = consts[0:2, r], consts[0:2, q]
    for n in range(DOUBLE_TERMS):
        lanes = slice(n * ROWS, (n + 1) * ROWS)
        consts[6:8, lanes] = consts[0:2, :ROWS]
        for j in range(len(SERIES) - n if n < TERMS else 0):
            consts[8 + j, n] = consts[24 + j, lanes] = SERIES[n + j] * math.comb(n + j, n)
        for j in range(len(DOUBLE) - n):
            consts[40 + j, lanes] = DOUBLE[n + j] * math.comb(n + j, n)
    depth = -(-TERMS * ROWS // 16) * 16
    double_depth = -(-DOUBLE_TERMS * ROWS // 16) * 16
    yhigh, ylow = halves(ytable)
    ystack = np.block([[yhigh, ylow], [yhigh, np.zeros_like(yhigh)]])
    xhigh, xlow = halves(xtable.T)
    xown = np.stack(
        [
            np.concatenate([t[s * slab : (s + 1) * slab] for t in (xhigh, xlow, xhigh)], axis=1)
            for s in range(parts)
        ]
    )
    xparts = np.stack(
        [
            np.concatenate(
                [
                    np.concatenate(
                        [
                            t[(s + k) % parts * slab : ((s + k) % parts + 1) * slab,
                              s * slab : (s + 1) * slab]
                            for k in range(parts)
                        ],
                        axis=0,
                    )
                    for t in (xhigh, xlow, xhigh)
                ],
                axis=1,
            )
            for s in range(parts)
        ]
    )

    def tall_of(table):
        n = table.shape[0]
        tall = np.pad(table.T, ((n, n), (0, 0)))
        return jnp.asarray(np.concatenate([tall, table], axis=0).astype(np.float32))

    consts, ystack, xown, xparts = map(jnp.asarray, (consts, ystack, xown, xparts))
    xtall, ytall = tall_of(xtable), tall_of(ytable)

    def swap(piece):
        got = [piece]
        for k in range(1, parts):
            got.append(lax.ppermute(piece, "split", [(i, (i + k) % parts) for i in range(parts)]))
        return got

    def spread(packet):
        held = [packet]
        for k in range(1, inner):
            to = [(i, i // inner * inner + partner(i % inner, k, inner)) for i in range(count)]
            held.append(lax.ppermute(packet, "dom", to))
        return held

    def choose(held, after):
        return call(
            functools.partial(choose_kernel, width=inner),
            [shape_of(size, width)] * tall,
            [SMEM, ANY] + [VMEM] * inner,
            flops=COVER,
            moved=8 * size * width * 4,
            name="choose",
        )(group, after, *held)

    def deliver(chosen, after):
        got = [chosen[0]]
        for k in range(1, tall):
            to = [(i, (i + k * inner) % count) for i in range(count)]
            got.append(lax.ppermute(chosen[k], "dom", to))
        picked = call(
            functools.partial(pick_kernel, tall=tall, width=inner),
            [shape_of(size, width)],
            [SMEM] * 3 + [ANY] + [VMEM] * tall,
            moved=5 * size * width * 4,
            name="pick",
        )(group, lower_nbr, upper_nbr, after, *got)[0]
        return swap(picked)

    packet, rows = call(
        strip_kernel,
        [shape_of(size + HEAD, width), shape_of(zcap, width)],
        [SMEM] * 3 + [VMEM],
        moved=big,
        name="strip",
    )(z_extent, lower_nbr, upper_nbr, modes_now)
    held = spread(packet)
    ahead, coefs = call(
        functools.partial(ahead_kernel, full=full),
        [shape_of(size, width), shape_of(16, width)],
        [SMEM] * 2 + [VMEM] * 4,
        flops=10**8,
        moved=2 * big,
        name="ahead",
    )(z_extent, own, modes_now, modes_prev, rows, consts)
    chosen = choose(held, ahead)
    mine = swap(packet)
    aheads = swap(ahead)

    tx, uy, vx, wy, near1, mixing, _ = call(
        functools.partial(relation_kernel, parts=parts),
        [
            shape_of(2, full, full),
            shape_of(2, width, width),
            shape_of(2, full, full),
            shape_of(2, width, width),
            shape_of(ROWS * full, width),
            shape_of(len(PAIRS), full, width),
            shape_of(ROWS * full, width),
        ],
        [SMEM] * 6 + [ANY] + [VMEM] * (2 + parts),
        flops=10**8,
        moved=2 * big,
        name="relation",
    )(lower_nbr, upper_nbr, x_shift, y_shift, own, coefs, chosen[0], xtall, ytall, *mine)
    far1 = deliver(chosen, near1)

    free = call(
        functools.partial(unforced_kernel, full=full),
        [shape_of(slab * zcap, width)] * parts,
        [SMEM] * 2 + [ANY] + [VMEM] * 4,
        scratch=[pltpu.VMEM((slab * zcap, width), F32)],
        flops=10**9,
        moved=4 * big,
        name="unforced",
    )(z_extent, own, far1[0], modes_now, modes_prev, ystack, xparts)
    given = [
        lax.ppermute(free[k], "split", [(i, (i + k) % parts) for i in range(parts)])
        for k in range(1, parts)
    ]

    packet2, force1, strip2 = call(
        functools.partial(middle_kernel, parts=parts),
        [
            shape_of(size + HEAD, width),
            shape_of(ROWS * full, width),
            shape_of(ROWS * full, width),
        ],
        [SMEM] * 3 + [ANY] + [VMEM] * (4 + 2 * parts),
        scratch=[pltpu.VMEM((ROWS * full, width), F32)],
        flops=10**8,
        moved=2 * big,
        name="middle",
    )(own, lower_nbr, upper_nbr, free[0], near1, tx, uy, mixing, *far1, *aheads)

    current, onward, estack, hstack, gstack = call(
        functools.partial(between_kernel, full=full),
        [
            shape_of(slab, zcap, width),
            shape_of(slab, zcap, width),
            shape_of(zcap, 3 * depth, dtype=BF16),
            shape_of(zcap, 3 * depth, dtype=BF16),
            shape_of(zcap, 3 * double_depth, dtype=BF16),
        ],
        [SMEM] * 2 + [VMEM] * 5,
        flops=10**9,
        moved=4 * big,
        name="between",
    )(z_extent, own, modes_now, modes_prev, force1, rows, consts)
    chosen2 = choose(spread(packet2), onward)
    summed = call(
        first_kernel,
        [shape_of(slab * zcap, width)],
        [SMEM] + [VMEM] * 5,
        scratch=[
            pltpu.VMEM((DOUBLE_TERMS * ROWS * full, width), F32),
            pltpu.VMEM((double_depth * slab, width), F32),
        ],
        flops=10**9,
        moved=2 * big,
        name="first",
    )(own, force1, gstack, ystack, xown, free[0])[0]
    near2 = call(
        near_kernel,
        [shape_of(ROWS * full, width)],
        [VMEM] * 3,
        flops=10**7,
        moved=big,
        name="near",
    )(strip2, vx, wy)[0]

    modes, pressure = call(
        functools.partial(last_kernel, full=full, parts=parts),
        [shape_of(slab, zcap, width), shape_of(slab * zcap, width)],
        [SMEM] + [VMEM] * (8 + 2 * parts),
        scratch=[
            pltpu.VMEM((slab, zcap, width), F32),
            pltpu.VMEM((slab * zcap, width), F32),
            pltpu.VMEM((ROWS * full, width), F32),
            pltpu.VMEM((ROWS * full, width), F32),
            pltpu.VMEM((depth * full, width), F32),
            pltpu.VMEM((depth * slab, width), F32),
            pltpu.SemaphoreType.DMA((2 * (slab // CHUNK),)),
        ],
        flops=10**9,
        moved=6 * big,
        name="last",
        out=HBM,
    )(
        own, near2, tx, uy, onward, estack, hstack, ystack, xown,
        *deliver(chosen2, summed), summed, *given,
    )
    return (modes, current, pressure.reshape(slab, zcap, width))


def solution(mesh):
    placed = (
        P("split", "dom", None),
        P("split", "dom", None),
        P("dom"),
        P("dom"),
        P("dom"),
        P("dom", None),
        P("dom", None),
    )
    return jax.shard_map(
        on_device,
        mesh=mesh,
        in_specs=placed,
        out_specs=(P("split", "dom", None), P("split", "dom", None), P("split", "dom", None)),
        check_vma=False,
    )
```

```python
import functools
import math

import jax
import jax.numpy as jnp
import numpy as np
from jax import lax
from jax.experimental import pallas as pl
from jax.experimental.pallas import tpu as pltpu
from jax.sharding import PartitionSpec as P

HIGH = lax.Precision.HIGHEST
F32 = jnp.float32
BF16 = jnp.bfloat16
STENCIL = (-490.0 / 180.0, 270.0 / 180.0, -27.0 / 180.0, 2.0 / 180.0)
COURANT = 0.5
FACE = 3
ROWS = 2 * FACE
HEAD = 8
SERIES = [(-1) ** n * 2.0 / math.factorial(2 * n + 2) for n in range(10)]
TERMS = 6
DOUBLE = [(-1) ** (n + 1) * (4 - 2.0 * 4.0 ** (n + 1)) / math.factorial(2 * n + 2) for n in range(14)]
DOUBLE_TERMS = 9
BASE = (COURANT * math.pi) ** 2
PAIRS = [(r, q) for r in range(ROWS) for q in range(r, ROWS)]
VMEM = pl.BlockSpec(memory_space=pltpu.VMEM)
SMEM = pl.BlockSpec(memory_space=pltpu.SMEM)
ANY = pl.BlockSpec(memory_space=pl.ANY)
HBM = pl.BlockSpec(memory_space=pltpu.HBM)
CHUNK = 8
COVER = 10**10
LIMIT = 12 * 1024 * 1024


def static_table(count):
    kk = np.arange(count)[:, None]
    xx = np.arange(count)[None, :]
    scale = np.where(kk == 0, np.sqrt(1.0 / count), np.sqrt(2.0 / count))
    return scale * np.cos(np.pi * kk * (xx + 0.5) / count)


def halves(table):
    high = table.astype(np.float32).astype(BF16)
    low = (table.astype(np.float32) - high.astype(np.float32)).astype(BF16)
    return high, low


def inner_size(count):
    best = 1
    for n in range(1, count + 1):
        if count % n == 0 and n * n <= count:
            best = n
    return best


def partner(place, step, count):
    if count & (count - 1) == 0:
        return place ^ step
    return (place + step) % count


def tall_split(data):
    high = data.astype(BF16).astype(F32)
    return jnp.concatenate([high, high, data - high], axis=0).astype(BF16)


def wide_split(data):
    high = data.astype(BF16)
    return jnp.concatenate([high, (data - high.astype(F32)).astype(BF16)], axis=1)


def dot(left, right):
    return jnp.dot(left, right, preferred_element_type=F32)


def exact_dot(left, right):
    return jnp.dot(left, right, precision=HIGH, preferred_element_type=F32)


def exact_dot_t(left, right):
    return lax.dot_general(
        left, right, (((1,), (1,)), ((), ())), precision=HIGH, preferred_element_type=F32
    )


def along_y(data, ystack):
    width = data.shape[1]
    both = dot(wide_split(data), ystack)
    return both[:, :width] + both[:, width:]


def cosine_of(count, odd, lenf):
    prod = count * odd
    turn = 4.0 * lenf
    rest = prod - jnp.floor(prod / turn) * turn
    return jnp.cos(rest * (0.5 * jnp.pi / lenf))


def scale_of(kk, lenf):
    return jnp.where(kk == 0, jnp.sqrt(1.0 / lenf), jnp.sqrt(2.0 / lenf))


def face_rows(near, flip, shape, extent):
    kk = lax.broadcasted_iota(jnp.int32, shape, 0)
    kf = kk.astype(F32)
    lenf = jnp.full(shape, extent.astype(F32))
    table = scale_of(kk, lenf) * cosine_of(kf, 2.0 * near + 1.0, lenf)
    sign = jnp.where((flip > 0) & (kk % 2 == 1), -1.0, 1.0)
    return jnp.where(kk < extent, table * sign, 0.0)


def gain_of(square):
    total = jnp.full_like(square, SERIES[-1])
    for value in reversed(SERIES[:-1]):
        total = total * square + value
    return total


def plane_square(shape, extent):
    kk = lax.broadcasted_iota(jnp.int32, shape, 0)
    kf = kk.astype(F32) / jnp.full(shape, extent.astype(F32))
    kf = jnp.where(kk < extent, kf, 0.0)
    ky = lax.broadcasted_iota(jnp.int32, shape, 1).astype(F32) / shape[1]
    return BASE * (kf * kf + ky * ky)


def x_square(kx, full):
    frac = kx.astype(F32) / full
    return BASE * (frac * frac)


def stencil(face, order):
    rows = []
    for jj in range(FACE):
        total = None
        for mm in range(FACE - jj):
            term = STENCIL[jj + mm + 1] * face[order[mm]]
            total = term if total is None else total + term
        rows.append(total)
    return rows


def through(planes, across, along):
    full, width = planes[0].shape
    out = exact_dot(across, jnp.concatenate(planes, axis=1))
    out = jnp.concatenate([out[:, i * width : (i + 1) * width] for i in range(FACE)], axis=0)
    out = exact_dot_t(out, along)
    return [out[i * full : (i + 1) * full] for i in range(FACE)]


def gather_kx(out, pieces, own):
    count = len(pieces)
    full = out.shape[0] // ROWS
    slab = full // count
    for k, piece in enumerate(pieces):
        at = pl.multiple_of(lax.rem(own + count - k, count) * slab, slab)
        for r in range(ROWS):
            out[pl.ds(r * full + at, slab), :] = piece[r * slab : (r + 1) * slab, :]


def plane(ref, r):
    full = ref.shape[0] // ROWS
    return ref[r * full : (r + 1) * full, :]


def call(
    kernel, out_shape, in_specs, scratch=(), flops=0, moved=0, name=None, out=VMEM
):
    return pl.pallas_call(
        kernel,
        out_shape=out_shape,
        in_specs=in_specs,
        out_specs=[out] * len(out_shape),
        scratch_shapes=list(scratch),
        compiler_params=pltpu.CompilerParams(vmem_limit_bytes=LIMIT),
        cost_estimate=pl.CostEstimate(flops=flops, bytes_accessed=moved, transcendentals=0),
        name=name,
    )


def shape_of(*dims, dtype=F32):
    return jax.ShapeDtypeStruct(dims, dtype)


def label(packet, below, above):
    at = lax.broadcasted_iota(jnp.int32, (HEAD, packet.shape[1]), 0)
    names = jnp.where(at < HEAD // 2, above, below)
    packet[packet.shape[0] - HEAD :, :] = names.astype(F32)


def strip_kernel(extent, below, above, now, packet, rows):
    slab, zcap, width = now.shape
    at = lax.broadcasted_iota(jnp.int32, (1, width), 1)
    far_face = at >= FACE
    near = jnp.where(far_face, ROWS - 1 - at, at)
    near = jnp.where(at < ROWS, near, 0).astype(F32)
    table = face_rows(near, far_face.astype(F32), (zcap, width), extent[0])
    rows[...] = table
    label(packet, below[0], above[0])
    weights = [jnp.broadcast_to(table[:, r : r + 1], (zcap, width)) for r in range(ROWS)]
    for i in range(slab // CHUNK):
        part = now[i * CHUNK : (i + 1) * CHUNK]
        for r in range(ROWS):
            span = slice(r * slab + i * CHUNK, r * slab + (i + 1) * CHUNK)
            packet[span, :] = jnp.sum(part * weights[r][None], axis=1)


def lane_series(consts, first, count, shape, extent):
    kz = lax.broadcasted_iota(jnp.int32, shape, 0)
    frac = kz.astype(F32) / jnp.full(shape, extent.astype(F32))
    middle = jnp.where(kz < extent, BASE * frac * frac, 0.0) + BASE
    total = jnp.zeros(shape, F32)
    for j in reversed(range(count)):
        total = total * middle + consts[first + j : first + j + 1, :]
    return total


def z_table(ext, zcap):
    kk = lax.broadcasted_iota(jnp.int32, (zcap, zcap), 1)
    zz = lax.broadcasted_iota(jnp.int32, (zcap, zcap), 0)
    lenf = jnp.full((zcap, zcap), ext.astype(F32))
    table = scale_of(kk, lenf) * cosine_of(kk.astype(F32), 2.0 * zz.astype(F32) + 1.0, lenf)
    return jnp.where((kk < ext) & (zz < ext), table, 0.0)


def stack_lanes(table, depth):
    table = table[:, :depth]
    high = table.astype(BF16).astype(F32)
    return jnp.concatenate([high, table - high, high], axis=1).astype(BF16)


def ahead_kernel(
    extent, own, packet, now, prev, rows, consts, strip, coefs, same, *, full
):
    slab, zcap, width = now.shape
    ext = extent[0]

    shape = (zcap, width)
    pairs = face_rows(consts[2:3, :], consts[3:4, :], shape, ext)
    pairs = pairs * face_rows(consts[4:5, :], consts[5:6, :], shape, ext)
    same[...] = packet[: same.shape[0], :]
    series = lane_series(consts, 8, len(SERIES), shape, ext)
    coefs[...] = exact_dot(series.T[: coefs.shape[0]], pairs)

    keep = lax.broadcasted_iota(jnp.int32, shape, 0) < ext
    square = plane_square(shape, ext)
    weights = [jnp.broadcast_to(rows[:, r : r + 1], shape) for r in range(ROWS)]
    for kx in range(slab):
        local = square + x_square(own[0] * slab + kx, full)
        twice = 2.0 - local * gain_of(local)
        ahead = jnp.where(keep, twice * now[kx] - prev[kx], 0.0)
        for r in range(ROWS):
            strip[r * slab + kx : r * slab + kx + 1, :] = jnp.sum(
                ahead * weights[r], axis=0, keepdims=True
            )


def relation_kernel(
    below, above, x_shift, y_shift, own, coefs, after, xtall, ytall, *rest, parts
):
    strips, (tx, uy, vx, wy, near, mixing, mine) = rest[:parts], rest[parts:]
    full, width = xtall.shape[1], ytall.shape[1]
    for f, (nbr, dx, dy) in enumerate(
        ((below, x_shift[0, 0], y_shift[0, 0]), (above, x_shift[0, 1], y_shift[0, 1]))
    ):
        has = jnp.where(nbr[0] >= 0, COURANT**2, 0.0).astype(F32)
        for count, move, tall, take, keep, scale in (
            (full, dx, xtall, tx, vx, has),
            (width, dy, ytall, uy, wy, None),
        ):
            move = jnp.clip(move, -count, count)
            slid = tall[pl.ds(count + move, count), :]
            at = lax.broadcasted_iota(jnp.int32, (count, count), 0) + move
            kept = jnp.where((at >= 0) & (at < count), tall[count : 2 * count, :], 0.0)
            plain = tall[3 * count :, :]
            taken, stay = exact_dot(plain, slid), exact_dot(plain, kept)
            take[f] = taken if scale is None else taken * scale
            keep[f] = stay if scale is None else stay * scale
    gather_kx(mine, strips, own[0])
    near_planes(mine, vx, wy, near)
    shape = (full, width)
    ax = lax.broadcasted_iota(jnp.int32, shape, 0).astype(F32) / full
    ay = lax.broadcasted_iota(jnp.int32, shape, 1).astype(F32) / width
    square = BASE * (ax * ax + ay * ay) - BASE
    for p in range(len(PAIRS)):
        total = jnp.full(shape, coefs[TERMS - 1, p])
        for n in reversed(range(TERMS - 1)):
            total = total * square + coefs[n, p]
        mixing[p] = total


def near_planes(mine, vx, wy, near):
    full = vx.shape[1]
    low = through(stencil([plane(mine, r) for r in range(FACE)], (0, 1, 2)), vx[0], wy[0])
    upp = through(stencil([plane(mine, FACE + r) for r in range(FACE)], (2, 1, 0)), vx[1], wy[1])
    for r, value in enumerate(low + upp[::-1]):
        near[r * full : (r + 1) * full, :] = value


def force_planes(far, near, tx, uy, force):
    full = tx.shape[1]
    low = through(stencil([plane(far, r) for r in range(FACE)], (2, 1, 0)), tx[0], uy[0])
    upp = through(stencil([plane(far, FACE + r) for r in range(FACE)], (0, 1, 2)), tx[1], uy[1])
    for r, value in enumerate(low + upp[::-1]):
        force[r * full : (r + 1) * full, :] = value - plane(near, r)


def choose_kernel(group, after, *refs, width):
    held, out = refs[:width], refs[width:]
    rows = out[0].shape[0]
    half = rows // 2
    h, l = group[0] // width, lax.rem(group[0], width)
    for k in range(len(out)):
        dest = (lax.rem(h + k, len(out)) * width + l).astype(F32)
        for f in range(2):
            lo, hi = f * half, (f + 1) * half
            row = rows + (0 if f == 1 else HEAD // 2)
            chosen = held[0][lo:hi, :]
            for other in held[1:]:
                chosen = jnp.where(other[row : row + 1, :] == dest, other[lo:hi, :], chosen)
            out[k][lo:hi, :] = chosen


def pick_kernel(group, below, above, after, *refs, tall, width):
    got, out = refs[:-1], refs[-1]
    half = out.shape[0] // 2
    h = group[0] // width
    for f, nbr in enumerate((below, above)):
        lo = half if f == 0 else 0
        value = got[0][lo : lo + half, :]
        for k in range(1, tall):
            here = jnp.maximum(nbr[0], 0) // width == lax.rem(h + tall - k, tall)
            value = jnp.where(here, got[k][lo : lo + half, :], value)
        out[f * half : (f + 1) * half, :] = value


def middle_kernel(own, below, above, after, near, tx, uy, mixing, *rest, parts):
    far, ahead = rest[:parts], rest[parts : 2 * parts]
    packet, force, strip, spare = rest[2 * parts :]
    gather_kx(spare, far, own[0])
    force_planes(spare, near, tx, uy, force)
    gather_kx(strip, ahead, own[0])
    full = tx.shape[1]
    slab = full // parts
    for r in range(ROWS):
        total = plane(strip, r)
        for q in range(ROWS):
            total = total + mixing[PAIRS.index((min(r, q), max(r, q)))] * plane(force, q)
        strip[r * full : (r + 1) * full, :] = total
    at = pl.multiple_of(own[0] * slab, slab)
    for r in range(ROWS):
        packet[r * slab : (r + 1) * slab, :] = strip[pl.ds(r * full + at, slab), :]
    label(packet, below[0], above[0])


def near_kernel(strip, vx, wy, near):
    near_planes(strip, vx, wy, near)


def unforced_kernel(
    extent, own, after, now, prev, ystack, xparts, *rest, full
):
    free, field = rest[:-1], rest[-1]
    slab, zcap, width = now.shape
    shape = (zcap, width)
    ext = extent[0]
    zstack = stack_lanes(z_table(ext, zcap), zcap)
    keep = lax.broadcasted_iota(jnp.int32, shape, 0) < ext
    square = plane_square(shape, ext)
    group = min(4, slab)

    def body(i, _):
        planes = []
        for half in range(group):
            at = group * i + half
            local = square + x_square(own[0] * slab + at, full)
            twice = 2.0 - local * gain_of(local)
            first = now[at]
            later = twice * (twice * first - prev[at]) - first
            planes.append(jnp.where(keep, later, 0.0))
        for j in range(0, group, 2):
            wide = dot(zstack, tall_split(jnp.concatenate(planes[j : j + 2], axis=1)))
            for half in range(2):
                at = pl.multiple_of((group * i + j + half) * zcap, zcap)
                field[pl.ds(at, zcap), :] = wide[:, half * width : (half + 1) * width]
        return 0

    lax.fori_loop(0, slab // group, body, 0)
    block = min(16, slab) * zcap
    for i in range(slab * zcap // block):
        span = slice(i * block, (i + 1) * block)
        field[span, :] = along_y(field[span, :], ystack[...])
    parts = full // slab
    across = xparts[own[0]]
    for i in range(0, zcap, 2):
        pair = [field[pl.ds(i + half, slab, stride=zcap), :] for half in range(2)]
        wide = dot(across, tall_split(jnp.concatenate(pair, axis=1)))
        for k in range(parts):
            for half in range(2):
                free[k][pl.ds(i + half, slab, stride=zcap), :] = wide[
                    k * slab : (k + 1) * slab, half * width : (half + 1) * width
                ]


def between_kernel(
    extent, own, now, prev, force, rows, consts, current, onward, estack, hstack, gstack, *, full
):
    slab, zcap, width = now.shape
    shape = (zcap, width)
    ext = extent[0]
    ztable = z_table(ext, zcap)
    face = face_rows(consts[6:7, :], consts[7:8, :], shape, ext)
    terms = face * lane_series(consts, 24, len(SERIES), shape, ext)
    depth = estack.shape[1] // 3
    estack[...] = stack_lanes(terms, depth)
    hstack[...] = stack_lanes(exact_dot(ztable, terms), depth)
    terms = face * lane_series(consts, 40, len(DOUBLE), shape, ext)
    gstack[...] = stack_lanes(exact_dot(ztable, terms), gstack.shape[1] // 3)
    keep = lax.broadcasted_iota(jnp.int32, shape, 0) < extent[0]
    square = plane_square(shape, extent[0])
    weights = [jnp.broadcast_to(rows[:, r : r + 1], shape) for r in range(ROWS)]
    group = min(4, slab)

    def body(i, _):
        for half in range(group):
            at = group * i + half
            kx = own[0] * slab + at
            local = square + x_square(kx, full)
            gain = gain_of(local)
            total = None
            for r in range(ROWS):
                term = weights[r] * force[pl.ds(r * full + kx, 1), :]
                total = term if total is None else total + term
            twice = 2.0 - local * gain
            first = jnp.where(keep, now[at], 0.0)
            value = twice * first - jnp.where(keep, prev[at], 0.0) + gain * total
            current[at] = value
            onward[at] = twice * value - first
        return 0

    lax.fori_loop(0, slab // group, body, 0)


def series_planes(force, terms, count):
    full, width = force.shape[0] // ROWS, force.shape[1]
    ax = lax.broadcasted_iota(jnp.int32, (full, width), 0).astype(F32) / full
    ay = lax.broadcasted_iota(jnp.int32, (full, width), 1).astype(F32) / width
    square = BASE * (ax * ax + ay * ay) - BASE
    planes = [plane(force, r) for r in range(ROWS)]
    for n in range(count):
        if n:
            planes = [value * square for value in planes]
        for r in range(ROWS):
            at = (n * ROWS + r) * full
            terms[at : at + full, :] = planes[r]
    used = count * ROWS * full
    if used < terms.shape[0]:
        terms[used:, :] = jnp.zeros((terms.shape[0] - used, width), F32)


def lift(terms, across, table, ystack, given, turned, pressure, count, done):
    zcap = table.shape[0]
    depth = table.shape[1] // 3
    used = count * ROWS
    full, width = across.shape[1] // 3, terms.shape[1]
    slab = across.shape[0]
    turned[used * slab :, :] = jnp.zeros(((depth - used) * slab, width), F32)
    for at in range(0, used, 2):
        pair = [terms[(at + half) * full : (at + half + 1) * full, :] for half in range(2)]
        wide = dot(across, tall_split(jnp.concatenate(pair, axis=1)))
        for half in range(2):
            turned[(at + half) * slab : (at + half + 1) * slab, :] = wide[
                :, half * width : (half + 1) * width
            ]
    block = ROWS * slab
    for n in range(count):
        span = slice(n * block, (n + 1) * block)
        turned[span, :] = along_y(turned[span, :], ystack[...])
    for i in range(0, slab, 2):
        pair = [turned[pl.ds(i + half, depth, stride=slab), :] for half in range(2)]
        wide = dot(table[...], tall_split(jnp.concatenate(pair, axis=1)))
        for half in range(2):
            span = slice((i + half) * zcap, (i + half + 1) * zcap)
            value = wide[:, half * width : (half + 1) * width]
            for piece in given:
                value = value + piece[span, :]
            pressure[span, :] = value
        done(i + 2)


def first_kernel(own, force, gstack, ystack, xown, free, summed, terms, turned):
    series_planes(force, terms, DOUBLE_TERMS)
    lift(
        terms, xown[own[0]], gstack, ystack, [free], turned, summed, DOUBLE_TERMS, lambda i: None
    )


def last_kernel(own, near, tx, uy, onward, estack, hstack, ystack, xown, *rest, full, parts):
    far, given = rest[:parts], rest[parts : 2 * parts]
    modes_out, pressure_out, modes, pressure, spare, force, terms, turned, sems = rest[2 * parts :]
    slab, zcap, width = onward.shape
    depth = estack.shape[1] // 3
    gather_kx(spare, far, own[0])
    force_planes(spare, near, tx, uy, force)
    sends = []

    def send(source, target, at, size):
        span = pl.ds(at, size)
        sends.append(
            pltpu.make_async_copy(source.at[span], target.at[span], sems.at[len(sends)])
        )
        sends[-1].start()

    series_planes(force, terms, TERMS)
    own_at = own[0] * slab
    for i in range(0, slab, 2):
        pair = [terms[pl.ds(own_at + i + half, depth, stride=full), :] for half in range(2)]
        wide = dot(estack[...], tall_split(jnp.concatenate(pair, axis=1)))
        for half in range(2):
            modes[i + half] = onward[i + half] + wide[:, half * width : (half + 1) * width]
        if (i + 2) % CHUNK == 0:
            send(modes, modes_out, i + 2 - CHUNK, CHUNK)

    def done(i):
        if i % CHUNK == 0:
            send(pressure, pressure_out, (i - CHUNK) * zcap, CHUNK * zcap)

    lift(terms, xown[own[0]], hstack, ystack, given, turned, pressure, TERMS, done)
    for copy in sends:
        copy.wait()


def on_device(modes_now, modes_prev, z_extent, lower_nbr, upper_nbr, x_shift, y_shift):
    slab, zcap, width = modes_now.shape
    parts = lax.axis_size("split")
    count = lax.axis_size("dom")
    full = slab * parts
    own = lax.axis_index("split").astype(jnp.int32)[None]
    group = lax.axis_index("dom").astype(jnp.int32)[None]
    inner = inner_size(count)
    tall = count // inner
    size = ROWS * slab
    big = 4 * slab * zcap * width

    xtable, ytable = static_table(full), static_table(width)
    consts = np.zeros((56, width), np.float32)
    for r in range(ROWS):
        consts[0, r], consts[1, r] = (r, 0) if r < FACE else (ROWS - 1 - r, 1)
    for p, (r, q) in enumerate(PAIRS):
        consts[2:4, p], consts[4:6, p] = consts[0:2, r], consts[0:2, q]
    for n in range(DOUBLE_TERMS):
        lanes = slice(n * ROWS, (n + 1) * ROWS)
        consts[6:8, lanes] = consts[0:2, :ROWS]
        for j in range(len(SERIES) - n if n < TERMS else 0):
            consts[8 + j, n] = consts[24 + j, lanes] = SERIES[n + j] * math.comb(n + j, n)
        for j in range(len(DOUBLE) - n):
            consts[40 + j, lanes] = DOUBLE[n + j] * math.comb(n + j, n)
    depth = -(-TERMS * ROWS // 16) * 16
    double_depth = -(-DOUBLE_TERMS * ROWS // 16) * 16
    yhigh, ylow = halves(ytable)
    ystack = np.block([[yhigh, ylow], [yhigh, np.zeros_like(yhigh)]])
    xhigh, xlow = halves(xtable.T)
    xown = np.stack(
        [
            np.concatenate([t[s * slab : (s + 1) * slab] for t in (xhigh, xlow, xhigh)], axis=1)
            for s in range(parts)
        ]
    )
    xparts = np.stack(
        [
            np.concatenate(
                [
                    np.concatenate(
                        [
                            t[(s + k) % parts * slab : ((s + k) % parts + 1) * slab,
                              s * slab : (s + 1) * slab]
                            for k in range(parts)
                        ],
                        axis=0,
                    )
                    for t in (xhigh, xlow, xhigh)
                ],
                axis=1,
            )
            for s in range(parts)
        ]
    )

    def tall_of(table):
        n = table.shape[0]
        tall = np.pad(table.T, ((n, n), (0, 0)))
        return jnp.asarray(np.concatenate([tall, table], axis=0).astype(np.float32))

    consts, ystack, xown, xparts = map(jnp.asarray, (consts, ystack, xown, xparts))
    xtall, ytall = tall_of(xtable), tall_of(ytable)

    def swap(piece):
        got = [piece]
        for k in range(1, parts):
            got.append(lax.ppermute(piece, "split", [(i, (i + k) % parts) for i in range(parts)]))
        return got

    def spread(packet):
        held = [packet]
        for k in range(1, inner):
            to = [(i, i // inner * inner + partner(i % inner, k, inner)) for i in range(count)]
            held.append(lax.ppermute(packet, "dom", to))
        return held

    def choose(held, after):
        return call(
            functools.partial(choose_kernel, width=inner),
            [shape_of(size, width)] * tall,
            [SMEM, ANY] + [VMEM] * inner,
            flops=COVER,
            moved=8 * size * width * 4,
            name="choose",
        )(group, after, *held)

    def deliver(chosen, after):
        got = [chosen[0]]
        for k in range(1, tall):
            to = [(i, (i + k * inner) % count) for i in range(count)]
            got.append(lax.ppermute(chosen[k], "dom", to))
        picked = call(
            functools.partial(pick_kernel, tall=tall, width=inner),
            [shape_of(size, width)],
            [SMEM] * 3 + [ANY] + [VMEM] * tall,
            moved=5 * size * width * 4,
            name="pick",
        )(group, lower_nbr, upper_nbr, after, *got)[0]
        return swap(picked)

    packet, rows = call(
        strip_kernel,
        [shape_of(size + HEAD, width), shape_of(zcap, width)],
        [SMEM] * 3 + [VMEM],
        moved=big,
        name="strip",
    )(z_extent, lower_nbr, upper_nbr, modes_now)
    held = spread(packet)
    ahead, coefs, strip = call(
        functools.partial(ahead_kernel, full=full),
        [shape_of(size, width), shape_of(16, width), shape_of(size, width)],
        [SMEM] * 2 + [VMEM] * 5,
        flops=10**8,
        moved=2 * big,
        name="ahead",
    )(z_extent, own, packet, modes_now, modes_prev, rows, consts)
    chosen = choose(held, ahead)
    mine = swap(strip)
    aheads = swap(ahead)

    tx, uy, vx, wy, near1, mixing, _ = call(
        functools.partial(relation_kernel, parts=parts),
        [
            shape_of(2, full, full),
            shape_of(2, width, width),
            shape_of(2, full, full),
            shape_of(2, width, width),
            shape_of(ROWS * full, width),
            shape_of(len(PAIRS), full, width),
            shape_of(ROWS * full, width),
        ],
        [SMEM] * 6 + [ANY] + [VMEM] * (2 + parts),
        flops=10**8,
        moved=2 * big,
        name="relation",
    )(lower_nbr, upper_nbr, x_shift, y_shift, own, coefs, chosen[0], xtall, ytall, *mine)
    far1 = deliver(chosen, near1)

    free = call(
        functools.partial(unforced_kernel, full=full),
        [shape_of(slab * zcap, width)] * parts,
        [SMEM] * 2 + [ANY] + [VMEM] * 4,
        scratch=[pltpu.VMEM((slab * zcap, width), F32)],
        flops=10**9,
        moved=4 * big,
        name="unforced",
    )(z_extent, own, far1[0], modes_now, modes_prev, ystack, xparts)
    given = [
        lax.ppermute(free[k], "split", [(i, (i + k) % parts) for i in range(parts)])
        for k in range(1, parts)
    ]

    packet2, force1, strip2 = call(
        functools.partial(middle_kernel, parts=parts),
        [
            shape_of(size + HEAD, width),
            shape_of(ROWS * full, width),
            shape_of(ROWS * full, width),
        ],
        [SMEM] * 3 + [ANY] + [VMEM] * (4 + 2 * parts),
        scratch=[pltpu.VMEM((ROWS * full, width), F32)],
        flops=10**8,
        moved=2 * big,
        name="middle",
    )(own, lower_nbr, upper_nbr, free[0], near1, tx, uy, mixing, *far1, *aheads)

    current, onward, estack, hstack, gstack = call(
        functools.partial(between_kernel, full=full),
        [
            shape_of(slab, zcap, width),
            shape_of(slab, zcap, width),
            shape_of(zcap, 3 * depth, dtype=BF16),
            shape_of(zcap, 3 * depth, dtype=BF16),
            shape_of(zcap, 3 * double_depth, dtype=BF16),
        ],
        [SMEM] * 2 + [VMEM] * 5,
        flops=10**9,
        moved=4 * big,
        name="between",
    )(z_extent, own, modes_now, modes_prev, force1, rows, consts)
    chosen2 = choose(spread(packet2), onward)
    summed = call(
        first_kernel,
        [shape_of(slab * zcap, width)],
        [SMEM] + [VMEM] * 5,
        scratch=[
            pltpu.VMEM((DOUBLE_TERMS * ROWS * full, width), F32),
            pltpu.VMEM((double_depth * slab, width), F32),
        ],
        flops=10**9,
        moved=2 * big,
        name="first",
    )(own, force1, gstack, ystack, xown, free[0])[0]
    near2 = call(
        near_kernel,
        [shape_of(ROWS * full, width)],
        [VMEM] * 3,
        flops=10**7,
        moved=big,
        name="near",
    )(strip2, vx, wy)[0]

    modes, pressure = call(
        functools.partial(last_kernel, full=full, parts=parts),
        [shape_of(slab, zcap, width), shape_of(slab * zcap, width)],
        [SMEM] + [VMEM] * (8 + 2 * parts),
        scratch=[
            pltpu.VMEM((slab, zcap, width), F32),
            pltpu.VMEM((slab * zcap, width), F32),
            pltpu.VMEM((ROWS * full, width), F32),
            pltpu.VMEM((ROWS * full, width), F32),
            pltpu.VMEM((depth * full, width), F32),
            pltpu.VMEM((depth * slab, width), F32),
            pltpu.SemaphoreType.DMA((2 * (slab // CHUNK),)),
        ],
        flops=10**9,
        moved=6 * big,
        name="last",
        out=HBM,
    )(
        own, near2, tx, uy, onward, estack, hstack, ystack, xown,
        *deliver(chosen2, summed), summed, *given,
    )
    return (modes, current, pressure.reshape(slab, zcap, width))


def solution(mesh):
    placed = (
        P("split", "dom", None),
        P("split", "dom", None),
        P("dom"),
        P("dom"),
        P("dom"),
        P("dom", None),
        P("dom", None),
    )
    return jax.shard_map(
        on_device,
        mesh=mesh,
        in_specs=placed,
        out_specs=(P("split", "dom", None), P("split", "dom", None), P("split", "dom", None)),
        check_vma=False,
    )
```
